32 devices in a mesh: dp: 8 (over z, y), ctx: 4 (over x, core).
Axes of the slice: x: 2, y: 2, z: 4, core: 2. Of those that a mesh axis runs over, the one named last changes fastest.
Arguments:
- layer_input: bfloat16 [8192, 1024], P(('dp', 'ctx')), may hold values from -6 to 6
- dest_slot: int32 [8192], P(('dp', 'ctx')), may hold values from 0 to 8191, as said below
- doc_len: int32 [8, 2], P('dp'), may hold values from 0 to 1024, as said below
- out_grad: bfloat16 [8192, 1024], P(('dp', 'ctx')), may hold values from -6 to 6
- attn_gain: bfloat16 [1024], P(('dp', 'ctx')), may hold values from 0.5 to 1.5
- w_query: bfloat16 [1024, 2048], P(('dp', 'ctx')), may hold values from -0.1875 to 0.1875
- w_key: bfloat16 [1024, 1024], P(('dp', 'ctx')), may hold values from -0.1875 to 0.1875
- w_value: bfloat16 [1024, 1024], P(('dp', 'ctx')), may hold values from -0.1875 to 0.1875
- q_gain: bfloat16 [128], P(('dp', 'ctx')), may hold values from 1 to 2
- k_gain: bfloat16 [128], P(('dp', 'ctx')), may hold values from 0.5 to 1.5
- w_out: bfloat16 [2048, 1024], P(('dp', 'ctx')), may hold values from -0.5 to 0.5
- mlp_gain: bfloat16 [1024], P(('dp', 'ctx')), may hold values from 0.5 to 1.5
- w_gate: bfloat16 [1024, 3072], P(('dp', 'ctx')), may hold values from -0.1875 to 0.1875
- w_up: bfloat16 [1024, 3072], P(('dp', 'ctx')), may hold values from -0.1875 to 0.1875
- w_down: bfloat16 [3072, 1024], P(('dp', 'ctx')), may hold values from -0.109375 to 0.109375
Outputs:
- layer_output: bfloat16 [8192, 1024], P(('dp', 'ctx'))
- input_grad: bfloat16 [8192, 1024], P(('dp', 'ctx'))
- grad_attn_gain: float32 [1024], P(('dp', 'ctx'))
- grad_query: float32 [1024, 2048], P(('dp', 'ctx'))
- grad_key: float32 [1024, 1024], P(('dp', 'ctx'))
- grad_value: float32 [1024, 1024], P(('dp', 'ctx'))
- grad_q_gain: float32 [128], P(('dp', 'ctx'))
- grad_k_gain: float32 [128], P(('dp', 'ctx'))
- grad_out: float32 [2048, 1024], P(('dp', 'ctx'))
- grad_mlp_gain: float32 [1024], P(('dp', 'ctx'))
- grad_gate: float32 [1024, 3072], P(('dp', 'ctx'))
- grad_up: float32 [1024, 3072], P(('dp', 'ctx'))
- grad_down: float32 [3072, 1024], P(('dp', 'ctx'))
The draws below stay inside these ranges and needn't reach their ends.
Inputs may be any that keep to these rules, and one draw needn't show every extreme that they name: `dest_slot`: A permutation of the rows that keeps a row's ctx index: the row held by the device at (dp i, ctx c) goes to a device at (dp j, ctx c). At most 64 rows of one device go to one device, and in every draw some pairs carry exactly 64. `doc_len`: row g gives the lengths of group g's documents in slot order: the nonzero entries come first, each at least 1024, and a row sums to at most 1024; in every draw some row holds one document of 1024 tokens.
All inputs are finite; a program needn't handle non-finite values.
Results may differ from the reference program's by a relative error of at most 0.02.
Values may be sent and summed in bfloat16 or wider, within the bound.
A program may use at most 192 MiB of HBM per device.

```python
import math
import jax
import jax.numpy as jnp
from jax import lax

D = 1024
H = 16
KVH = 8
HD = 128
FF = 3072
TOK_DEV = 256
DOCS = 2
MIN_DOC = 1024
GROUP = 1024
TOKENS = 8192
N_DP = 8
N_CTX = 4


def draw_dest_slot(key, part):
    per_pair = TOK_DEV // N_DP
    dev_ids = jnp.arange(N_DP, dtype=jnp.int32)
    row_ids = jnp.arange(TOK_DEV, dtype=jnp.int32)

    def shuffled(sub_key):
        return jax.random.permutation(sub_key, TOK_DEV)

    def one_column(column_key, column):
        perm_key, source_key, slot_key = jax.random.split(column_key, 3)
        chosen = jax.random.permutation(perm_key, N_DP).astype(jnp.int32)
        counts = jnp.full((N_DP, N_DP), per_pair, jnp.int32)
        counts = counts.at[dev_ids, chosen].add(per_pair)
        counts = counts.at[dev_ids, jnp.roll(chosen, -1)].add(-per_pair)
        row_end = jnp.cumsum(counts, axis=1, dtype=jnp.int32)
        row_start = row_end - counts
        dest_of = jnp.sum((row_ids[None, :, None] >= row_end[:, None, :]).astype(jnp.int32), axis=2, dtype=jnp.int32)
        rank_in = row_ids[None, :] - jnp.take_along_axis(row_start, dest_of, axis=1)
        shuffle = jax.vmap(shuffled)(jax.random.split(source_key, N_DP)).astype(jnp.int32)
        owner_of = jnp.take_along_axis(dest_of, shuffle, axis=1)
        rank_of = jnp.take_along_axis(rank_in, shuffle, axis=1)
        col_start = jnp.cumsum(counts, axis=0, dtype=jnp.int32) - counts
        slot_order = jax.vmap(shuffled)(jax.random.split(slot_key, N_DP)).astype(jnp.int32)
        start_of = col_start[dev_ids[:, None], owner_of]
        local_slot = slot_order[owner_of, start_of + rank_of]
        return (owner_of * N_CTX + column) * TOK_DEV + local_slot
    columns = jax.vmap(one_column)(jax.random.split(key, N_CTX), jnp.arange(N_CTX, dtype=jnp.int32))
    return jnp.transpose(columns, (1, 0, 2)).reshape(-1).astype(jnp.int32)


def draw_doc_len(key, part):
    pad_key, cut_key, full_key = jax.random.split(key, 3)
    most_pad = min(GROUP // 8, GROUP - MIN_DOC)
    padding = jax.random.randint(pad_key, (N_DP, 1), 0, most_pad + 1, dtype=jnp.int32)
    filled = GROUP - padding
    count = jnp.minimum(DOCS, filled // MIN_DOC)
    extra = filled - count * MIN_DOC
    cut_points = jax.random.randint(cut_key, (N_DP, DOCS - 1), 0, 1 << 20, dtype=jnp.int32) % (extra + 1)
    cut_index = jnp.arange(DOCS - 1, dtype=jnp.int32)[None, :]
    cut_points = jnp.where(cut_index >= count - 1, extra, cut_points)
    cut_points = jnp.sort(cut_points, axis=1)
    boundary = jnp.concatenate([jnp.zeros((N_DP, 1), jnp.int32), cut_points, extra], axis=1)
    shares = boundary[:, 1:] - boundary[:, :-1]
    entry_index = jnp.arange(DOCS, dtype=jnp.int32)[None, :]
    lengths = jnp.where(entry_index < count, MIN_DOC + shares, 0)
    single = jnp.concatenate([jnp.full((1,), GROUP, jnp.int32), jnp.zeros((DOCS - 1,), jnp.int32)])
    full_group = jax.random.randint(full_key, (), 0, N_DP, dtype=jnp.int32)
    lengths = jnp.where((jnp.arange(N_DP, dtype=jnp.int32) == full_group)[:, None], single[None, :], lengths)
    return lengths.astype(jnp.int32)


def shard_levels(own_key, extent, cuts, least, high):
    def one(position, shards_of):
        draws = jax.random.uniform(jax.random.fold_in(jax.random.fold_in(own_key, 6), position), (shards_of,), jnp.float32, least / len(cuts), high / len(cuts))
        return jnp.repeat(jnp.exp(draws), extent[position] // shards_of).reshape((-1,) + (1,) * (len(extent) - position - 1))

    factor_of = one(*cuts[0])
    for cut in cuts[1:]:
        factor_of = factor_of * one(*cut)
    return factor_of


def normal_values(own_key, dims, deviation, limit, cuts=(), kind=jnp.bfloat16):
    gain = shard_levels(own_key, dims, cuts, -0.22, 0.18) if cuts else 1.0
    values = jax.random.normal(own_key, dims, jnp.float32) * deviation * gain
    return jnp.minimum(jnp.maximum(values, -limit), limit).astype(kind)


def setup_inputs(seed: int = 0) -> dict:
    streams_of = jax.random.split(jax.random.key(seed), 16)
    return {
        "layer_input": normal_values(streams_of[0], (TOKENS, D), 1.0, 6.0, ((0, 32),)),
        "dest_slot": draw_dest_slot(jax.random.fold_in(streams_of[15], 71), 0),
        "doc_len": draw_doc_len(jax.random.fold_in(streams_of[15], 71), 0),
        "out_grad": normal_values(streams_of[3], (TOKENS, D), 1.0, 6.0, ((0, 32),)),
        "attn_gain": jnp.clip(1.0 + 0.1 * jax.random.normal(streams_of[4], (D,), jnp.float32), 0.5, 1.5).astype(jnp.bfloat16),
        "w_query": normal_values(streams_of[5], (D, H * HD), D ** -0.5, 0.1875, ((0, 32),)),
        "w_key": normal_values(streams_of[6], (D, KVH * HD), D ** -0.5, 0.1875, ((0, 32),)),
        "w_value": normal_values(streams_of[7], (D, KVH * HD), D ** -0.5, 0.1875, ((0, 32),)),
        "q_gain": jnp.clip(1.0 + 1.0 * jax.random.uniform(streams_of[8], (HD,), jnp.float32) ** shard_levels(streams_of[8], (HD,), ((0, 32),), -0.2, 0.2), 1.0, 2.0).astype(jnp.bfloat16),
        "k_gain": jnp.clip(1.0 + 0.1 * jax.random.normal(streams_of[9], (HD,), jnp.float32), 0.5, 1.5).astype(jnp.bfloat16),
        "w_out": normal_values(streams_of[10], (H * HD, D), (H * HD // 16) ** -0.5, 0.5, ((0, 32),)),
        "mlp_gain": jnp.clip(1.0 + 0.1 * jax.random.normal(streams_of[11], (D,), jnp.float32), 0.5, 1.5).astype(jnp.bfloat16),
        "w_gate": normal_values(streams_of[12], (D, FF), D ** -0.5, 0.1875, ((0, 32),)),
        "w_up": normal_values(streams_of[13], (D, FF), D ** -0.5, 0.1875, ((0, 32),)),
        "w_down": normal_values(streams_of[14], (FF, D), FF ** -0.5, 0.109375, ((0, 32),)),
    }


EPS = 1e-06
THETA = 1000000.0
MASKED = -1e+30
HIGH = lax.Precision.HIGHEST

@jax.custom_vjp
def low(v):
    return lax.optimization_barrier(v.astype(jnp.bfloat16)).astype(jnp.float32)

@jax.custom_vjp
def low_back(v):
    return v

def low_keep(v):
    return (low(v), None)

def low_pass(kept, grad):
    return (grad,)

def back_keep(v):
    return (v, None)

def back_low(kept, grad):
    return (low(grad),)
low.defvjp(low_keep, low_pass)
low_back.defvjp(back_keep, back_low)

def matmul(left_rows, right_rows):
    return jnp.dot(left_rows, right_rows, precision=HIGH, preferred_element_type=jnp.float32)

def doc_layout(lengths, slot_ids):
    doc_ends = jnp.cumsum(lengths, dtype=jnp.int32)
    starts = doc_ends - lengths
    documents = lax.optimization_barrier(jnp.sum((slot_ids[:, None] >= doc_ends[None, :]).astype(jnp.int32), axis=1, dtype=jnp.int32))
    one_hot = (documents[:, None] == jnp.arange(lengths.shape[0], dtype=jnp.int32)[None, :]).astype(jnp.int32)
    positions = slot_ids - lax.optimization_barrier(jnp.sum(one_hot * starts[None, :], axis=1, dtype=jnp.int32))
    return (documents, positions)

def allowed_mask(query_slots, query_docs, key_slots, key_docs):
    same_doc = (query_docs[:, None] == key_docs[None, :]) & (query_docs[:, None] < DOCS) & (key_slots[None, :] <= query_slots[:, None])
    return same_doc | (key_slots[None, :] == query_slots[:, None])

def rope_tables(positions):
    freq_index = jnp.arange(HD // 2, dtype=jnp.float32)
    inverse = jnp.exp(freq_index * (-2.0 / HD) * math.log(THETA))
    doubled = jnp.concatenate([inverse, inverse])
    angles = positions.astype(jnp.float32)[:, None] * doubled[None, :]
    return (jnp.cos(angles), jnp.sin(angles))

def rms_scale(values_in, gain_vec):
    factor = lax.rsqrt(lax.optimization_barrier(jnp.mean(values_in * values_in, axis=-1, keepdims=True)) + EPS)
    return values_in * factor * gain_vec

def qk_rope(projected, gain_vec, cosine_table, sine_table):
    row_count = projected.shape[0]
    per_head = projected.reshape(row_count, -1, HD)
    normed = rms_scale(per_head, gain_vec)
    half_dim = HD // 2
    turned = jnp.concatenate([-normed[..., half_dim:], normed[..., :half_dim]], axis=-1)
    rotated = normed * cosine_table[:, None, :] + turned * sine_table[:, None, :]
    return rotated.reshape(row_count, -1)

def block_forward(inputs, weights, cosine_table, sine_table, allowed):
    gain_attn, query_mat, key_mat, value_mat, gain_q, gain_k, out_mat, gain_mlp, gate_mat, up_mat, down_mat = weights
    row_count = inputs.shape[0]
    head_groups = H // KVH
    normed_attn = low(rms_scale(inputs, gain_attn))
    q_proj = low_back(matmul(normed_attn, query_mat))
    k_proj = low_back(matmul(normed_attn, key_mat))
    value_rows = low(low_back(matmul(normed_attn, value_mat)))
    queries = low(qk_rope(q_proj, gain_q, cosine_table, sine_table))
    key_rows = low(qk_rope(k_proj, gain_k, cosine_table, sine_table))
    query_heads = queries.reshape(row_count, KVH, head_groups, HD)
    key_heads = key_rows.reshape(row_count, KVH, HD)
    value_heads = value_rows.reshape(row_count, KVH, HD)
    scores = low_back(jnp.einsum('qhgd,khd->hgqk', query_heads, key_heads, precision=HIGH) * HD ** (-0.5))
    scores = jnp.where(allowed[None, None], scores, MASKED)
    attn_probs = jax.nn.softmax(scores, axis=-1)
    attended = jnp.einsum('hgqk,khd->qhgd', low(attn_probs), value_heads, precision=HIGH).reshape(row_count, H * HD)
    attended = low(low_back(attended))
    middle = inputs + low_back(matmul(attended, out_mat))
    normed_mlp = low(rms_scale(middle, gain_mlp))
    gate_proj = low_back(matmul(normed_mlp, gate_mat))
    up_proj = low_back(matmul(normed_mlp, up_mat))
    hidden = low(jax.nn.silu(gate_proj) * up_proj)
    return middle + matmul(hidden, down_mat)

def reference(layer_input, dest_slot, doc_len, out_grad, attn_gain, w_query, w_key, w_value, q_gain, k_gain, w_out, mlp_gain, w_gate, w_up, w_down):
    owned_rows = jnp.zeros_like(layer_input).at[dest_slot].set(layer_input)
    weights = tuple((member.astype(jnp.float32) for member in (attn_gain, w_query, w_key, w_value, q_gain, k_gain, w_out, mlp_gain, w_gate, w_up, w_down)))
    inputs = owned_rows.astype(jnp.float32).reshape(N_DP, GROUP, D)
    cotangent = out_grad.astype(jnp.float32).reshape(N_DP, GROUP, D)
    slot_ids = jnp.arange(GROUP, dtype=jnp.int32)

    def one_group(totals, member):
        group_in, group_grad, lengths = member
        documents, positions = doc_layout(lengths, slot_ids)
        allowed = allowed_mask(slot_ids, documents, slot_ids, documents)
        cosine_table, sine_table = rope_tables(positions)

        def forward(values_in, params):
            return block_forward(values_in, params, cosine_table, sine_table, allowed)
        result, pullback = jax.vjp(forward, group_in, weights)
        grad_in, grad_weights = pullback(group_grad)
        totals = jax.tree.map(lambda running, adding: running + adding, totals, grad_weights)
        return (totals, (result.astype(jnp.bfloat16), grad_in.astype(jnp.bfloat16)))
    zeros_tree = jax.tree.map(jnp.zeros_like, weights)
    totals, (outputs, grads_in) = lax.scan(one_group, zeros_tree, (inputs, cotangent, doc_len))
    layer_output = outputs.reshape(N_DP * GROUP, D)
    input_grad = grads_in.reshape(N_DP * GROUP, D)[dest_slot]
    return (layer_output, input_grad, totals[0], totals[1], totals[2], totals[3], totals[4], totals[5], totals[6], totals[7], totals[8], totals[9], totals[10])
```

```python
import functools
import math

import jax
import jax.numpy as jnp
import numpy as np
from jax import lax
from jax.experimental import pallas as pl
from jax.experimental.pallas import tpu as pltpu
from jax.sharding import PartitionSpec as P

H = 16
KVH = 8
HD = 128
EPS = 1e-06
THETA = 1000000.0
MASKED = -1e30
QB = 256
SCALE = HD ** (-0.5)
LOG2E = math.log2(math.e)
BF = jnp.bfloat16
F32 = jnp.float32
BOTH = ("dp", "ctx")
VMEM_LIMIT = 60 << 20


def dot(a, b):
    return lax.dot_general(a, b, (((1,), (0,)), ((), ())), preferred_element_type=F32)


def dot_nt(a, b):
    return lax.dot_general(a, b, (((1,), (1,)), ((), ())), preferred_element_type=F32)


def dot_tn(a, b):
    return lax.dot_general(a, b, (((0,), (0,)), ((), ())), preferred_element_type=F32)


def lanes(start, size):
    return pl.ds(pl.multiple_of(start * size, size), size)


def rope_tables(rows):
    inverse = np.exp(np.arange(HD // 2, dtype=np.float32) * np.float32(-2.0 / HD * math.log(THETA)))
    doubled = np.concatenate([inverse, inverse]).astype(np.float32)
    angles = np.arange(rows, dtype=np.float32)[:, None] * doubled[None, :]
    sign = np.where(np.arange(HD) < HD // 2, -1.0, 1.0).astype(np.float32)
    return np.cos(angles), np.sin(angles) * sign[None, :]


def mask_block(off_bias):
    rows = lax.broadcasted_iota(jnp.int32, (QB, QB), 0)
    cols = lax.broadcasted_iota(jnp.int32, (QB, QB), 1)
    return jnp.where(rows == cols, 0.0, jnp.where(cols < rows, off_bias, MASKED))


def attn_fwd_body(
    x_ref, wqkv_ref, wo_ref, ga_ref, gq_ref, gk_ref, cos_ref, sin_ref, bias_ref,
    part_ref, q_ref, k_ref, v_ref, p_ref, xn_ref, att_ref, mask_ref,
):
    rows = x_ref.shape[0]
    nq = q_ref.shape[1] // HD
    nk = k_ref.shape[1] // HD
    gain_a = ga_ref[...]

    @pl.loop(0, rows // QB)
    def _(i):
        here = lanes(i, QB)
        x = x_ref[here, :].astype(F32)
        r = lax.rsqrt(jnp.mean(x * x, axis=-1, keepdims=True) + EPS)
        xn = (x * r * gain_a).astype(BF)
        xn_ref[here, :] = xn
        p = dot(xn, wqkv_ref[...])
        p_ref[here, :] = p[:, : (nq + nk) * HD]
        v_ref[here, :] = p[:, (nq + nk) * HD :].astype(BF)
        cos = cos_ref[here, :]
        sin = sin_ref[here, :]
        for h in range(nq + nk):
            ph = p[:, h * HD : (h + 1) * HD]
            g = gq_ref[...] if h < nq else gk_ref[...]
            n = ph * lax.rsqrt(jnp.mean(ph * ph, axis=-1, keepdims=True) + EPS) * g
            rot = (n * cos + pltpu.roll(n, HD // 2, 1) * sin).astype(BF)
            if h < nq:
                q_ref[here, h * HD : (h + 1) * HD] = rot
            else:
                k_ref[here, (h - nq) * HD : (h - nq + 1) * HD] = rot

    off = bias_ref[0:1, 0:1]
    mask_ref[...] = mask_block(off)

    @pl.loop(0, nq)
    def _(h):
        hq = lanes(h, HD)
        hk = lanes(lax.div(h * nk, nq), HD)
        for i in range(rows // QB):
            q = q_ref[i * QB : (i + 1) * QB, hq]
            es, total = [], None
            for j in range(i + 1):
                s = dot_nt(q, k_ref[j * QB : (j + 1) * QB, hk]) * (SCALE * LOG2E)
                e = jnp.exp2(s + (mask_ref[...] if j == i else off))
                t = jnp.sum(e, axis=-1, keepdims=True)
                total = t if total is None else total + t
                es.append(e)
            inv = 1.0 / total
            o = None
            for j in range(i + 1):
                c = dot((es[j] * inv).astype(BF), v_ref[j * QB : (j + 1) * QB, hk])
                o = c if o is None else o + c
            att_ref[i * QB : (i + 1) * QB, hq] = o.astype(BF)

    @pl.loop(0, rows // QB)
    def _(i):
        here = lanes(i, QB)
        part_ref[here, :] = dot(att_ref[here, :], wo_ref[...]).astype(BF)


def attn_bwd_body(
    db_ref, wo_ref, wqkv_ref, q_ref, k_ref, v_ref, p_ref, xn_ref, att_ref,
    gq_ref, gk_ref, cos_ref, sin_ref, bias_ref,
    gwqkv_ref, gwo_ref, dxn_ref, ggq_ref, ggk_ref,
    mask_ref, da_ref, dq_ref, dk_ref, dv_ref, dp_ref,
):
    rows = db_ref.shape[0]
    nq = q_ref.shape[1] // HD
    nk = k_ref.shape[1] // HD
    group = nq // nk

    @pl.loop(0, rows // QB)
    def _(i):
        here = lanes(i, QB)
        da_ref[here, :] = dot_nt(db_ref[here, :], wo_ref[...]).astype(BF)

    off = bias_ref[0:1, 0:1]
    mask_ref[...] = mask_block(off)
    dk_ref[...] = jnp.zeros_like(dk_ref)
    dv_ref[...] = jnp.zeros_like(dv_ref)

    @pl.loop(0, nq)
    def _(h):
        hq = lanes(h, HD)
        hk = lanes(lax.div(h, group), HD)
        for i in range(rows // QB):
            here = slice(i * QB, (i + 1) * QB)
            q = q_ref[here, hq]
            da = da_ref[here, hq]
            inner = jnp.sum(da.astype(F32) * att_ref[here, hq].astype(F32), axis=-1, keepdims=True)
            es, total = [], None
            for j in range(i + 1):
                s = dot_nt(q, k_ref[j * QB : (j + 1) * QB, hk]) * (SCALE * LOG2E)
                e = jnp.exp2(s + (mask_ref[...] if j == i else off))
                t = jnp.sum(e, axis=-1, keepdims=True)
                total = t if total is None else total + t
                es.append(e)
            inv = 1.0 / total
            dq = None
            for j in range(i + 1):
                keys = slice(j * QB, (j + 1) * QB)
                probs = es[j] * inv
                ds = (probs * (dot_nt(da, v_ref[keys, hk]) - inner)).astype(BF)
                c = dot(ds, k_ref[keys, hk])
                dq = c if dq is None else dq + c
                dk_ref[keys, hk] += dot_tn(ds, q)
                dv_ref[keys, hk] += dot_tn(probs.astype(BF), da)
            dq_ref[here, hq] = dq

    ggq_ref[...] = jnp.zeros_like(ggq_ref)
    ggk_ref[...] = jnp.zeros_like(ggk_ref)

    @pl.loop(0, rows // QB)
    def _(i):
        here = lanes(i, QB)
        cos = cos_ref[here, :]
        sin = sin_ref[here, :]
        sums = [jnp.zeros((1, HD), F32), jnp.zeros((1, HD), F32)]
        for h in range(nq + nk):
            which = 0 if h < nq else 1
            g = (gq_ref if h < nq else gk_ref)[...]
            cols = slice(h * HD, (h + 1) * HD)
            if h < nq:
                d = dq_ref[here, cols] * SCALE
            else:
                d = dk_ref[here, (h - nq) * HD : (h - nq + 1) * HD] * SCALE
            dn = d * cos + pltpu.roll(d * sin, HD // 2, 1)
            ph = p_ref[here, cols]
            r = lax.rsqrt(jnp.mean(ph * ph, axis=-1, keepdims=True) + EPS)
            nh = ph * r
            sums[which] += jnp.sum(dn * nh, axis=0, keepdims=True)
            cg = dn * g
            dp_ref[here, cols] = (r * (cg - nh * jnp.mean(cg * nh, axis=-1, keepdims=True))).astype(BF)
        dp_ref[here, (nq + nk) * HD :] = dv_ref[here, :].astype(BF)
        ggq_ref[0:1, :] += sums[0]
        ggk_ref[0:1, :] += sums[1]
        dxn_ref[here, :] = dot_nt(dp_ref[here, :], wqkv_ref[...]).astype(BF)

    @pl.loop(0, gwo_ref.shape[0] // 128)
    def _(i):
        cols = lanes(i, 128)
        gwo_ref[cols, :] = dot_tn(att_ref[:, cols], db_ref[...]).astype(BF)

    @pl.loop(0, gwqkv_ref.shape[0] // 128)
    def _(i):
        cols = lanes(i, 128)
        gwqkv_ref[cols, :] = dot_tn(xn_ref[:, cols], dp_ref[...]).astype(BF)


def shape(*dims, dtype=BF):
    return jax.ShapeDtypeStruct(dims, dtype)


def in_vmem(body, outs, scratch, name):
    return pl.pallas_call(
        body,
        out_shape=outs,
        scratch_shapes=scratch,
        compiler_params=pltpu.CompilerParams(vmem_limit_bytes=VMEM_LIMIT),
        name=name,
    )


def slab_moves(n_data):
    return [(s, (s % n_data) * 4 + s // n_data) for s in range(4 * n_data)]


def to_quarters(weight):
    rows, cols = weight.shape
    return weight.reshape(rows, 4, cols // 4).transpose(1, 0, 2)


def from_quarters(blocks):
    n, rows, cols = blocks.shape
    return blocks.transpose(1, 0, 2).reshape(rows, n * cols)


def rms_back(c, v, gain):
    r = lax.rsqrt(jnp.mean(v * v, axis=-1, keepdims=True) + EPS)
    n = v * r
    cg = c * gain
    return jnp.sum(c * n, axis=0), r * (cg - n * jnp.mean(cg * n, axis=-1, keepdims=True))


def local(
    layer_input, dest_slot, doc_len, out_grad, attn_gain, w_query, w_key, w_value, q_gain, k_gain,
    w_out, mlp_gain, w_gate, w_up, w_down,
):
    tok, width = layer_input.shape
    n = lax.axis_size("dp")
    cap = 2 * tok // n
    rows = 4 * tok
    owner = dest_slot // (4 * tok)
    slot = dest_slot % tok
    hot = (owner[:, None] == jnp.arange(n, dtype=jnp.int32)[None, :]).astype(BF)
    lower = (jnp.arange(tok)[:, None] > jnp.arange(tok)[None, :]).astype(BF)
    rank = jnp.sum(dot(lower, hot) * hot.astype(F32), axis=1).astype(jnp.int32)
    send_slot = owner * cap + rank
    place = send_slot[:, None] == jnp.arange(n * cap, dtype=jnp.int32)[None, :]
    outgoing = dot_tn(place.astype(BF), layer_input).astype(BF)
    labels = jnp.sum(jnp.where(place, slot[:, None] - tok, 0), axis=0, dtype=jnp.int32) + tok
    received = lax.all_to_all(outgoing.reshape(n, cap, width), "dp", 0, 0, tiled=True).reshape(n * cap, width)
    in_labels = lax.all_to_all(labels.reshape(n, cap), "dp", 0, 0, tiled=True).reshape(-1)
    pick = (jnp.arange(tok, dtype=jnp.int32)[:, None] == in_labels[None, :]).astype(BF)
    owned = dot(pick, received).astype(BF)
    x_all = lax.all_gather(owned, "ctx", axis=0, tiled=True)
    og_all = lax.all_gather(out_grad, "ctx", axis=0, tiled=True)
    gains = lax.all_gather(jnp.concatenate([attn_gain, mlp_gain, q_gain, k_gain])[None, :], BOTH, axis=0, tiled=True)
    g_rows, g_heads = attn_gain.shape[0], q_gain.shape[0]
    gains = gains.astype(F32)
    ga = gains[:, :g_rows].reshape(1, width)
    gm = gains[:, g_rows : 2 * g_rows].reshape(1, width)
    gq = gains[:, 2 * g_rows : 2 * g_rows + g_heads].reshape(1, HD)
    gk = gains[:, 2 * g_rows + g_heads :].reshape(1, HD)
    qkv = jnp.concatenate([to_quarters(w_query), to_quarters(w_key), to_quarters(w_value)], axis=2)
    gu = jnp.concatenate([to_quarters(w_gate), to_quarters(w_up)], axis=2)
    qkv = lax.all_to_all(qkv, "ctx", 0, 0, tiled=True).reshape(-1, qkv.shape[2])
    gu = lax.all_to_all(gu, "ctx", 0, 0, tiled=True).reshape(-1, gu.shape[2])
    wo, wd = (lax.ppermute(w, BOTH, slab_moves(n)) for w in (w_out, w_down))
    wqkv, wo, wgu, wd = (lax.all_gather(w, "dp", axis=0, tiled=True) for w in (qkv, wo, gu, wd))
    cos, sin = rope_tables(rows)
    bias = jnp.where(doc_len[0, 0] > 0, 0.0, MASKED).astype(F32).reshape(1, 1) + jnp.zeros((8, 128), F32)
    part, q, k, v, p, xn, att = in_vmem(
        attn_fwd_body,
        (shape(rows, width), shape(rows, 512), shape(rows, 256), shape(rows, 256),
         shape(rows, 768, dtype=F32), shape(rows, width), shape(rows, 512)),
        [pltpu.VMEM((QB, QB), F32)],
        "attn_fwd",
    )(x_all, wqkv, wo, ga, gq, gk, cos, sin, bias)
    x_own = owned.astype(F32)
    middle = x_own + lax.psum_scatter(part, "ctx", scatter_dimension=0, tiled=True).astype(F32)
    normed = (middle * lax.rsqrt(jnp.mean(middle * middle, axis=-1, keepdims=True) + EPS) * gm).astype(BF)
    nm = lax.all_gather(normed, "ctx", axis=0, tiled=True)
    ff = wd.shape[0]
    wg, wu = wgu[:, :ff], wgu[:, ff:]
    gate, up = dot(nm, wg), dot(nm, wu)
    s = jax.nn.sigmoid(gate)
    silu = gate * s
    hidden = (silu * up).astype(BF)
    out_part = dot(hidden, wd).astype(BF)
    dh = dot_nt(og_all, wd)
    d_gate = (dh * up * s * (1.0 + gate * (1.0 - s))).astype(BF)
    d_up = (dh * silu).astype(BF)
    gwd = dot_tn(hidden, og_all).astype(BF)
    gwgu = jnp.concatenate([dot_tn(nm, d_gate), dot_tn(nm, d_up)], axis=1).astype(BF)
    dnm_part = (dot_nt(d_gate, wg) + dot_nt(d_up, wu)).astype(BF)
    dnm = lax.psum_scatter(dnm_part, "ctx", scatter_dimension=0, tiled=True).astype(F32)
    layer_output = (middle + lax.psum_scatter(out_part, "ctx", scatter_dimension=0, tiled=True).astype(F32)).astype(BF)
    ggm, d_mid = rms_back(dnm, middle, gm)
    d_middle = out_grad.astype(F32) + d_mid
    db = lax.all_gather(d_middle.astype(BF), "ctx", axis=0, tiled=True)
    gwqkv, gwo, dxn_part, ggq, ggk = in_vmem(
        attn_bwd_body,
        (shape(width, 1024), shape(512, width), shape(rows, width), shape(8, HD, dtype=F32), shape(8, HD, dtype=F32)),
        [pltpu.VMEM((QB, QB), F32), pltpu.VMEM((rows, 512), BF), pltpu.VMEM((rows, 512), F32),
         pltpu.VMEM((rows, 256), F32), pltpu.VMEM((rows, 256), F32), pltpu.VMEM((rows, 1024), BF)],
        "attn_bwd",
    )(db, wo, wqkv, q, k, v, p, xn, att, gq, gk, cos, sin, bias)
    dxn = lax.psum_scatter(dxn_part, "ctx", scatter_dimension=0, tiled=True).astype(F32)
    gga, d_x = rms_back(dxn, x_own, ga)
    owned_grad = (d_middle + d_x).astype(BF)
    picked = dot_tn(pick, owned_grad).astype(BF)
    returned = lax.all_to_all(picked.reshape(n, cap, width), "dp", 0, 0, tiled=True).reshape(n * cap, width)
    input_grad = dot(place.astype(BF), returned).astype(BF)
    gwqkv, gwo, gwgu, gwd = (lax.psum_scatter(g, "dp", scatter_dimension=0, tiled=True) for g in (gwqkv, gwo, gwgu, gwd))
    gwo, gwd = (lax.ppermute(g, BOTH, [(b, a) for a, b in slab_moves(n)]).astype(F32) for g in (gwo, gwd))
    gwqkv = lax.all_to_all(gwqkv.reshape(4, -1, 1024), "ctx", 0, 0, tiled=True).astype(F32)
    gwgu = lax.all_to_all(gwgu.reshape(4, -1, 2 * ff), "ctx", 0, 0, tiled=True).astype(F32)
    small = [gga.reshape(4 * n, g_rows), ggm.reshape(4 * n, g_rows), ggq[0].reshape(4 * n, g_heads), ggk[0].reshape(4 * n, g_heads)]
    small = lax.psum_scatter(jnp.concatenate(small, axis=1), BOTH, scatter_dimension=0, tiled=True)[0]
    return (
        layer_output,
        input_grad,
        small[:g_rows],
        from_quarters(gwqkv[:, :, :512]),
        from_quarters(gwqkv[:, :, 512:768]),
        from_quarters(gwqkv[:, :, 768:]),
        small[2 * g_rows : 2 * g_rows + g_heads],
        small[2 * g_rows + g_heads :],
        gwo,
        small[g_rows : 2 * g_rows],
        from_quarters(gwgu[:, :, :ff]),
        from_quarters(gwgu[:, :, ff:]),
        gwd,
    )


def solution(mesh):
    rows = P(BOTH, None)
    vec = P(BOTH)
    return jax.shard_map(
        local,
        mesh=mesh,
        in_specs=(rows, vec, P("dp", None), rows, vec, rows, rows, rows, vec, vec, rows, vec, rows, rows, rows),
        out_specs=(rows, rows, vec, rows, rows, rows, vec, vec, rows, vec, rows, rows, rows),
        check_vma=False,
    )
```

```python
import functools
import math

import jax
import jax.numpy as jnp
import numpy as np
from jax import lax
from jax.experimental import pallas as pl
from jax.experimental.pallas import tpu as pltpu
from jax.sharding import PartitionSpec as P

H = 16
KVH = 8
HD = 128
EPS = 1e-06
THETA = 1000000.0
MASKED = -1e30
QB = 256
SCALE = HD ** (-0.5)
LOG2E = math.log2(math.e)
BF = jnp.bfloat16
F32 = jnp.float32
BOTH = ("dp", "ctx")
VMEM_LIMIT = 60 << 20


def dot(a, b):
    return lax.dot_general(a, b, (((1,), (0,)), ((), ())), preferred_element_type=F32)


def dot_nt(a, b):
    return lax.dot_general(a, b, (((1,), (1,)), ((), ())), preferred_element_type=F32)


def dot_tn(a, b):
    return lax.dot_general(a, b, (((0,), (0,)), ((), ())), preferred_element_type=F32)


def lanes(start, size):
    return pl.ds(pl.multiple_of(start * size, size), size)


def rope_tables(rows):
    inverse = np.exp(np.arange(HD // 2, dtype=np.float32) * np.float32(-2.0 / HD * math.log(THETA)))
    doubled = np.concatenate([inverse, inverse]).astype(np.float32)
    angles = np.arange(rows, dtype=np.float32)[:, None] * doubled[None, :]
    sign = np.where(np.arange(HD) < HD // 2, -1.0, 1.0).astype(np.float32)
    return np.cos(angles), np.sin(angles) * sign[None, :]


def mask_block(off_bias):
    rows = lax.broadcasted_iota(jnp.int32, (QB, QB), 0)
    cols = lax.broadcasted_iota(jnp.int32, (QB, QB), 1)
    return jnp.where(rows == cols, 0.0, jnp.where(cols < rows, off_bias, MASKED))


def attn_fwd_body(
    x_ref, wqkv_ref, wo_ref, ga_ref, gq_ref, gk_ref, cos_ref, sin_ref, bias_ref,
    part_ref, q_ref, k_ref, v_ref, p_ref, xn_ref, att_ref, mask_ref,
):
    rows = x_ref.shape[0]
    nq = q_ref.shape[1] // HD
    nk = k_ref.shape[1] // HD
    gain_a = ga_ref[...]

    @pl.loop(0, rows // QB)
    def _(i):
        here = lanes(i, QB)
        x = x_ref[here, :].astype(F32)
        r = lax.rsqrt(jnp.mean(x * x, axis=-1, keepdims=True) + EPS)
        xn = (x * r * gain_a).astype(BF)
        xn_ref[here, :] = xn
        p = dot(xn, wqkv_ref[...])
        p_ref[here, :] = p[:, : (nq + nk) * HD]
        v_ref[here, :] = p[:, (nq + nk) * HD :].astype(BF)
        cos = cos_ref[here, :]
        sin = sin_ref[here, :]
        for h in range(nq + nk):
            ph = p[:, h * HD : (h + 1) * HD]
            g = gq_ref[...] if h < nq else gk_ref[...]
            n = ph * lax.rsqrt(jnp.mean(ph * ph, axis=-1, keepdims=True) + EPS) * g
            rot = (n * cos + pltpu.roll(n, HD // 2, 1) * sin).astype(BF)
            if h < nq:
                q_ref[here, h * HD : (h + 1) * HD] = rot
            else:
                k_ref[here, (h - nq) * HD : (h - nq + 1) * HD] = rot

    off = bias_ref[0:1, 0:1]
    mask_ref[...] = mask_block(off)

    @pl.loop(0, nq)
    def _(h):
        hq = lanes(h, HD)
        hk = lanes(lax.div(h * nk, nq), HD)
        for i in range(rows // QB):
            q = q_ref[i * QB : (i + 1) * QB, hq]
            es, total = [], None
            for j in range(i + 1):
                s = dot_nt(q, k_ref[j * QB : (j + 1) * QB, hk]) * (SCALE * LOG2E)
                e = jnp.exp2(s + (mask_ref[...] if j == i else off))
                t = jnp.sum(e, axis=-1, keepdims=True)
                total = t if total is None else total + t
                es.append(e)
            inv = 1.0 / total
            o = None
            for j in range(i + 1):
                c = dot((es[j] * inv).astype(BF), v_ref[j * QB : (j + 1) * QB, hk])
                o = c if o is None else o + c
            att_ref[i * QB : (i + 1) * QB, hq] = o.astype(BF)

    @pl.loop(0, rows // QB)
    def _(i):
        here = lanes(i, QB)
        part_ref[here, :] = dot(att_ref[here, :], wo_ref[...]).astype(BF)


def attn_bwd_body(
    db_ref, wo_ref, wqkv_ref, q_ref, k_ref, v_ref, p_ref, xn_ref, att_ref,
    gq_ref, gk_ref, cos_ref, sin_ref, bias_ref,
    gwqkv_ref, gwo_ref, dxn_ref, ggq_ref, ggk_ref,
    mask_ref, da_ref, dq_ref, dk_ref, dv_ref, dp_ref,
):
    rows = db_ref.shape[0]
    nq = q_ref.shape[1] // HD
    nk = k_ref.shape[1] // HD
    group = nq // nk

    @pl.loop(0, rows // QB)
    def _(i):
        here = lanes(i, QB)
        da_ref[here, :] = dot_nt(db_ref[here, :], wo_ref[...]).astype(BF)

    off = bias_ref[0:1, 0:1]
    mask_ref[...] = mask_block(off)
    dk_ref[...] = jnp.zeros_like(dk_ref)
    dv_ref[...] = jnp.zeros_like(dv_ref)

    @pl.loop(0, nq)
    def _(h):
        hq = lanes(h, HD)
        hk = lanes(lax.div(h, group), HD)
        for i in range(rows // QB):
            here = slice(i * QB, (i + 1) * QB)
            q = q_ref[here, hq]
            da = da_ref[here, hq]
            inner = jnp.sum(da.astype(F32) * att_ref[here, hq].astype(F32), axis=-1, keepdims=True)
            es, total = [], None
            for j in range(i + 1):
                s = dot_nt(q, k_ref[j * QB : (j + 1) * QB, hk]) * (SCALE * LOG2E)
                e = jnp.exp2(s + (mask_ref[...] if j == i else off))
                t = jnp.sum(e, axis=-1, keepdims=True)
                total = t if total is None else total + t
                es.append(e)
            inv = 1.0 / total
            dq = None
            for j in range(i + 1):
                keys = slice(j * QB, (j + 1) * QB)
                probs = es[j] * inv
                ds = (probs * (dot_nt(da, v_ref[keys, hk]) - inner)).astype(BF)
                c = dot(ds, k_ref[keys, hk])
                dq = c if dq is None else dq + c
                dk_ref[keys, hk] += dot_tn(ds, q)
                dv_ref[keys, hk] += dot_tn(probs.astype(BF), da)
            dq_ref[here, hq] = dq

    ggq_ref[...] = jnp.zeros_like(ggq_ref)
    ggk_ref[...] = jnp.zeros_like(ggk_ref)

    @pl.loop(0, rows // QB)
    def _(i):
        here = lanes(i, QB)
        cos = cos_ref[here, :]
        sin = sin_ref[here, :]
        sums = [jnp.zeros((1, HD), F32), jnp.zeros((1, HD), F32)]
        for h in range(nq + nk):
            which = 0 if h < nq else 1
            g = (gq_ref if h < nq else gk_ref)[...]
            cols = slice(h * HD, (h + 1) * HD)
            if h < nq:
                d = dq_ref[here, cols] * SCALE
            else:
                d = dk_ref[here, (h - nq) * HD : (h - nq + 1) * HD] * SCALE
            dn = d * cos + pltpu.roll(d * sin, HD // 2, 1)
            ph = p_ref[here, cols]
            r = lax.rsqrt(jnp.mean(ph * ph, axis=-1, keepdims=True) + EPS)
            nh = ph * r
            sums[which] += jnp.sum(dn * nh, axis=0, keepdims=True)
            cg = dn * g
            dp_ref[here, cols] = (r * (cg - nh * jnp.mean(cg * nh, axis=-1, keepdims=True))).astype(BF)
        dp_ref[here, (nq + nk) * HD :] = dv_ref[here, :].astype(BF)
        ggq_ref[0:1, :] += sums[0]
        ggk_ref[0:1, :] += sums[1]
        dxn_ref[here, :] = dot_nt(dp_ref[here, :], wqkv_ref[...]).astype(BF)

    @pl.loop(0, gwo_ref.shape[0] // 128)
    def _(i):
        cols = lanes(i, 128)
        gwo_ref[cols, :] = dot_tn(att_ref[:, cols], db_ref[...]).astype(BF)

    @pl.loop(0, gwqkv_ref.shape[0] // 128)
    def _(i):
        cols = lanes(i, 128)
        gwqkv_ref[cols, :] = dot_tn(xn_ref[:, cols], dp_ref[...]).astype(BF)


MESH = pl.DeviceIdType.MESH


def rcopy(src, dst, send, recv, **device):
    return pltpu.make_async_remote_copy(
        src_ref=src, dst_ref=dst, send_sem=send, recv_sem=recv, device_id=device, device_id_type=MESH
    )


class Place:
    def __init__(self, n):
        self.n, self.line = n, n // 2
        self.dp, self.ctx = lax.axis_index("dp"), lax.axis_index("ctx")
        self.outer, self.inner = self.dp // 2, self.dp % 2
        self.dp_inner = self.outer * 2 + 1 - self.inner
        self.dp_up, self.dp_down = self.dp + 2, self.dp - 2
        self.has_up, self.has_down = self.outer < self.line - 1, self.outer > 0
        core = self.ctx % 2
        self.c_core = self.ctx + 1 - 2 * core
        self.c_x = (self.ctx + 2) % 4
        self.c_far = 3 - self.ctx
        mine = self.dp * 4 + self.ctx
        self.slab_to = {"dp": mine % n, "ctx": mine // n}
        source = self.ctx * n + self.dp
        self.slab_from = {"dp": source // 4, "ctx": source % 4}
        self.slab_stays = source == mine


def greet(place, line, all_dp, slabs):
    barrier = pltpu.get_barrier_semaphore()

    def signal(**device):
        pl.semaphore_signal(barrier, inc=1, device_id=device, device_id_type=MESH)

    for c in (place.c_core, place.c_x, place.c_far):
        signal(ctx=c)
    count = 3
    if all_dp:
        for k in range(1, place.n):
            signal(dp=(place.dp + k) % place.n)
        count = count + place.n - 1
    elif line:
        signal(dp=place.dp_inner)
        count = count + 1
        for there, dp in ((place.has_up, place.dp_up), (place.has_down, place.dp_down)):

            @pl.when(there)
            def _():
                signal(dp=dp)

            count = count + jnp.where(there, 1, 0)
    if slabs is not None:

        @pl.when(jnp.logical_not(place.slab_stays))
        def _():
            signal(**slabs)

        count = count + jnp.where(place.slab_stays, 0, 1)
    pl.semaphore_wait(barrier, count)


class Gather:
    def __init__(self, place, bufs, sems):
        self.at, self.bufs, self.sems = place, bufs, sems

    @staticmethod
    def scratch(n, bufs):
        return pltpu.SemaphoreType.DMA((5, bufs, n // 2))

    def copy(self, b, p, way):
        at = self.at
        block = self.bufs[b].at[p * 2 + at.inner]
        device = (at.dp_up, at.dp_down, at.dp_inner)[way]
        recv = self.sems.at[4 if way == 2 else 3, b, p]
        return rcopy(block, block, self.sems.at[way, b, p], recv, dp=device)

    def send(self, p, up, down):
        at = self.at
        for b in range(len(self.bufs)):
            if up:

                @pl.when(at.has_up)
                def _():
                    self.copy(b, p, 0).start()

            if down:

                @pl.when(at.has_down)
                def _():
                    self.copy(b, p, 1).start()

            self.copy(b, p, 2).start()

    def start(self):
        self.send(self.at.outer, True, True)

    def step(self, t):
        at = self.at
        for p, there, up in ((at.outer - t, at.outer >= t, True), (at.outer + t, at.outer + t < at.line, False)):

            @pl.when(there)
            def _():
                for b in range(len(self.bufs)):
                    self.copy(b, p, 0).wait_recv()
                self.send(p, up, not up)

    def finish(self):
        at = self.at
        for b in range(len(self.bufs)):
            for p in range(at.line):
                block = self.bufs[b].at[p * 2 + 1 - at.inner]
                rcopy(block, block, self.sems.at[2, b, p], self.sems.at[4, b, p], dp=at.dp_inner).wait_recv()
                self.copy(b, p, 2).wait_send()

                @pl.when(jnp.logical_and(at.has_up, p <= at.outer))
                def _():
                    self.copy(b, p, 0).wait_send()

                @pl.when(jnp.logical_and(at.has_down, p >= at.outer))
                def _():
                    self.copy(b, p, 1).wait_send()


class Reduce:
    def __init__(self, place, parts, from_inner, from_line, sems):
        self.at, self.parts, self.from_inner, self.from_line, self.sems = place, parts, from_inner, from_line, sems

    @staticmethod
    def scratch(n, blocks):
        line = n // 2
        return (
            [pltpu.VMEM((line, *dims), dtype) for dims, dtype in blocks],
            [pltpu.VMEM((line + 1, *dims), dtype) for dims, dtype in blocks],
            pltpu.SemaphoreType.DMA((4, len(blocks), line + 1)),
        )

    def inner_copy(self, b, p):
        at = self.at
        return rcopy(
            self.parts[b].at[p * 2 + 1 - at.inner], self.from_inner[b].at[p],
            self.sems.at[0, b, p], self.sems.at[1, b, p], dp=at.dp_inner,
        )

    def line_copy(self, b, p, slot, up):
        at = self.at
        return rcopy(
            self.parts[b].at[p * 2 + at.inner], self.from_line[b].at[slot],
            self.sems.at[2, b, p], self.sems.at[3, b, slot], dp=at.dp_up if up else at.dp_down,
        )

    def start(self, which):
        at = self.at
        for d in range(at.line - 1, -1, -1):
            for p, there in ((at.outer + d, at.outer + d < at.line), (at.outer - d, at.outer >= d))[: 2 if d else 1]:

                @pl.when(there)
                def _():
                    for b in which:
                        self.inner_copy(b, p).start()

    def total(self, b, p, slots):
        s = self.parts[b][p * 2 + self.at.inner].astype(F32) + self.from_inner[b][p].astype(F32)
        for slot in slots:
            s = s + self.from_line[b][slot].astype(F32)
        return s

    def step(self, d, which):
        at = self.at
        for p, there, more, up in (
            (at.outer + d, at.outer + d < at.line, at.has_down, True),
            (at.outer - d, at.outer >= d, at.has_up, False),
        ):
            for b in which:

                @pl.when(there)
                def _():
                    self.inner_copy(b, p).wait_recv()
                    into = self.parts[b].at[p * 2 + at.inner]

                    @pl.when(more)
                    def _():
                        self.line_copy(b, p, p, up).wait_recv()
                        into[...] = self.total(b, p, [p]).astype(into.dtype)

                    @pl.when(jnp.logical_not(more))
                    def _():
                        into[...] = self.total(b, p, []).astype(into.dtype)

                    slot = p if up or d > 1 else at.line
                    self.line_copy(b, p, slot, up).start()

    def result(self, b, store):
        at = self.at
        p = at.outer
        self.inner_copy(b, p).wait_recv()
        lo, hi = at.has_down, at.has_up

        @pl.when(lo)
        def _():
            self.line_copy(b, p, p, True).wait_recv()

        @pl.when(hi)
        def _():
            self.line_copy(b, p, at.line, False).wait_recv()

        @pl.when(jnp.logical_and(lo, hi))
        def _():
            store(self.total(b, p, [p, at.line]))

        @pl.when(jnp.logical_and(lo, jnp.logical_not(hi)))
        def _():
            store(self.total(b, p, [p]))

        @pl.when(jnp.logical_and(hi, jnp.logical_not(lo)))
        def _():
            store(self.total(b, p, [at.line]))

    def finish(self):
        at = self.at
        for b in range(len(self.parts)):
            for p in range(at.line):
                self.inner_copy(b, p).wait_send()

                @pl.when(p != at.outer)
                def _():
                    self.line_copy(b, p, p, True).wait_send()


class CtxGather:
    def __init__(self, place, buf, sems):
        self.at, self.buf, self.sems = place, buf, sems

    def copy(self, k, owner):
        block = self.buf.at[owner]
        ctx = self.at.c_x if k == 1 else self.at.c_core
        return rcopy(block, block, self.sems.at[0, k], self.sems.at[1, k], ctx=ctx)

    def start(self):
        self.copy(1, self.at.ctx).start()
        self.copy(0, self.at.ctx).start()

    def forward(self):
        self.copy(1, self.at.c_x).wait_recv()
        self.copy(2, self.at.c_x).start()

    def finish(self):
        self.copy(0, self.at.c_core).wait_recv()
        self.copy(2, self.at.c_far).wait_recv()
        for k in range(3):
            self.copy(k, self.at.ctx).wait_send()


class CtxReduce:
    def __init__(self, place, part, got, sems):
        self.at, self.part, self.got, self.sems = place, part, got, sems

    def copy(self, k):
        at = self.at
        block = self.part.at[(at.c_core, at.c_far, at.c_x)[k]]
        return rcopy(block, self.got.at[k], self.sems.at[0, k], self.sems.at[1, k], ctx=at.c_x if k == 2 else at.c_core)

    def start(self):
        self.copy(1).start()
        self.copy(0).start()

    def across(self):
        self.copy(1).wait_recv()
        into = self.part.at[self.at.c_x]
        into[...] = (into[...].astype(F32) + self.got[1].astype(F32)).astype(into.dtype)
        self.copy(2).start()

    def result(self):
        self.copy(0).wait_recv()
        self.copy(2).wait_recv()
        return self.part[self.at.ctx].astype(F32) + self.got[0].astype(F32) + self.got[2].astype(F32)

    def finish(self):
        for k in range(3):
            self.copy(k).wait_send()


class Quarters:
    def __init__(self, place, src, dst, sems):
        self.at, self.src, self.dst, self.sems = place, src, dst, sems

    def copies(self):
        at = self.at
        return [
            rcopy(self.src.at[c], self.dst.at[at.ctx], self.sems.at[0, k], self.sems.at[1, k], ctx=c)
            for k, c in enumerate((at.c_x, at.c_far, at.c_core))
        ]

    def start(self):
        for c in self.copies():
            c.start()
        self.dst[self.at.ctx] = self.src[self.at.ctx]

    def finish(self):
        for c in self.copies():
            c.wait()


class Slab:
    def __init__(self, place, src, dst, sems, to):
        self.at, self.src, self.dst, self.sems, self.to = place, src, dst, sems, to

    def copy(self):
        return rcopy(self.src, self.dst, self.sems.at[0, 0], self.sems.at[1, 0], **self.to)

    def start(self):
        @pl.when(self.at.slab_stays)
        def _():
            self.dst[...] = self.src[...]

        @pl.when(jnp.logical_not(self.at.slab_stays))
        def _():
            self.copy().start()

    def finish(self):
        @pl.when(jnp.logical_not(self.at.slab_stays))
        def _():
            self.copy().wait()


class Exchange:
    def __init__(self, place, src, dst, cap, sems):
        self.at, self.src, self.dst, self.cap, self.sems = place, src, dst, cap, sems

    def rows(self, ref, j):
        return ref.at[pl.ds(pl.multiple_of(j * self.cap, self.cap), self.cap)]

    def copy(self, k):
        at = self.at
        to = (at.dp + k) % at.n
        return rcopy(self.rows(self.src, to), self.rows(self.dst, at.dp), self.sems.at[0, k], self.sems.at[1, k], dp=to)

    def start(self):
        for k in range(1, self.at.n):
            self.copy(k).start()
        self.rows(self.dst, self.at.dp)[...] = self.rows(self.src, self.at.dp)[...]

    def finish(self):
        for k in range(1, self.at.n):
            self.copy(k).wait()


def sem_pairs(count):
    return pltpu.SemaphoreType.DMA((2, count))


def fetch_body(
    n, cap,
    out_ref, lab_ref, qkv_ref, wo_src, gu_ref, wd_src, gain_ref, og_ref,
    wqkv_ref, wo_ref, gu_out, wd_out, x_ref, og_all, pick_ref, ga_ref, gm_ref, gqk_ref,
    recv, labels, gains_c, gains_n,
    s_gather, s_rows, s_labs, s_qkv, s_gu, s_wo, s_wd, s_gain, s_x, s_og,
):
    at = Place(n)
    greet(at, line=True, all_dp=True, slabs=at.slab_from)
    qkv = Quarters(at, qkv_ref, wqkv_ref.at[at.dp], s_qkv)
    wo = Slab(at, wo_src, wo_ref.at[at.slab_to["dp"]], s_wo, at.slab_to)
    rows = Exchange(at, out_ref, recv, cap, s_rows)
    labs = Exchange(at, lab_ref, labels, 8, s_labs)
    wo.start()
    qkv.start()
    labs.start()
    rows.start()
    gains = [
        rcopy(gain_ref, gains_c.at[at.ctx], s_gain.at[0, k], s_gain.at[1, k], ctx=c)
        for k, c in enumerate((at.c_x, at.c_far, at.c_core))
    ]
    for g in gains:
        g.start()
    gains_c[at.ctx] = gain_ref[...]
    wd = Slab(at, wd_src, wd_out, s_wd, at.slab_to)
    gu = Quarters(at, gu_ref, gu_out, s_gu)
    wd.start()
    gu.start()
    og_all[at.ctx] = og_ref[...]
    og = CtxGather(at, og_all, s_og)
    og.start()
    for g in gains:
        g.wait()
    gains_n[at.dp] = gains_c[0] + gains_c[1] + gains_c[2] + gains_c[3]
    qkv.finish()
    wo.finish()
    gather = Gather(at, [wqkv_ref, wo_ref, gains_n], s_gather)
    gather.start()
    gather.step(1)
    labs.finish()
    tok = x_ref.shape[1]
    slots = lax.broadcasted_iota(jnp.int32, (tok, cap), 0)
    for j in range(n):
        pick_ref[:, j * cap : (j + 1) * cap] = (slots == labels[j * 8 : j * 8 + 1, :cap]).astype(BF)
    rows.finish()
    x_ref[at.ctx] = dot(pick_ref[...], recv[...]).astype(BF)
    x = CtxGather(at, x_ref, s_x)
    x.start()
    og.forward()
    for t in range(2, at.line):
        gather.step(t)
    x.forward()
    gather.finish()
    own = 4 * ga_ref.shape[1] // (4 * n)
    ga_ref[...] = jnp.zeros_like(ga_ref)
    gm_ref[...] = jnp.zeros_like(gm_ref)
    gqk = jnp.zeros((8, 128), F32)
    for d in range(n):
        tile = slice(d * own // 128 * 128, d * own // 128 * 128 + 128)
        block = gains_n[d]
        ga_ref[0:1, tile] += block[0:1]
        gm_ref[0:1, tile] += block[1:2]
        gqk = gqk + block
    gqk_ref[...] = gqk
    for part in (og, x, wd, gu):
        part.finish()


def middle_body(
    n,
    part_in, x_ref, gm_ref, gu_ref, wd_src,
    wgu_ref, wd_ref, nm_ref, mid_ref,
    part_ref, got, s_gather, s_red, s_nm,
):
    at = Place(n)
    wgu_ref[at.dp] = gu_ref[...]
    wd_ref[at.dp] = wd_src[...]
    part_ref[...] = part_in[...]
    greet(at, line=True, all_dp=False, slabs=None)
    gather = Gather(at, [wgu_ref, wd_ref], s_gather)
    red = CtxReduce(at, part_ref, got, s_red)
    red.start()
    gather.start()
    red.across()
    gather.step(1)
    middle = x_ref[...].astype(F32) + red.result()
    mid_ref[...] = middle
    r = lax.rsqrt(jnp.mean(middle * middle, axis=-1, keepdims=True) + EPS)
    nm_ref[at.ctx] = (middle * r * gm_ref[0:1, :]).astype(BF)
    nm = CtxGather(at, nm_ref, s_nm)
    nm.start()
    for t in range(2, at.line):
        gather.step(t)
        if t == 2:
            nm.forward()
    gather.finish()
    nm.finish()
    red.finish()


def norm_back(c, v, gain):
    r = lax.rsqrt(jnp.mean(v * v, axis=-1, keepdims=True) + EPS)
    nv = v * r
    cg = c * gain
    return jnp.sum(c * nv, axis=0, keepdims=True), r * (cg - nv * jnp.mean(cg * nv, axis=-1, keepdims=True))


def back_body(
    n,
    dnm_in, outp_in, mid_ref, gm_ref, og_ref, gwgu_in, gwd_in,
    db_ref, dmid_ref, out_ref, ggm_ref, gu_ref, gd_ref,
    dnm_part, out_part, gwgu, gwd, got_d, got_o, yi0, yi1, ln0, ln1,
    s_red, s_dnm, s_out, s_db,
):
    at = Place(n)
    dnm_part[...] = dnm_in[...]
    out_part[...] = outp_in[...]
    gwgu[...] = gwgu_in[...]
    gwd[...] = gwd_in[...]
    greet(at, line=True, all_dp=False, slabs=None)
    dnm = CtxReduce(at, dnm_part, got_d, s_dnm)
    dnm.start()
    grads = Reduce(at, [gwgu, gwd], [yi0, yi1], [ln0, ln1], s_red)
    grads.start([0, 1])
    dnm.across()
    out = CtxReduce(at, out_part, got_o, s_out)
    out.start()
    grads.step(at.line - 1, [0, 1])
    gg, d = norm_back(dnm.result(), mid_ref[...], gm_ref[0:1, :])
    ggm_ref[...] = jnp.broadcast_to(gg, ggm_ref.shape)
    d = d + og_ref[...].astype(F32)
    dmid_ref[...] = d
    db_ref[at.ctx] = d.astype(BF)
    db = CtxGather(at, db_ref, s_db)
    db.start()
    out.across()
    for t in range(at.line - 2, 0, -1):
        grads.step(t, [0, 1])
        if t == 1:
            db.forward()
    out_ref[...] = (mid_ref[...] + out.result()).astype(BF)

    def to_gu(v):
        gu_ref[...] = v.astype(BF)

    def to_gd(v):
        gd_ref[...] = v.astype(BF)

    grads.result(0, to_gu)
    grads.result(1, to_gd)
    for part in (grads, db, out, dnm):
        part.finish()


def finish_body(
    n, cap,
    dxn_in, dmid_ref, x_ref, ga_ref, pick_ref, place_ref, gwqkv_in, gwo_in, gu_in, gd_in, ggm_ref, ggq_ref, ggk_ref,
    ig_ref, qkv_out, o_out, gu_out, gd_out, gain_out,
    dxn_part, gwqkv, gwo, gains, got, sendb, recv, yi0, yi1, yi2, ln0, ln1, ln2, qkv_sum, o_sum, gain_sum, gain_all,
    s_red, s_dxn, s_rows, s_gu, s_gd, s_qkv, s_o, s_gain,
):
    at = Place(n)
    dxn_part[...] = dxn_in[...]
    gwqkv[...] = gwqkv_in[...]
    gwo[...] = gwo_in[...]
    greet(at, line=True, all_dp=True, slabs=at.slab_to)
    dxn = CtxReduce(at, dxn_part, got, s_dxn)
    dxn.start()
    grads = Reduce(at, [gwqkv, gwo, gains], [yi0, yi1, yi2], [ln0, ln1, ln2], s_red)
    grads.start([0, 1])
    dxn.across()
    gu = Quarters(at, gu_in, gu_out, s_gu)
    gd = Slab(at, gd_in, gd_out, s_gd, at.slab_from)
    gu.start()
    gd.start()
    gg, d = norm_back(dxn.result(), x_ref[...].astype(F32), ga_ref[0:1, :])
    owned = (dmid_ref[...] + d).astype(BF)
    sendb[...] = dot_tn(pick_ref[...], owned).astype(BF)
    rows = Exchange(at, sendb, recv, cap, s_rows)
    rows.start()
    own = 4 * gg.shape[1] // (4 * n)
    lines = lax.broadcasted_iota(jnp.int32, (8, 128), 0)
    for j in range(n):
        tile = slice(j * own // 128 * 128, j * own // 128 * 128 + 128)
        gains[j] = (
            jnp.where(lines == 0, gg[:, tile], 0.0) + jnp.where(lines == 1, ggm_ref[0:1, tile], 0.0)
            + jnp.where(lines == 2, ggq_ref[0:1, :], 0.0) + jnp.where(lines == 3, ggk_ref[0:1, :], 0.0)
        )
    grads.start([2])
    for t in range(at.line - 1, 0, -1):
        grads.step(t, [0, 1, 2])

    def to(ref):
        def store(v):
            ref[...] = v.astype(ref.dtype)

        return store

    grads.result(0, to(qkv_sum))
    qkv = Quarters(at, qkv_sum, qkv_out, s_qkv)
    qkv.start()
    grads.result(1, to(o_sum))
    o = Slab(at, o_sum, o_out, s_o, at.slab_from)
    o.start()
    grads.result(2, to(gain_sum))
    small = [
        rcopy(gain_sum, gain_all.at[at.ctx], s_gain.at[0, k], s_gain.at[1, k], ctx=c)
        for k, c in enumerate((at.c_x, at.c_far, at.c_core))
    ]
    for g in small:
        g.start()
    gain_all[at.ctx] = gain_sum[...]
    rows.finish()
    ig_ref[...] = dot(place_ref[...], recv[...]).astype(BF)
    for g in small:
        g.wait()
    gain_out[...] = gain_all[0] + gain_all[1] + gain_all[2] + gain_all[3]
    for part in (qkv, o, gu, gd, dxn, grads):
        part.finish()


def shape(*dims, dtype=BF):
    return jax.ShapeDtypeStruct(dims, dtype)


def in_vmem(body, outs, scratch, name):
    return pl.pallas_call(
        body,
        out_shape=outs,
        scratch_shapes=scratch,
        compiler_params=pltpu.CompilerParams(vmem_limit_bytes=VMEM_LIMIT),
        name=name,
    )


def linked(body, outs, scratch, name, number):
    return pl.pallas_call(
        body,
        out_shape=outs,
        scratch_shapes=scratch,
        compiler_params=pltpu.CompilerParams(vmem_limit_bytes=VMEM_LIMIT, collective_id=number, has_side_effects=True),
        name=name,
    )


def to_quarters(weight):
    rows, cols = weight.shape
    return weight.reshape(rows, 4, cols // 4).transpose(1, 0, 2)


def from_quarters(blocks):
    n, rows, cols = blocks.shape
    return blocks.transpose(1, 0, 2).reshape(rows, n * cols)


def local(
    layer_input, dest_slot, doc_len, out_grad, attn_gain, w_query, w_key, w_value, q_gain, k_gain,
    w_out, mlp_gain, w_gate, w_up, w_down,
):
    tok, width = layer_input.shape
    n = lax.axis_size("dp")
    cap = 2 * tok // n
    rows = 4 * tok
    slabs = n * cap
    rq, ro, rd = w_query.shape[0], w_out.shape[0], w_down.shape[0]
    ff = rd * n
    owner = dest_slot // (4 * tok)
    slot = dest_slot % tok
    hot = (owner[:, None] == jnp.arange(n, dtype=jnp.int32)[None, :]).astype(BF)
    lower = (jnp.arange(tok)[:, None] > jnp.arange(tok)[None, :]).astype(BF)
    rank = jnp.sum(dot(lower, hot) * hot.astype(F32), axis=1).astype(jnp.int32)
    send_slot = owner * cap + rank
    place = send_slot[:, None] == jnp.arange(slabs, dtype=jnp.int32)[None, :]
    labels = jnp.sum(jnp.where(place, slot[:, None] - tok, 0), axis=0, dtype=jnp.int32) + tok
    place = place.astype(BF)
    outgoing = dot_tn(place, layer_input).astype(BF)
    labels = jnp.broadcast_to(jnp.pad(labels.reshape(n, 1, cap), ((0, 0), (0, 0), (0, 128 - cap))), (n, 8, 128)).reshape(n * 8, 128)
    index = lax.axis_index("dp") * 4 + lax.axis_index("ctx")
    g_rows, g_heads = attn_gain.shape[0], q_gain.shape[0]

    def at_lane(values):
        start = (index * values.shape[0]) % 128
        return lax.dynamic_update_slice(jnp.zeros((128,), F32), values.astype(F32), (start,))

    gain_block = jnp.stack([at_lane(attn_gain), at_lane(mlp_gain), at_lane(q_gain), at_lane(k_gain)])
    gain_block = jnp.pad(gain_block, ((0, 4), (0, 0)))
    qkv = jnp.concatenate([to_quarters(w_query), to_quarters(w_key), to_quarters(w_value)], axis=2)
    gu = jnp.concatenate([to_quarters(w_gate), to_quarters(w_up)], axis=2)
    nb = 4 * rq
    fw = 2 * ff
    wqkv, wo, gu, wd, x_all, og_all, pick, ga, gm, gqk = linked(
        functools.partial(fetch_body, n, cap),
        (shape(n, 4, rq, width), shape(n, ro, width), shape(4, rq, fw), shape(rd, width), shape(4, tok, width),
         shape(4, tok, width), shape(tok, slabs), shape(8, width, dtype=F32), shape(8, width, dtype=F32), shape(8, 128, dtype=F32)),
        [pltpu.VMEM((slabs, width), BF), pltpu.VMEM((n * 8, 128), jnp.int32), pltpu.VMEM((4, 8, 128), F32), pltpu.VMEM((n, 8, 128), F32),
         Gather.scratch(n, 3), sem_pairs(n), sem_pairs(n), sem_pairs(3), sem_pairs(3), sem_pairs(1), sem_pairs(1), sem_pairs(3), sem_pairs(3), sem_pairs(3)],
        "fetch", 0,
    )(outgoing, labels, qkv, w_out, gu, w_down, gain_block, out_grad)
    wqkv, wo = wqkv.reshape(width, 1024), wo.reshape(512, width)
    ga, gm, gq, gk = ga[0:1], gm[0:1], gqk[2:3], gqk[3:4]
    og_all = og_all.reshape(rows, width)
    x_own = lax.dynamic_index_in_dim(x_all, lax.axis_index("ctx"), 0, keepdims=False)
    cos, sin = rope_tables(rows)
    bias = jnp.where(doc_len[0, 0] > 0, 0.0, MASKED).astype(F32).reshape(1, 1) + jnp.zeros((8, 128), F32)
    part, q, k, v, p, xn, att = in_vmem(
        attn_fwd_body,
        (shape(rows, width), shape(rows, 512), shape(rows, 256), shape(rows, 256),
         shape(rows, 768, dtype=F32), shape(rows, width), shape(rows, 512)),
        [pltpu.VMEM((QB, QB), F32)],
        "attn_fwd",
    )(x_all.reshape(rows, width), wqkv, wo, ga, gq, gk, cos, sin, bias)
    wgu, wd, nm, middle = linked(
        functools.partial(middle_body, n),
        (shape(n, 4, rq, fw), shape(n, rd, width), shape(4, tok, width), shape(tok, width, dtype=F32)),
        [pltpu.VMEM((4, tok, width), BF), pltpu.VMEM((3, tok, width), BF), Gather.scratch(n, 2), sem_pairs(3), sem_pairs(3)],
        "middle", 1,
    )(part.reshape(4, tok, width), x_own, gm, gu, wd)
    nm = nm.reshape(rows, width)
    wgu, wd = wgu.reshape(width, fw), wd.reshape(fw // 2, width)
    wg, wu = wgu[:, : fw // 2], wgu[:, fw // 2 :]
    gate, up = dot(nm, wg), dot(nm, wu)
    s = jax.nn.sigmoid(gate)
    silu = gate * s
    hidden = (silu * up).astype(BF)
    out_part = dot(hidden, wd).astype(BF)
    dh = dot_nt(og_all, wd)
    d_gate = (dh * up * s * (1.0 + gate * (1.0 - s))).astype(BF)
    d_up = (dh * silu).astype(BF)
    gwd = dot_tn(hidden, og_all).astype(BF)
    gwgu = jnp.concatenate([dot_tn(nm, d_gate), dot_tn(nm, d_up)], axis=1).astype(BF)
    dnm_part = (dot_nt(d_gate, wg) + dot_nt(d_up, wu)).astype(BF)
    red, lines, sems = Reduce.scratch(n, [((4, rq, fw), BF), ((rd, width), BF)])
    db, d_middle, layer_output, ggm, gu, gd = linked(
        functools.partial(back_body, n),
        (shape(4, tok, width), shape(tok, width, dtype=F32), shape(tok, width), shape(8, width, dtype=F32), shape(4, rq, fw), shape(rd, width)),
        [pltpu.VMEM((4, tok, width), BF), pltpu.VMEM((4, tok, width), BF), pltpu.VMEM((n, 4, rq, fw), BF), pltpu.VMEM((n, rd, width), BF),
         pltpu.VMEM((3, tok, width), BF), pltpu.VMEM((3, tok, width), BF), *red, *lines, sems, sem_pairs(3), sem_pairs(3), sem_pairs(3)],
        "back", 2,
    )(dnm_part.reshape(4, tok, width), out_part.reshape(4, tok, width), middle, gm, out_grad,
      gwgu.reshape(n, 4, rq, fw), gwd.reshape(n, rd, width))
    gwqkv, gwo, dxn_part, ggq, ggk = in_vmem(
        attn_bwd_body,
        (shape(width, 1024), shape(512, width), shape(rows, width), shape(8, HD, dtype=F32), shape(8, HD, dtype=F32)),
        [pltpu.VMEM((QB, QB), F32), pltpu.VMEM((rows, 512), BF), pltpu.VMEM((rows, 512), F32),
         pltpu.VMEM((rows, 256), F32), pltpu.VMEM((rows, 256), F32), pltpu.VMEM((rows, 1024), BF)],
        "attn_bwd",
    )(db.reshape(rows, width), wo, wqkv, q, k, v, p, xn, att, gq, gk, cos, sin, bias)
    red, lines, sems = Reduce.scratch(n, [((4, rq, 1024), BF), ((ro, width), BF), ((8, 128), F32)])
    input_grad, g_qkv, g_o, g_gu, g_d, small = linked(
        functools.partial(finish_body, n, cap),
        (shape(tok, width), shape(4, rq, 1024), shape(ro, width), shape(4, rq, fw), shape(rd, width), shape(8, 128, dtype=F32)),
        [pltpu.VMEM((4, tok, width), BF), pltpu.VMEM((n, 4, rq, 1024), BF), pltpu.VMEM((n, ro, width), BF), pltpu.VMEM((n, 8, 128), F32),
         pltpu.VMEM((3, tok, width), BF), pltpu.VMEM((slabs, width), BF), pltpu.VMEM((slabs, width), BF), *red, *lines,
         pltpu.VMEM((4, rq, 1024), BF), pltpu.VMEM((ro, width), BF), pltpu.VMEM((8, 128), F32), pltpu.VMEM((4, 8, 128), F32),
         sems, sem_pairs(3), sem_pairs(n), sem_pairs(3), sem_pairs(1), sem_pairs(3), sem_pairs(1), sem_pairs(3)],
        "finish", 3,
    )(dxn_part.reshape(4, tok, width), d_middle, x_own, ga, pick, place, gwqkv.reshape(n, 4, rq, 1024), gwo.reshape(n, ro, width),
      gu, gd, ggm, ggq, ggk)

    def own_lanes(row, count):
        return lax.dynamic_slice(small[row], ((index * count) % 128,), (count,))

    g_qkv, g_gu = g_qkv.astype(F32), g_gu.astype(F32)
    return (
        layer_output,
        input_grad,
        own_lanes(0, g_rows),
        from_quarters(g_qkv[:, :, :512]),
        from_quarters(g_qkv[:, :, 512:768]),
        from_quarters(g_qkv[:, :, 768:]),
        own_lanes(2, g_heads),
        own_lanes(3, g_heads),
        g_o.astype(F32),
        own_lanes(1, g_rows),
        from_quarters(g_gu[:, :, : fw // 2]),
        from_quarters(g_gu[:, :, fw // 2 :]),
        g_d.astype(F32),
    )


def solution(mesh):
    rows = P(BOTH, None)
    vec = P(BOTH)
    return jax.shard_map(
        local,
        mesh=mesh,
        in_specs=(rows, vec, P("dp", None), rows, vec, rows, rows, rows, vec, vec, rows, vec, rows, rows, rows),
        out_specs=(rows, rows, vec, rows, rows, rows, vec, vec, rows, vec, rows, rows, rows),
        check_vma=False,
    )
```

```python
import functools
import math

import jax
import jax.numpy as jnp
import numpy as np
from jax import lax
from jax.experimental import pallas as pl
from jax.experimental.pallas import tpu as pltpu
from jax.sharding import PartitionSpec as P

H = 16
KVH = 8
HD = 128
EPS = 1e-06
THETA = 1000000.0
MASKED = -1e30
QB = 256
SCALE = HD ** (-0.5)
LOG2E = math.log2(math.e)
BF = jnp.bfloat16
F32 = jnp.float32
BOTH = ("dp", "ctx")
VMEM_LIMIT = 60 << 20


def dot(a, b):
    return lax.dot_general(a, b, (((1,), (0,)), ((), ())), preferred_element_type=F32)


def dot_nt(a, b):
    return lax.dot_general(a, b, (((1,), (1,)), ((), ())), preferred_element_type=F32)


def dot_tn(a, b):
    return lax.dot_general(a, b, (((0,), (0,)), ((), ())), preferred_element_type=F32)


def lanes(start, size):
    return pl.ds(pl.multiple_of(start * size, size), size)


def rope_tables(rows):
    inverse = np.exp(np.arange(HD // 2, dtype=np.float32) * np.float32(-2.0 / HD * math.log(THETA)))
    doubled = np.concatenate([inverse, inverse]).astype(np.float32)
    angles = np.arange(rows, dtype=np.float32)[:, None] * doubled[None, :]
    sign = np.where(np.arange(HD) < HD // 2, -1.0, 1.0).astype(np.float32)
    return np.cos(angles), np.sin(angles) * sign[None, :]


def mask_block(off_bias):
    rows = lax.broadcasted_iota(jnp.int32, (QB, QB), 0)
    cols = lax.broadcasted_iota(jnp.int32, (QB, QB), 1)
    return jnp.where(rows == cols, 0.0, jnp.where(cols < rows, off_bias, MASKED))


def rows_of(ref):
    value = ref[...]
    return value.reshape(-1, value.shape[-1])


def attn_project(x_ref, w, ga, gq, gk, cos_ref, sin_ref, q_ref, k_ref, v_ref, p_ref, xn_ref):
    rows = xn_ref.shape[0]
    tok = x_ref.shape[1]
    nq = q_ref.shape[1] // HD
    nk = k_ref.shape[1] // HD

    @pl.loop(0, rows // tok)
    def _(i):
        here = lanes(i, tok)
        x = x_ref[i].astype(F32)
        r = lax.rsqrt(jnp.mean(x * x, axis=-1, keepdims=True) + EPS)
        xn = (x * r * ga[0:1, :]).astype(BF)
        xn_ref[here, :] = xn
        p = dot(xn, rows_of(w))
        p_ref[here, :] = p[:, : (nq + nk) * HD]
        v_ref[here, :] = p[:, (nq + nk) * HD :].astype(BF)
        cos = cos_ref[here, :]
        sin = sin_ref[here, :]
        for h in range(nq + nk):
            ph = p[:, h * HD : (h + 1) * HD]
            g = gq if h < nq else gk
            nv = ph * lax.rsqrt(jnp.mean(ph * ph, axis=-1, keepdims=True) + EPS) * g
            rot = (nv * cos + pltpu.roll(nv, HD // 2, 1) * sin).astype(BF)
            if h < nq:
                q_ref[here, h * HD : (h + 1) * HD] = rot
            else:
                k_ref[here, (h - nq) * HD : (h - nq + 1) * HD] = rot


def attn_head(h, off, q_ref, k_ref, v_ref, att_ref, mask_ref):
    rows = q_ref.shape[0]
    group = q_ref.shape[1] // k_ref.shape[1]
    hq = lanes(h, HD)
    hk = lanes(h // group, HD)
    for i in range(rows // QB):
        q = q_ref[i * QB : (i + 1) * QB, hq]
        es, total = [], None
        for j in range(i + 1):
            s = dot_nt(q, k_ref[j * QB : (j + 1) * QB, hk]) * (SCALE * LOG2E)
            e = jnp.exp2(s + (mask_ref[...] if j == i else off))
            t = jnp.sum(e, axis=-1, keepdims=True)
            total = t if total is None else total + t
            es.append(e)
        inv = 1.0 / total
        o = None
        for j in range(i + 1):
            c = dot((es[j] * inv).astype(BF), v_ref[j * QB : (j + 1) * QB, hk])
            o = c if o is None else o + c
        att_ref[i * QB : (i + 1) * QB, hq] = o.astype(BF)


def attn_head_back(h, off, q_ref, k_ref, v_ref, att_ref, da_ref, dq_ref, dk_ref, dv_ref, mask_ref):
    rows = q_ref.shape[0]
    group = q_ref.shape[1] // k_ref.shape[1]
    hq = lanes(h, HD)
    hk = lanes(h // group, HD)
    for i in range(rows // QB):
        here = slice(i * QB, (i + 1) * QB)
        q = q_ref[here, hq]
        da = da_ref[here, hq]
        inner = jnp.sum(da.astype(F32) * att_ref[here, hq].astype(F32), axis=-1, keepdims=True)
        es, total = [], None
        for j in range(i + 1):
            s = dot_nt(q, k_ref[j * QB : (j + 1) * QB, hk]) * (SCALE * LOG2E)
            e = jnp.exp2(s + (mask_ref[...] if j == i else off))
            t = jnp.sum(e, axis=-1, keepdims=True)
            total = t if total is None else total + t
            es.append(e)
        inv = 1.0 / total
        dq = None
        for j in range(i + 1):
            keys = slice(j * QB, (j + 1) * QB)
            probs = es[j] * inv
            ds = (probs * (dot_nt(da, v_ref[keys, hk]) - inner)).astype(BF)
            c = dot(ds, k_ref[keys, hk])
            dq = c if dq is None else dq + c
            dk_ref[keys, hk] += dot_tn(ds, q)
            dv_ref[keys, hk] += dot_tn(probs.astype(BF), da)
        dq_ref[here, hq] = dq


def attn_unproject(gq, gk, cos_ref, sin_ref, p_ref, dq_ref, dk_ref, dv_ref, dp_ref, w, dxn_ref, ggq_ref, ggk_ref):
    rows = p_ref.shape[0]
    tok = dxn_ref.shape[1]
    nq = dq_ref.shape[1] // HD
    nk = dk_ref.shape[1] // HD
    ggq_ref[...] = jnp.zeros_like(ggq_ref)
    ggk_ref[...] = jnp.zeros_like(ggk_ref)

    @pl.loop(0, rows // tok)
    def _(i):
        here = lanes(i, tok)
        cos = cos_ref[here, :]
        sin = sin_ref[here, :]
        sums = [jnp.zeros((1, HD), F32), jnp.zeros((1, HD), F32)]
        for h in range(nq + nk):
            which = 0 if h < nq else 1
            g = gq if h < nq else gk
            cols = slice(h * HD, (h + 1) * HD)
            if h < nq:
                d = dq_ref[here, cols] * SCALE
            else:
                d = dk_ref[here, (h - nq) * HD : (h - nq + 1) * HD] * SCALE
            dn = d * cos + pltpu.roll(d * sin, HD // 2, 1)
            ph = p_ref[here, cols]
            r = lax.rsqrt(jnp.mean(ph * ph, axis=-1, keepdims=True) + EPS)
            nh = ph * r
            sums[which] += jnp.sum(dn * nh, axis=0, keepdims=True)
            cg = dn * g
            dp_ref[here, cols] = (r * (cg - nh * jnp.mean(cg * nh, axis=-1, keepdims=True))).astype(BF)
        dp_ref[here, (nq + nk) * HD :] = dv_ref[here, :].astype(BF)
        ggq_ref[0:1, :] += sums[0]
        ggk_ref[0:1, :] += sums[1]
        dxn_ref[i] = dot_nt(dp_ref[here, :], rows_of(w)).astype(BF)


def weight_grad(out_ref, left_ref, right, chunk=128):
    size = math.prod(out_ref.shape[1:-1])
    width = out_ref.shape[-1]

    @pl.loop(0, left_ref.shape[1] // chunk)
    def _(i):
        g = dot_tn(left_ref[:, lanes(i, chunk)], rows_of(right)).astype(BF)
        for j in range(chunk // size):
            out_ref[i * (chunk // size) + j] = g[j * size : (j + 1) * size].reshape(out_ref.shape[1:-1] + (width,))


MESH = pl.DeviceIdType.MESH


def rcopy(src, dst, send, recv, **device):
    return pltpu.make_async_remote_copy(
        src_ref=src, dst_ref=dst, send_sem=send, recv_sem=recv, device_id=device, device_id_type=MESH
    )


class Place:
    def __init__(self, n):
        self.n, self.line = n, n // 2
        self.dp, self.ctx = lax.axis_index("dp"), lax.axis_index("ctx")
        self.outer, self.inner = self.dp // 2, self.dp % 2
        self.dp_inner = self.outer * 2 + 1 - self.inner
        self.dp_up, self.dp_down = self.dp + 2, self.dp - 2
        self.has_up, self.has_down = self.outer < self.line - 1, self.outer > 0
        core = self.ctx % 2
        self.c_core = self.ctx + 1 - 2 * core
        self.c_x = (self.ctx + 2) % 4
        self.c_far = 3 - self.ctx
        mine = self.dp * 4 + self.ctx
        self.slab_to = {"dp": mine % n, "ctx": mine // n}
        source = self.ctx * n + self.dp
        self.slab_from = {"dp": source // 4, "ctx": source % 4}
        self.slab_stays = source == mine


def greet(place, line, all_dp, slabs):
    barrier = pltpu.get_barrier_semaphore()

    def signal(**device):
        pl.semaphore_signal(barrier, inc=1, device_id=device, device_id_type=MESH)

    for c in (place.c_core, place.c_x, place.c_far):
        signal(ctx=c)
    count = 3
    if all_dp:
        for k in range(1, place.n):
            signal(dp=(place.dp + k) % place.n)
        count = count + place.n - 1
    elif line:
        signal(dp=place.dp_inner)
        count = count + 1
        for there, dp in ((place.has_up, place.dp_up), (place.has_down, place.dp_down)):

            @pl.when(there)
            def _():
                signal(dp=dp)

            count = count + jnp.where(there, 1, 0)
    if slabs is not None:

        @pl.when(jnp.logical_not(place.slab_stays))
        def _():
            signal(**slabs)

        count = count + jnp.where(place.slab_stays, 0, 1)
    pl.semaphore_wait(barrier, count)


class Gather:
    def __init__(self, place, bufs, sems):
        self.at, self.bufs, self.sems = place, bufs, sems

    @staticmethod
    def scratch(n, bufs):
        return pltpu.SemaphoreType.DMA((5, bufs, n // 2))

    def copy(self, b, p, way):
        at = self.at
        block = self.bufs[b].at[p * 2 + at.inner]
        device = (at.dp_up, at.dp_down, at.dp_inner)[way]
        recv = self.sems.at[4 if way == 2 else 3, b, p]
        return rcopy(block, block, self.sems.at[way, b, p], recv, dp=device)

    def send(self, p, up, down):
        at = self.at
        for b in range(len(self.bufs)):
            if up:

                @pl.when(at.has_up)
                def _():
                    self.copy(b, p, 0).start()

            if down:

                @pl.when(at.has_down)
                def _():
                    self.copy(b, p, 1).start()

            self.copy(b, p, 2).start()

    def start(self):
        self.send(self.at.outer, True, True)

    def step(self, t):
        at = self.at
        for p, there, up in ((at.outer - t, at.outer >= t, True), (at.outer + t, at.outer + t < at.line, False)):

            @pl.when(there)
            def _():
                for b in range(len(self.bufs)):
                    self.copy(b, p, 0).wait_recv()
                self.send(p, up, not up)

    def arrive(self):
        at = self.at
        for b in range(len(self.bufs)):
            for p in range(at.line):
                block = self.bufs[b].at[p * 2 + 1 - at.inner]
                rcopy(block, block, self.sems.at[2, b, p], self.sems.at[4, b, p], dp=at.dp_inner).wait_recv()

    def finish(self):
        at = self.at
        for b in range(len(self.bufs)):
            for p in range(at.line):
                self.copy(b, p, 2).wait_send()

                @pl.when(jnp.logical_and(at.has_up, p <= at.outer))
                def _():
                    self.copy(b, p, 0).wait_send()

                @pl.when(jnp.logical_and(at.has_down, p >= at.outer))
                def _():
                    self.copy(b, p, 1).wait_send()


class Reduce:
    def __init__(self, place, parts, from_inner, from_line, sems):
        self.at, self.parts, self.from_inner, self.from_line, self.sems = place, parts, from_inner, from_line, sems

    @staticmethod
    def scratch(n, blocks):
        line = n // 2
        return (
            [pltpu.VMEM((line, *dims), dtype) for dims, dtype in blocks],
            [pltpu.VMEM((line + 1, *dims), dtype) for dims, dtype in blocks],
            pltpu.SemaphoreType.DMA((4, len(blocks), line + 1)),
        )

    def inner_copy(self, b, p):
        at = self.at
        return rcopy(
            self.parts[b].at[p * 2 + 1 - at.inner], self.from_inner[b].at[p],
            self.sems.at[0, b, p], self.sems.at[1, b, p], dp=at.dp_inner,
        )

    def line_copy(self, b, p, slot, up):
        at = self.at
        return rcopy(
            self.from_inner[b].at[p], self.from_line[b].at[slot],
            self.sems.at[2, b, p], self.sems.at[3, b, slot], dp=at.dp_up if up else at.dp_down,
        )

    def start(self, which):
        at = self.at
        for d in range(at.line - 1, -1, -1):
            for p, there in ((at.outer + d, at.outer + d < at.line), (at.outer - d, at.outer >= d))[: 2 if d else 1]:

                @pl.when(there)
                def _():
                    for b in which:
                        self.inner_copy(b, p).start()

    def total(self, b, p, slots):
        s = self.parts[b][p * 2 + self.at.inner].astype(F32) + self.from_inner[b][p].astype(F32)
        for slot in slots:
            s = s + self.from_line[b][slot].astype(F32)
        return s

    def step(self, d, which):
        at = self.at
        for p, there, more, up in (
            (at.outer + d, at.outer + d < at.line, at.has_down, True),
            (at.outer - d, at.outer >= d, at.has_up, False),
        ):
            for b in which:

                @pl.when(there)
                def _():
                    self.inner_copy(b, p).wait_recv()
                    into = self.from_inner[b].at[p]

                    @pl.when(more)
                    def _():
                        self.line_copy(b, p, p, up).wait_recv()
                        into[...] = self.total(b, p, [p]).astype(into.dtype)

                    @pl.when(jnp.logical_not(more))
                    def _():
                        into[...] = self.total(b, p, []).astype(into.dtype)

                    slot = p if up or d > 1 else at.line
                    self.line_copy(b, p, slot, up).start()

    def result(self, b, store):
        at = self.at
        p = at.outer
        self.inner_copy(b, p).wait_recv()
        lo, hi = at.has_down, at.has_up

        @pl.when(lo)
        def _():
            self.line_copy(b, p, p, True).wait_recv()

        @pl.when(hi)
        def _():
            self.line_copy(b, p, at.line, False).wait_recv()

        @pl.when(jnp.logical_and(lo, hi))
        def _():
            store(self.total(b, p, [p, at.line]))

        @pl.when(jnp.logical_and(lo, jnp.logical_not(hi)))
        def _():
            store(self.total(b, p, [p]))

        @pl.when(jnp.logical_and(hi, jnp.logical_not(lo)))
        def _():
            store(self.total(b, p, [at.line]))

    def finish(self):
        at = self.at
        for b in range(len(self.parts)):
            for p in range(at.line):
                self.inner_copy(b, p).wait_send()

                @pl.when(p != at.outer)
                def _():
                    self.line_copy(b, p, p, True).wait_send()


class CtxGather:
    def __init__(self, place, buf, sems):
        self.at, self.buf, self.sems = place, buf, sems

    def copy(self, k, owner):
        block = self.buf.at[owner]
        ctx = self.at.c_x if k == 1 else self.at.c_core
        return rcopy(block, block, self.sems.at[0, k], self.sems.at[1, k], ctx=ctx)

    def start(self):
        self.copy(1, self.at.ctx).start()
        self.copy(0, self.at.ctx).start()

    def forward(self):
        self.copy(1, self.at.c_x).wait_recv()
        self.copy(2, self.at.c_x).start()

    def arrive(self):
        self.copy(0, self.at.c_core).wait_recv()
        self.copy(2, self.at.c_far).wait_recv()

    def finish(self):
        for k in range(3):
            self.copy(k, self.at.ctx).wait_send()


class CtxReduce:
    def __init__(self, place, part, got, sems):
        self.at, self.part, self.got, self.sems = place, part, got, sems

    def copy(self, k):
        at = self.at
        block = self.got.at[1] if k == 2 else self.part.at[(at.c_core, at.c_far)[k]]
        return rcopy(block, self.got.at[k], self.sems.at[0, k], self.sems.at[1, k], ctx=at.c_x if k == 2 else at.c_core)

    def start(self):
        self.copy(1).start()
        self.copy(0).start()

    def across(self):
        self.copy(1).wait_recv()
        into = self.got.at[1]
        into[...] = (self.part[self.at.c_x].astype(F32) + into[...].astype(F32)).astype(into.dtype)
        self.copy(2).start()

    def result(self):
        self.copy(0).wait_recv()
        self.copy(2).wait_recv()
        return self.part[self.at.ctx].astype(F32) + self.got[0].astype(F32) + self.got[2].astype(F32)

    def finish(self):
        for k in range(3):
            self.copy(k).wait_send()


class Quarters:
    def __init__(self, place, src, dst, sems):
        self.at, self.src, self.dst, self.sems = place, src, dst, sems

    def copies(self):
        at = self.at
        return [
            rcopy(self.src.at[c], self.dst.at[at.ctx], self.sems.at[0, k], self.sems.at[1, k], ctx=c)
            for k, c in enumerate((at.c_x, at.c_far, at.c_core))
        ]

    def start(self):
        for c in self.copies():
            c.start()
        self.dst[self.at.ctx] = self.src[self.at.ctx]

    def finish(self):
        for c in self.copies():
            c.wait()


class Slab:
    def __init__(self, place, src, dst, sems, to):
        self.at, self.src, self.dst, self.sems, self.to = place, src, dst, sems, to

    def copy(self):
        return rcopy(self.src, self.dst, self.sems.at[0, 0], self.sems.at[1, 0], **self.to)

    def start(self):
        @pl.when(self.at.slab_stays)
        def _():
            self.dst[...] = self.src[...]

        @pl.when(jnp.logical_not(self.at.slab_stays))
        def _():
            self.copy().start()

    def finish(self):
        @pl.when(jnp.logical_not(self.at.slab_stays))
        def _():
            self.copy().wait()


class Exchange:
    def __init__(self, place, src, dst, cap, sems):
        self.at, self.src, self.dst, self.cap, self.sems = place, src, dst, cap, sems

    def rows(self, ref, j):
        return ref.at[pl.ds(pl.multiple_of(j * self.cap, self.cap), self.cap)]

    def copy(self, k):
        at = self.at
        to = (at.dp + k) % at.n
        return rcopy(self.rows(self.src, to), self.rows(self.dst, at.dp), self.sems.at[0, k], self.sems.at[1, k], dp=to)

    def start(self):
        for k in range(1, self.at.n):
            self.copy(k).start()
        self.rows(self.dst, self.at.dp)[...] = self.rows(self.src, self.at.dp)[...]

    def finish(self):
        for k in range(1, self.at.n):
            self.copy(k).wait()


def sem_pairs(count):
    return pltpu.SemaphoreType.DMA((2, count))


def forward_body(
    n, cap,
    out_ref, lab_ref, qkv_ref, wo_src, gu_ref, wd_src, gain_ref, og_ref, cos_ref, sin_ref, bias_ref,
    wqkv_ref, wo_ref, wgu_ref, wd_ref, x_own, og_all, pick_ref, ga_ref, gm_ref, gqk_ref,
    q_ref, k_ref, v_ref, p_ref, xn_ref, att_ref, nm_ref, mid_ref,
    recv, labels, gains_c, gains_n, x_ref, part_ref, got, mask_ref,
    s_ga, s_gb, s_gc, s_rows, s_labs, s_qkv, s_gu, s_wo, s_wd, s_gain, s_x, s_og, s_red, s_nm,
):
    at = Place(n)
    greet(at, line=True, all_dp=True, slabs=at.slab_from)
    qkv = Quarters(at, qkv_ref, wqkv_ref.at[at.dp], s_qkv)
    rows = Exchange(at, out_ref, recv, cap, s_rows)
    labs = Exchange(at, lab_ref, labels, 8, s_labs)
    qkv.start()
    gains = [
        rcopy(gain_ref, gains_c.at[at.ctx], s_gain.at[0, k], s_gain.at[1, k], ctx=c)
        for k, c in enumerate((at.c_x, at.c_far, at.c_core))
    ]
    for g in gains:
        g.start()
    gains_c[at.ctx] = gain_ref[...]
    labs.start()
    rows.start()
    for g in gains:
        g.wait()
    gains_n[at.dp] = gains_c[0] + gains_c[1] + gains_c[2] + gains_c[3]
    qkv.finish()
    first = Gather(at, [wqkv_ref, gains_n], s_ga)
    first.start()
    wo = Slab(at, wo_src, wo_ref.at[at.slab_to["dp"]], s_wo, at.slab_to)
    wd = Slab(at, wd_src, wd_ref.at[at.slab_to["dp"]], s_wd, at.slab_to)
    gu = Quarters(at, gu_ref, wgu_ref.at[at.dp], s_gu)
    wo.start()
    gu.start()
    wd.start()
    og_all[at.ctx] = og_ref[...]
    og = CtxGather(at, og_all, s_og)
    labs.finish()
    tok = x_ref.shape[1]
    slots = lax.broadcasted_iota(jnp.int32, (tok, cap), 0)
    for j in range(n):
        pick_ref[:, j * cap : (j + 1) * cap] = (slots == labels[j * 8 : j * 8 + 1, :cap]).astype(BF)
    first.step(1)
    rows.finish()
    owned = dot(pick_ref[...], recv[...]).astype(BF)
    x_ref[at.ctx] = owned
    x_own[...] = owned
    x = CtxGather(at, x_ref, s_x)
    x.start()
    og.start()
    for t in range(2, at.line):
        first.step(t)
    wo.finish()
    second = Gather(at, [wo_ref], s_gb)
    second.start()
    wd.finish()
    gu.finish()
    third = Gather(at, [wgu_ref, wd_ref], s_gc)
    third.start()
    x.forward()
    first.arrive()
    own = 4 * ga_ref.shape[1] // (4 * n)
    ga_ref[...] = jnp.zeros_like(ga_ref)
    gm_ref[...] = jnp.zeros_like(gm_ref)
    gqk = jnp.zeros((8, 128), F32)
    for d in range(n):
        tile = slice(d * own // 128 * 128, d * own // 128 * 128 + 128)
        block = gains_n[d]
        ga_ref[0:1, tile] += block[0:1]
        gm_ref[0:1, tile] += block[1:2]
        gqk = gqk + block
    gqk_ref[...] = gqk
    off = bias_ref[0:1, 0:1]
    mask_ref[...] = mask_block(off)
    x.arrive()
    attn_project(x_ref, wqkv_ref, ga_ref, gqk[2:3], gqk[3:4], cos_ref, sin_ref, q_ref, k_ref, v_ref, p_ref, xn_ref)
    second.step(1)
    third.step(1)
    og.forward()
    nq = q_ref.shape[1] // HD
    for half in range(2):

        @pl.loop(half * nq // 2, (half + 1) * nq // 2)
        def _(h):
            attn_head(h, off, q_ref, k_ref, v_ref, att_ref, mask_ref)

        if half == 0:
            for t in range(2, at.line):
                second.step(t)
    second.arrive()

    @pl.loop(0, 4)
    def _(i):
        part_ref[i] = dot(att_ref[lanes(i, tok), :], rows_of(wo_ref)).astype(BF)

    red = CtxReduce(at, part_ref, got, s_red)
    red.start()
    red.across()
    third.step(2)
    middle = x_own[...].astype(F32) + red.result()
    mid_ref[...] = middle
    r = lax.rsqrt(jnp.mean(middle * middle, axis=-1, keepdims=True) + EPS)
    nm_ref[at.ctx] = (middle * r * gm_ref[0:1, :]).astype(BF)
    nm = CtxGather(at, nm_ref, s_nm)
    nm.start()
    for t in range(3, at.line):
        third.step(t)
    nm.forward()
    nm.arrive()
    og.arrive()
    third.arrive()
    for part in (first, second, third, og, x, nm, red):
        part.finish()


def norm_back(c, v, gain):
    r = lax.rsqrt(jnp.mean(v * v, axis=-1, keepdims=True) + EPS)
    nv = v * r
    cg = c * gain
    return jnp.sum(c * nv, axis=0, keepdims=True), r * (cg - nv * jnp.mean(cg * nv, axis=-1, keepdims=True))


def into(ref):
    def store(v):
        ref[...] = v.astype(ref.dtype)

    return store


def backward_body(
    n, cap,
    dnm_part, out_part, mid_ref, x_ref, og_ref, ga_ref, gm_ref, gqk_ref, gwgu, gwd, wo_ref, wqkv_ref,
    q_ref, k_ref, v_ref, p_ref, xn_ref, att_ref, pick_ref, place_ref, cos_ref, sin_ref, bias_ref,
    ig_ref, layer_ref, qkv_out, o_out, gu_out, gd_out, gain_out,
    got_d, got_o, got_x, db_ref, dmid_ref, mask_ref, da_ref, dq_ref, dk_ref, dv_ref, dp_ref, ggq_ref, ggk_ref, ggm_ref,
    gwqkv, gwo, gains, sendb, recv,
    yi0, yi1, ln0, ln1, s_ra, yo, lo, s_rb, yq, yg, lq, lg, s_rc,
    gu_sum, gd_sum, qkv_sum, o_sum, gain_sum, gain_all,
    s_dnm, s_out, s_db, s_dxn, s_rows, s_gu, s_gd, s_qkv, s_o, s_gain,
):
    at = Place(n)
    greet(at, line=True, all_dp=True, slabs=at.slab_to)
    dnm = CtxReduce(at, dnm_part, got_d, s_dnm)
    dnm.start()
    first = Reduce(at, [gwgu, gwd], [yi0, yi1], [ln0, ln1], s_ra)
    first.start([0, 1])
    dnm.across()
    out = CtxReduce(at, out_part, got_o, s_out)
    off = bias_ref[0:1, 0:1]
    mask_ref[...] = mask_block(off)
    dk_ref[...] = jnp.zeros_like(dk_ref)
    dv_ref[...] = jnp.zeros_like(dv_ref)
    first.step(at.line - 1, [0, 1])
    gg, d = norm_back(dnm.result(), mid_ref[...], gm_ref[0:1, :])
    ggm_ref[...] = gg
    d = d + og_ref[...].astype(F32)
    dmid_ref[...] = d
    db_ref[at.ctx] = d.astype(BF)
    db = CtxGather(at, db_ref, s_db)
    db.start()
    out.start()
    for t in range(at.line - 2, 1, -1):
        first.step(t, [0, 1])
    db.forward()
    out.across()
    db.arrive()
    tok = db_ref.shape[1]

    @pl.loop(0, 4)
    def _(i):
        da_ref[lanes(i, tok), :] = dot_nt(db_ref[i], rows_of(wo_ref)).astype(BF)

    weight_grad(gwo, att_ref, db_ref)
    first.step(1, [0, 1])
    second = Reduce(at, [gwo], [yo], [lo], s_rb)
    second.start([0])
    nq = q_ref.shape[1] // HD
    for quarter in range(4):

        @pl.loop(quarter * nq // 4, (quarter + 1) * nq // 4)
        def _(h):
            attn_head_back(h, off, q_ref, k_ref, v_ref, att_ref, da_ref, dq_ref, dk_ref, dv_ref, mask_ref)

        if quarter == 0:
            first.result(0, into(gu_sum))
            first.result(1, into(gd_sum))
            gu = Quarters(at, gu_sum, gu_out, s_gu)
            gd = Slab(at, gd_sum, gd_out, s_gd, at.slab_from)
            gu.start()
            gd.start()
            second.step(at.line - 1, [0])
        if quarter == 1:
            for t in range(at.line - 2, 1, -1):
                second.step(t, [0])
            layer_ref[...] = (mid_ref[...] + out.result()).astype(BF)
        if quarter == 2:
            second.step(1, [0])
    second.result(0, into(o_sum))
    o = Slab(at, o_sum, o_out, s_o, at.slab_from)
    o.start()
    db.finish()
    dxn_ref = db_ref
    attn_unproject(gqk_ref[2:3, :], gqk_ref[3:4, :], cos_ref, sin_ref, p_ref, dq_ref, dk_ref, dv_ref, dp_ref, wqkv_ref, dxn_ref, ggq_ref, ggk_ref)
    dxn = CtxReduce(at, dxn_ref, got_x, s_dxn)
    dxn.start()
    weight_grad(gwqkv, xn_ref, dp_ref)
    third = Reduce(at, [gwqkv, gains], [yq, yg], [lq, lg], s_rc)
    third.start([0])
    dxn.across()
    third.step(at.line - 1, [0])
    gg, d = norm_back(dxn.result(), x_ref[...].astype(F32), ga_ref[0:1, :])
    owned = (dmid_ref[...] + d).astype(BF)
    sendb[...] = dot_tn(pick_ref[...], owned).astype(BF)
    rows = Exchange(at, sendb, recv, cap, s_rows)
    rows.start()
    own = 4 * gg.shape[1] // (4 * n)
    lines = lax.broadcasted_iota(jnp.int32, (8, 128), 0)
    for j in range(n):
        tile = slice(j * own // 128 * 128, j * own // 128 * 128 + 128)
        gains[j] = (
            jnp.where(lines == 0, gg[:, tile], 0.0) + jnp.where(lines == 1, ggm_ref[0:1, tile], 0.0)
            + jnp.where(lines == 2, ggq_ref[0:1, :], 0.0) + jnp.where(lines == 3, ggk_ref[0:1, :], 0.0)
        )
    third.start([1])
    third.step(at.line - 1, [1])
    for t in range(at.line - 2, 0, -1):
        third.step(t, [0, 1])
    third.result(0, into(qkv_sum))
    qkv = Quarters(at, qkv_sum, qkv_out, s_qkv)
    qkv.start()
    third.result(1, into(gain_sum))
    small = [
        rcopy(gain_sum, gain_all.at[at.ctx], s_gain.at[0, k], s_gain.at[1, k], ctx=c)
        for k, c in enumerate((at.c_x, at.c_far, at.c_core))
    ]
    for g in small:
        g.start()
    gain_all[at.ctx] = gain_sum[...]
    rows.finish()
    ig_ref[...] = dot(place_ref[...], recv[...]).astype(BF)
    for g in small:
        g.wait()
    gain_out[...] = gain_all[0] + gain_all[1] + gain_all[2] + gain_all[3]
    for part in (qkv, o, gu, gd, dxn, out, dnm, first, second, third):
        part.finish()


def shape(*dims, dtype=BF):
    return jax.ShapeDtypeStruct(dims, dtype)


def linked(body, outs, scratch, name, number):
    return pl.pallas_call(
        body,
        out_shape=outs,
        scratch_shapes=scratch,
        compiler_params=pltpu.CompilerParams(vmem_limit_bytes=VMEM_LIMIT, collective_id=number, has_side_effects=True),
        name=name,
    )


def to_quarters(weight):
    rows, cols = weight.shape
    return weight.reshape(rows, 4, cols // 4).transpose(1, 0, 2)


def from_quarters(blocks):
    n, rows, cols = blocks.shape
    return blocks.transpose(1, 0, 2).reshape(rows, n * cols)


def local(
    layer_input, dest_slot, doc_len, out_grad, attn_gain, w_query, w_key, w_value, q_gain, k_gain,
    w_out, mlp_gain, w_gate, w_up, w_down,
):
    tok, width = layer_input.shape
    n = lax.axis_size("dp")
    cap = 2 * tok // n
    rows = 4 * tok
    slabs = n * cap
    rq, ro, rd = w_query.shape[0], w_out.shape[0], w_down.shape[0]
    ff = rd * n
    owner = dest_slot // (4 * tok)
    slot = dest_slot % tok
    hot = (owner[:, None] == jnp.arange(n, dtype=jnp.int32)[None, :]).astype(BF)
    lower = (jnp.arange(tok)[:, None] > jnp.arange(tok)[None, :]).astype(BF)
    rank = jnp.sum(dot(lower, hot) * hot.astype(F32), axis=1).astype(jnp.int32)
    send_slot = owner * cap + rank
    place = send_slot[:, None] == jnp.arange(slabs, dtype=jnp.int32)[None, :]
    labels = jnp.sum(jnp.where(place, slot[:, None] - tok, 0), axis=0, dtype=jnp.int32) + tok
    place = place.astype(BF)
    outgoing = dot_tn(place, layer_input).astype(BF)
    labels = jnp.broadcast_to(jnp.pad(labels.reshape(n, 1, cap), ((0, 0), (0, 0), (0, 128 - cap))), (n, 8, 128)).reshape(n * 8, 128)
    index = lax.axis_index("dp") * 4 + lax.axis_index("ctx")
    g_rows, g_heads = attn_gain.shape[0], q_gain.shape[0]

    def at_lane(values):
        start = (index * values.shape[0]) % 128
        return lax.dynamic_update_slice(jnp.zeros((128,), F32), values.astype(F32), (start,))

    gain_block = jnp.stack([at_lane(attn_gain), at_lane(mlp_gain), at_lane(q_gain), at_lane(k_gain)])
    gain_block = jnp.pad(gain_block, ((0, 4), (0, 0)))
    qkv = jnp.concatenate([to_quarters(w_query), to_quarters(w_key), to_quarters(w_value)], axis=2)
    gu = jnp.concatenate([to_quarters(w_gate), to_quarters(w_up)], axis=2)
    fw = 2 * ff
    cos, sin = rope_tables(rows)
    bias = jnp.where(doc_len[0, 0] > 0, 0.0, MASKED).astype(F32).reshape(1, 1) + jnp.zeros((8, 128), F32)
    (wqkv, wo, wgu, wd, x_own, og_all, pick, ga, gm, gqk, q, k, v, p, xn, att, nm, middle) = linked(
        functools.partial(forward_body, n, cap),
        (shape(n, 4, rq, width), shape(n, ro, width), shape(n, 4, rq, fw), shape(n, rd, width), shape(tok, width), shape(4, tok, width),
         shape(tok, slabs), shape(8, width, dtype=F32), shape(8, width, dtype=F32), shape(8, 128, dtype=F32),
         shape(rows, 512), shape(rows, 256), shape(rows, 256), shape(rows, 768, dtype=F32), shape(rows, width), shape(rows, 512),
         shape(4, tok, width), shape(tok, width, dtype=F32)),
        [pltpu.VMEM((slabs, width), BF), pltpu.VMEM((n * 8, 128), jnp.int32), pltpu.VMEM((4, 8, 128), F32), pltpu.VMEM((n, 8, 128), F32),
         pltpu.VMEM((4, tok, width), BF), pltpu.VMEM((4, tok, width), BF), pltpu.VMEM((3, tok, width), BF), pltpu.VMEM((QB, QB), F32),
         Gather.scratch(n, 2), Gather.scratch(n, 1), Gather.scratch(n, 2), sem_pairs(n), sem_pairs(n), sem_pairs(3), sem_pairs(3),
         sem_pairs(1), sem_pairs(1), sem_pairs(3), sem_pairs(3), sem_pairs(3), sem_pairs(3), sem_pairs(3)],
        "forward", 0,
    )(outgoing, labels, qkv, w_out, gu, w_down, gain_block, out_grad, cos, sin, bias)
    og_rows = og_all.reshape(rows, width)
    nm = nm.reshape(rows, width)
    wgu, wd = wgu.reshape(width, fw), wd.reshape(ff, width)
    wg, wu = wgu[:, :ff], wgu[:, ff:]
    gate, up = dot(nm, wg), dot(nm, wu)
    s = jax.nn.sigmoid(gate)
    silu = gate * s
    hidden = (silu * up).astype(BF)
    out_part = dot(hidden, wd).astype(BF)
    dh = dot_nt(og_rows, wd)
    d_gate = (dh * up * s * (1.0 + gate * (1.0 - s))).astype(BF)
    d_up = (dh * silu).astype(BF)
    gwd = dot_tn(hidden, og_rows).astype(BF)
    gwgu = jnp.concatenate([dot_tn(nm, d_gate), dot_tn(nm, d_up)], axis=1).astype(BF)
    dnm_part = (dot_nt(d_gate, wg) + dot_nt(d_up, wu)).astype(BF)
    blocks = ([((4, rq, fw), BF), ((rd, width), BF)], [((ro, width), BF)], [((4, rq, 1024), BF), ((8, 128), F32)])
    reduces = []
    for red, lines, sems in (Reduce.scratch(n, b) for b in blocks):
        reduces += [*red, *lines, sems]
    input_grad, layer_output, g_qkv, g_o, g_gu, g_d, small = linked(
        functools.partial(backward_body, n, cap),
        (shape(tok, width), shape(tok, width), shape(4, rq, 1024), shape(ro, width), shape(4, rq, fw), shape(rd, width), shape(8, 128, dtype=F32)),
        [pltpu.VMEM((3, tok, width), BF), pltpu.VMEM((3, tok, width), BF), pltpu.VMEM((3, tok, width), BF), pltpu.VMEM((4, tok, width), BF),
         pltpu.VMEM((tok, width), F32), pltpu.VMEM((QB, QB), F32), pltpu.VMEM((rows, 512), BF), pltpu.VMEM((rows, 512), F32),
         pltpu.VMEM((rows, 256), F32), pltpu.VMEM((rows, 256), F32), pltpu.VMEM((rows, 1024), BF),
         pltpu.VMEM((8, HD), F32), pltpu.VMEM((8, HD), F32), pltpu.VMEM((1, width), F32),
         pltpu.VMEM((n, 4, rq, 1024), BF), pltpu.VMEM((n, ro, width), BF), pltpu.VMEM((n, 8, 128), F32),
         pltpu.VMEM((slabs, width), BF), pltpu.VMEM((slabs, width), BF), *reduces,
         pltpu.VMEM((4, rq, fw), BF), pltpu.VMEM((rd, width), BF), pltpu.VMEM((4, rq, 1024), BF), pltpu.VMEM((ro, width), BF),
         pltpu.VMEM((8, 128), F32), pltpu.VMEM((4, 8, 128), F32),
         sem_pairs(3), sem_pairs(3), sem_pairs(3), sem_pairs(3), sem_pairs(n), sem_pairs(3), sem_pairs(1), sem_pairs(3), sem_pairs(1), sem_pairs(3)],
        "backward", 1,
    )(dnm_part.reshape(4, tok, width), out_part.reshape(4, tok, width), middle, x_own, out_grad, ga, gm, gqk,
      gwgu.reshape(n, 4, rq, fw), gwd.reshape(n, rd, width), wo, wqkv, q, k, v, p, xn, att, pick, place, cos, sin, bias)

    def own_lanes(row, count):
        return lax.dynamic_slice(small[row], ((index * count) % 128,), (count,))

    g_qkv, g_gu = g_qkv.astype(F32), g_gu.astype(F32)
    return (
        layer_output,
        input_grad,
        own_lanes(0, g_rows),
        from_quarters(g_qkv[:, :, :512]),
        from_quarters(g_qkv[:, :, 512:768]),
        from_quarters(g_qkv[:, :, 768:]),
        own_lanes(2, g_heads),
        own_lanes(3, g_heads),
        g_o.astype(F32),
        own_lanes(1, g_rows),
        from_quarters(g_gu[:, :, :ff]),
        from_quarters(g_gu[:, :, ff:]),
        g_d.astype(F32),
    )


def solution(mesh):
    rows = P(BOTH, None)
    vec = P(BOTH)
    return jax.shard_map(
        local,
        mesh=mesh,
        in_specs=(rows, vec, P("dp", None), rows, vec, rows, rows, rows, vec, vec, rows, vec, rows, rows, rows),
        out_specs=(rows, rows, vec, rows, rows, rows, vec, vec, rows, vec, rows, rows, rows),
        check_vma=False,
    )
```

```python
import functools
import math

import jax
import jax.numpy as jnp
import numpy as np
from jax import lax
from jax.experimental import pallas as pl
from jax.experimental.pallas import tpu as pltpu
from jax.sharding import PartitionSpec as P

H = 16
KVH = 8
HD = 128
EPS = 1e-06
THETA = 1000000.0
MASKED = -1e30
QB = 128
SCALE = HD ** (-0.5)
LOG2E = math.log2(math.e)
BF = jnp.bfloat16
F32 = jnp.float32
BOTH = ("dp", "ctx")
VMEM_LIMIT = 62 << 20


def dot(a, b):
    return lax.dot_general(a, b, (((1,), (0,)), ((), ())), preferred_element_type=F32)


def dot_nt(a, b):
    return lax.dot_general(a, b, (((1,), (1,)), ((), ())), preferred_element_type=F32)


def dot_tn(a, b):
    return lax.dot_general(a, b, (((0,), (0,)), ((), ())), preferred_element_type=F32)


def lanes(start, size):
    return pl.ds(pl.multiple_of(start * size, size), size)


def rope_tables(rows):
    inverse = np.exp(np.arange(HD // 2, dtype=np.float32) * np.float32(-2.0 / HD * math.log(THETA)))
    doubled = np.concatenate([inverse, inverse]).astype(np.float32)
    angles = np.arange(rows, dtype=np.float32)[:, None] * doubled[None, :]
    sign = np.where(np.arange(HD) < HD // 2, -1.0, 1.0).astype(np.float32)
    return np.cos(angles), np.sin(angles) * sign[None, :]


def mask_block(off_bias):
    rows = lax.broadcasted_iota(jnp.int32, (QB, QB), 0)
    cols = lax.broadcasted_iota(jnp.int32, (QB, QB), 1)
    return jnp.where(rows == cols, 0.0, jnp.where(cols < rows, off_bias, MASKED))


def lane_mean(v):
    ones = jnp.full((HD, HD), 1.0 / HD, BF)
    high = v.astype(BF)
    return dot(high, ones) + dot((v - high.astype(F32)).astype(BF), ones)


def rows_of(ref):
    value = ref[...]
    return value.reshape(-1, value.shape[-1])


def attn_project(x_ref, w, ga, gq, gk, cos_ref, sin_ref, q_ref, k_ref, v_ref, p_ref, xn_ref):
    rows = xn_ref.shape[0]
    tok = x_ref.shape[1]
    nq = q_ref.shape[1] // HD
    nk = k_ref.shape[1] // HD

    @pl.loop(0, rows // tok)
    def _(i):
        here = lanes(i, tok)
        x = x_ref[i].astype(F32)
        r = lax.rsqrt(jnp.mean(x * x, axis=-1, keepdims=True) + EPS)
        xn = (x * r * ga[0:1, :]).astype(BF)
        xn_ref[here, :] = xn
        p = dot(xn, rows_of(w))
        p_ref[here, :] = p[:, : (nq + nk) * HD].astype(BF)
        v_ref[here, :] = p[:, (nq + nk) * HD :].astype(BF)
        cos = cos_ref[here, :]
        sin = sin_ref[here, :]
        for h in range(nq + nk):
            ph = p[:, h * HD : (h + 1) * HD]
            g = gq if h < nq else gk
            nv = ph * lax.rsqrt(lane_mean(ph * ph) + EPS) * g
            rot = (nv * cos + pltpu.roll(nv, HD // 2, 1) * sin).astype(BF)
            if h < nq:
                q_ref[here, h * HD : (h + 1) * HD] = rot
            else:
                k_ref[here, (h - nq) * HD : (h - nq + 1) * HD] = rot


def group_rows(ref, here, g, group):
    return jnp.concatenate([ref[here, lanes(g * group + a, HD)] for a in range(group)], axis=0)


def attn_probs(q, k, off, mask_ref, group):
    s = dot_nt(q, k) * (SCALE * LOG2E)
    cut = s.shape[1] - QB
    last = jnp.exp2(s[:, cut:] + jnp.concatenate([mask_ref[...]] * group, axis=0))
    e = last if cut == 0 else jnp.concatenate([jnp.exp2(s[:, :cut] + off), last], axis=1)
    return e * (1.0 / jnp.sum(e, axis=-1, keepdims=True))


def attn_group(g, off, q_ref, k_ref, v_ref, att_ref, mask_ref):
    group = q_ref.shape[1] // k_ref.shape[1]
    hk = lanes(g, HD)
    for i in range(q_ref.shape[0] // QB):
        here, keys = slice(i * QB, (i + 1) * QB), slice(0, (i + 1) * QB)
        probs = attn_probs(group_rows(q_ref, here, g, group), k_ref[keys, hk], off, mask_ref, group)
        o = dot(probs.astype(BF), v_ref[keys, hk]).astype(BF)
        for a in range(group):
            att_ref[here, lanes(g * group + a, HD)] = o[a * QB : (a + 1) * QB]


def attn_group_back(g, i, off, q_ref, k_ref, v_ref, att_ref, da_ref, dq_ref, dk_ref, dv_ref, mask_ref):
    group = q_ref.shape[1] // k_ref.shape[1]
    hk = lanes(g, HD)
    here, keys = slice(i * QB, (i + 1) * QB), slice(0, (i + 1) * QB)
    q, da, att = (group_rows(ref, here, g, group) for ref in (q_ref, da_ref, att_ref))
    inner = jnp.sum(da.astype(F32) * att.astype(F32), axis=-1, keepdims=True)
    probs = attn_probs(q, k_ref[keys, hk], off, mask_ref, group)
    ds = (probs * (dot_nt(da, v_ref[keys, hk]) - inner)).astype(BF)
    dq = dot(ds, k_ref[keys, hk])
    for a in range(group):
        dq_ref[here, lanes(g * group + a, HD)] = dq[a * QB : (a + 1) * QB]
    dk_ref[keys, hk] += dot_tn(ds, q)
    dv_ref[keys, hk] += dot_tn(probs.astype(BF), da)


def attn_unproject(gq, gk, cos_ref, sin_ref, p_ref, dq_ref, dk_ref, dv_ref, dp_ref, w, dxn_ref, ggq_ref, ggk_ref):
    rows = p_ref.shape[0]
    tok = dxn_ref.shape[1]
    nq = dq_ref.shape[1] // HD
    nk = dk_ref.shape[1] // HD
    ggq_ref[...] = jnp.zeros_like(ggq_ref)
    ggk_ref[...] = jnp.zeros_like(ggk_ref)

    @pl.loop(0, rows // tok)
    def _(i):
        here = lanes(i, tok)
        cos = cos_ref[here, :]
        sin = sin_ref[here, :]
        sums = [jnp.zeros((1, HD), F32), jnp.zeros((1, HD), F32)]
        for h in range(nq + nk):
            which = 0 if h < nq else 1
            g = gq if h < nq else gk
            cols = slice(h * HD, (h + 1) * HD)
            if h < nq:
                d = dq_ref[here, cols] * SCALE
            else:
                d = dk_ref[here, (h - nq) * HD : (h - nq + 1) * HD] * SCALE
            dn = d * cos + pltpu.roll(d * sin, HD // 2, 1)
            ph = p_ref[here, cols].astype(F32)
            r = lax.rsqrt(lane_mean(ph * ph) + EPS)
            nh = ph * r
            dnh = dn * nh
            sums[which] += jnp.sum(dnh, axis=0, keepdims=True)
            dp_ref[here, cols] = (r * (dn * g - nh * lane_mean(dnh * g))).astype(BF)
        dp_ref[here, (nq + nk) * HD :] = dv_ref[here, :].astype(BF)
        ggq_ref[0:1, :] += sums[0]
        ggk_ref[0:1, :] += sums[1]
        dxn_ref[i] = dot_nt(dp_ref[here, :], rows_of(w)).astype(BF)


def feed_forward(nm_ref, og_ref, wgu_ref, wd_ref, hid_ref, dgu_ref, out_ref, dnm_ref):
    rows = nm_ref.shape[1]
    ff = hid_ref.shape[1]

    @pl.loop(0, nm_ref.shape[0])
    def _(i):
        here = lanes(i, rows)
        both = dot(nm_ref[i], rows_of(wgu_ref))
        gate, up = both[:, :ff], both[:, ff:]
        s = 1.0 / (1.0 + jnp.exp2(gate * -LOG2E))
        silu = gate * s
        hidden = (silu * up).astype(BF)
        hid_ref[here, :] = hidden
        dh = dot_nt(og_ref[i], rows_of(wd_ref))
        dgu_ref[here, :ff] = (dh * up * (s * (1.0 + gate * (1.0 - s)))).astype(BF)
        dgu_ref[here, ff:] = (dh * silu).astype(BF)
        dnm_ref[i] = dot_nt(dgu_ref[here, :], rows_of(wgu_ref)).astype(BF)
        out_ref[i] = dot(hidden, rows_of(wd_ref)).astype(BF)


def weight_grad(out_ref, left_ref, right, chunk=256):
    size = math.prod(out_ref.shape[1:-1])
    width = out_ref.shape[-1]

    @pl.loop(0, left_ref.shape[-1] // chunk)
    def _(i):
        left = left_ref[..., lanes(i, chunk)].reshape(-1, chunk)
        g = dot_tn(left, rows_of(right)).astype(BF)
        for j in range(chunk // size):
            out_ref[i * (chunk // size) + j] = g[j * size : (j + 1) * size].reshape(out_ref.shape[1:-1] + (width,))


MESH = pl.DeviceIdType.MESH


def rcopy(src, dst, send, recv, **device):
    return pltpu.make_async_remote_copy(
        src_ref=src, dst_ref=dst, send_sem=send, recv_sem=recv, device_id=device, device_id_type=MESH
    )


class Place:
    def __init__(self, n):
        self.n, self.line = n, n // 2
        self.dp, self.ctx = lax.axis_index("dp"), lax.axis_index("ctx")
        self.outer, self.inner = self.dp // 2, self.dp % 2
        self.dp_inner = self.outer * 2 + 1 - self.inner
        self.dp_up, self.dp_down = self.dp + 2, self.dp - 2
        self.has_up, self.has_down = self.outer < self.line - 1, self.outer > 0
        core = self.ctx % 2
        self.c_core = self.ctx + 1 - 2 * core
        self.c_x = (self.ctx + 2) % 4
        self.c_far = 3 - self.ctx
        mine = self.dp * 4 + self.ctx
        self.slab_to = {"dp": mine % n, "ctx": mine // n}
        source = self.ctx * n + self.dp
        self.slab_from = {"dp": source // 4, "ctx": source % 4}
        self.slab_stays = source == mine


def greet(place, slabs):
    barrier = pltpu.get_barrier_semaphore()

    def signal(**device):
        pl.semaphore_signal(barrier, inc=1, device_id=device, device_id_type=MESH)

    for c in (place.c_core, place.c_x, place.c_far):
        signal(ctx=c)
    for k in range(1, place.n):
        signal(dp=(place.dp + k) % place.n)
    count = place.n + 2
    for slab in slabs:

        @pl.when(jnp.logical_not(place.slab_stays))
        def _():
            signal(**slab)

        count = count + jnp.where(place.slab_stays, 0, 1)
    pl.semaphore_wait(barrier, count)


class Gather:
    def __init__(self, place, bufs, sems):
        self.at, self.bufs, self.sems = place, bufs, sems

    @staticmethod
    def scratch(n, bufs):
        return pltpu.SemaphoreType.DMA((5, bufs, n // 2))

    def copy(self, b, p, way):
        at = self.at
        block = self.bufs[b].at[p * 2 + at.inner]
        device = (at.dp_up, at.dp_down, at.dp_inner)[way]
        recv = self.sems.at[4 if way == 2 else 3, b, p]
        return rcopy(block, block, self.sems.at[way, b, p], recv, dp=device)

    def send(self, p, up, down, inner=True):
        at = self.at
        for b in range(len(self.bufs)):
            if up:

                @pl.when(at.has_up)
                def _():
                    self.copy(b, p, 0).start()

            if down:

                @pl.when(at.has_down)
                def _():
                    self.copy(b, p, 1).start()

            if inner:
                self.copy(b, p, 2).start()

    def start(self):
        self.send(self.at.outer, True, True)

    def start_inner(self):
        self.send(self.at.outer, False, False)

    def start_line(self):
        self.send(self.at.outer, True, True, False)

    def step(self, t):
        at = self.at
        for p, there, up in ((at.outer - t, at.outer >= t, True), (at.outer + t, at.outer + t < at.line, False)):

            @pl.when(there)
            def _():
                for b in range(len(self.bufs)):
                    self.copy(b, p, 0).wait_recv()
                self.send(p, up, not up)

    def arrive(self):
        at = self.at
        for b in range(len(self.bufs)):
            for p in range(at.line):
                block = self.bufs[b].at[p * 2 + 1 - at.inner]
                rcopy(block, block, self.sems.at[2, b, p], self.sems.at[4, b, p], dp=at.dp_inner).wait_recv()

    def finish(self):
        at = self.at
        for b in range(len(self.bufs)):
            for p in range(at.line):
                self.copy(b, p, 2).wait_send()

                @pl.when(jnp.logical_and(at.has_up, p <= at.outer))
                def _():
                    self.copy(b, p, 0).wait_send()

                @pl.when(jnp.logical_and(at.has_down, p >= at.outer))
                def _():
                    self.copy(b, p, 1).wait_send()


class Reduce:
    def __init__(self, place, parts, from_inner, from_line, sems):
        self.at, self.parts, self.from_inner, self.from_line, self.sems = place, parts, from_inner, from_line, sems

    @staticmethod
    def scratch(n, blocks):
        line = n // 2
        return (
            [pltpu.VMEM((line, *dims), dtype) for dims, dtype in blocks],
            [pltpu.VMEM((line + 1, *dims), dtype) for dims, dtype in blocks],
            pltpu.SemaphoreType.DMA((4, len(blocks), line + 1)),
        )

    def inner_copy(self, b, p):
        at = self.at
        return rcopy(
            self.parts[b].at[p * 2 + 1 - at.inner], self.from_inner[b].at[p],
            self.sems.at[0, b, p], self.sems.at[1, b, p], dp=at.dp_inner,
        )

    def line_copy(self, b, p, slot, up):
        at = self.at
        return rcopy(
            self.from_inner[b].at[p], self.from_line[b].at[slot],
            self.sems.at[2, b, p], self.sems.at[3, b, slot], dp=at.dp_up if up else at.dp_down,
        )

    def start(self, which):
        at = self.at
        for d in range(at.line - 1, -1, -1):
            for p, there in ((at.outer + d, at.outer + d < at.line), (at.outer - d, at.outer >= d))[: 2 if d else 1]:

                @pl.when(there)
                def _():
                    for b in which:
                        self.inner_copy(b, p).start()

    def total(self, b, p, slots):
        s = self.parts[b][p * 2 + self.at.inner].astype(F32) + self.from_inner[b][p].astype(F32)
        for slot in slots:
            s = s + self.from_line[b][slot].astype(F32)
        return s

    def step(self, d, which):
        at = self.at
        for p, there, more, up in (
            (at.outer + d, at.outer + d < at.line, at.has_down, True),
            (at.outer - d, at.outer >= d, at.has_up, False),
        ):
            for b in which:

                @pl.when(there)
                def _():
                    self.inner_copy(b, p).wait_recv()
                    into = self.from_inner[b].at[p]

                    @pl.when(more)
                    def _():
                        self.line_copy(b, p, p, up).wait_recv()
                        into[...] = self.total(b, p, [p]).astype(into.dtype)

                    @pl.when(jnp.logical_not(more))
                    def _():
                        into[...] = self.total(b, p, []).astype(into.dtype)

                    slot = p if up or d > 1 else at.line
                    self.line_copy(b, p, slot, up).start()

    def result(self, b, store):
        at = self.at
        p = at.outer
        self.inner_copy(b, p).wait_recv()
        lo, hi = at.has_down, at.has_up

        @pl.when(lo)
        def _():
            self.line_copy(b, p, p, True).wait_recv()

        @pl.when(hi)
        def _():
            self.line_copy(b, p, at.line, False).wait_recv()

        @pl.when(jnp.logical_and(lo, hi))
        def _():
            store(self.total(b, p, [p, at.line]))

        @pl.when(jnp.logical_and(lo, jnp.logical_not(hi)))
        def _():
            store(self.total(b, p, [p]))

        @pl.when(jnp.logical_and(hi, jnp.logical_not(lo)))
        def _():
            store(self.total(b, p, [at.line]))

    def finish(self):
        at = self.at
        for b in range(len(self.parts)):
            for p in range(at.line):
                self.inner_copy(b, p).wait_send()

                @pl.when(p != at.outer)
                def _():
                    self.line_copy(b, p, p, True).wait_send()


class CtxGather:
    def __init__(self, place, buf, sems):
        self.at, self.buf, self.sems = place, buf, sems

    def copy(self, k, owner):
        block = self.buf.at[owner]
        ctx = self.at.c_x if k == 1 else self.at.c_core
        return rcopy(block, block, self.sems.at[0, k], self.sems.at[1, k], ctx=ctx)

    def start(self):
        self.copy(1, self.at.ctx).start()
        self.copy(0, self.at.ctx).start()

    def forward(self):
        self.copy(1, self.at.c_x).wait_recv()
        self.copy(2, self.at.c_x).start()

    def arrive(self):
        self.copy(0, self.at.c_core).wait_recv()
        self.copy(2, self.at.c_far).wait_recv()

    def finish(self):
        for k in range(3):
            self.copy(k, self.at.ctx).wait_send()


class CtxReduce:
    def __init__(self, place, part, got, sems):
        self.at, self.part, self.got, self.sems = place, part, got, sems

    def copy(self, k):
        at = self.at
        block = self.got.at[1] if k == 2 else self.part.at[(at.c_core, at.c_far)[k]]
        return rcopy(block, self.got.at[k], self.sems.at[0, k], self.sems.at[1, k], ctx=at.c_x if k == 2 else at.c_core)

    def start(self):
        self.copy(1).start()
        self.copy(0).start()

    def across(self):
        self.copy(1).wait_recv()
        into = self.got.at[1]
        into[...] = (self.part[self.at.c_x].astype(F32) + into[...].astype(F32)).astype(into.dtype)
        self.copy(2).start()

    def result(self):
        self.copy(0).wait_recv()
        self.copy(2).wait_recv()
        return self.part[self.at.ctx].astype(F32) + self.got[0].astype(F32) + self.got[2].astype(F32)

    def finish(self):
        for k in range(3):
            self.copy(k).wait_send()


class Quarters:
    def __init__(self, place, src, dst, sems):
        self.at, self.src, self.dst, self.sems = place, src, dst, sems

    def copies(self):
        at = self.at
        return [
            rcopy(self.src.at[c], self.dst.at[at.ctx], self.sems.at[0, k], self.sems.at[1, k], ctx=c)
            for k, c in enumerate((at.c_x, at.c_far, at.c_core))
        ]

    def start(self):
        for c in self.copies():
            c.start()
        self.dst[self.at.ctx] = self.src[self.at.ctx]

    def finish(self):
        for c in self.copies():
            c.wait()


class Slab:
    def __init__(self, place, src, dst, sems, to):
        self.at, self.src, self.dst, self.sems, self.to = place, src, dst, sems, to

    def copy(self):
        return rcopy(self.src, self.dst, self.sems.at[0, 0], self.sems.at[1, 0], **self.to)

    def start(self):
        @pl.when(self.at.slab_stays)
        def _():
            self.dst[...] = self.src[...]

        @pl.when(jnp.logical_not(self.at.slab_stays))
        def _():
            self.copy().start()

    def finish(self):
        @pl.when(jnp.logical_not(self.at.slab_stays))
        def _():
            self.copy().wait()


class Exchange:
    def __init__(self, place, src, dst, cap, sems):
        self.at, self.src, self.dst, self.cap, self.sems = place, src, dst, cap, sems

    def rows(self, ref, j):
        return ref.at[pl.ds(pl.multiple_of(j * self.cap, self.cap), self.cap)]

    def copy(self, k):
        at = self.at
        to = (at.dp + k) % at.n
        return rcopy(self.rows(self.src, to), self.rows(self.dst, at.dp), self.sems.at[0, k], self.sems.at[1, k], dp=to)

    def start(self):
        for k in range(1, self.at.n):
            self.copy(k).start()
        self.rows(self.dst, self.at.dp)[...] = self.rows(self.src, self.at.dp)[...]

    def finish(self):
        for k in range(1, self.at.n):
            self.copy(k).wait()


def sem_pairs(count):
    return pltpu.SemaphoreType.DMA((2, count))


def norm_back(c, v, gain):
    r = lax.rsqrt(jnp.mean(v * v, axis=-1, keepdims=True) + EPS)
    nv = v * r
    cg = c * gain
    return jnp.sum(c * nv, axis=0, keepdims=True), r * (cg - nv * jnp.mean(cg * nv, axis=-1, keepdims=True))


def into(ref):
    def store(v):
        ref[...] = v.astype(ref.dtype)

    return store


def layer_body(
    n, cap,
    out_ref, lab_ref, qkv_ref, wo_src, gu_ref, wd_src, gain_ref, og_ref, place_ref, cos_ref, sin_ref, bias_ref,
    ig_ref, layer_ref, qkv_out, o_out, gu_out, gd_out, gain_out,
    wqkv_ref, wo_ref, wgu_ref, wd_ref, og_all, x_own, pick_ref, ga_ref, gm_ref, q_ref, k_ref, v_ref, p_ref, xn_ref, att_ref, nm_ref, mid_ref,
    recv, labels, gains_c, gains_n, x_ref, part_ref, got, mask_ref,
    hid_ref, dgu_ref, outp_ref, got_d, got_o, dmid_ref, dq_ref, dk_ref, dv_ref, ggq_ref, ggk_ref, ggm_ref, gains, recv_back,
    yi0, yi1, ln0, ln1, s_ra, yo, lo, s_rb, yq, yg, lq, lg, s_rc,
    gain_sum, gain_all,
    s_ga, s_gb, s_gc, s_rows, s_labs, s_qkv, s_gu, s_wo, s_wd, s_gain, s_x, s_og, s_red, s_nm,
    s_dnm, s_out, s_db, s_dxn, s_rows_back, s_gu_back, s_gd, s_qkv_back, s_o, s_gain_back,
):
    at = Place(n)
    greet(at, (at.slab_from, at.slab_to))
    qkv = Quarters(at, qkv_ref, wqkv_ref.at[at.dp], s_qkv)
    rows = Exchange(at, out_ref, recv, cap, s_rows)
    labs = Exchange(at, lab_ref, labels, 8, s_labs)
    qkv.start()
    gain_copies = [
        rcopy(gain_ref, gains_c.at[at.ctx], s_gain.at[0, k], s_gain.at[1, k], ctx=c)
        for k, c in enumerate((at.c_x, at.c_far, at.c_core))
    ]
    for g in gain_copies:
        g.start()
    gains_c[at.ctx] = gain_ref[...]
    wo = Slab(at, wo_src, wo_ref.at[at.slab_to["dp"]], s_wo, at.slab_to)
    wd = Slab(at, wd_src, wd_ref.at[at.slab_to["dp"]], s_wd, at.slab_to)
    gu = Quarters(at, gu_ref, wgu_ref.at[at.dp], s_gu)
    labs.start()
    rows.start()
    gu.start()
    wo.start()
    wd.start()
    for g in gain_copies:
        g.wait()
    gains_n[at.dp] = gains_c[0] + gains_c[1] + gains_c[2] + gains_c[3]
    qkv.finish()
    first = Gather(at, [wqkv_ref, gains_n], s_ga)
    first.start()
    og_all[at.ctx] = og_ref[...]
    og = CtxGather(at, og_all, s_og)
    gu.finish()
    og.start()
    wo.finish()
    second = Gather(at, [wo_ref], s_gb)
    second.start()
    wd.finish()
    third = Gather(at, [wgu_ref, wd_ref], s_gc)
    third.start_inner()
    labs.finish()
    tok = x_ref.shape[1]
    slots = lax.broadcasted_iota(jnp.int32, (tok, cap), 0)
    for j in range(n):
        pick_ref[:, j * cap : (j + 1) * cap] = (slots == labels[j * 8 : j * 8 + 1, :cap]).astype(BF)
    first.step(1)
    second.step(1)
    rows.finish()
    owned = dot(pick_ref[...], recv[...]).astype(BF)
    x_ref[at.ctx] = owned
    x_own[...] = owned
    x = CtxGather(at, x_ref, s_x)
    x.start()
    for t in range(2, at.line):
        first.step(t)
        second.step(t)
        if t == 2:
            third.start_line()
    og.forward()
    x.forward()
    first.arrive()
    own = 4 * ga_ref.shape[1] // (4 * n)
    ga_ref[...] = jnp.zeros_like(ga_ref)
    gm_ref[...] = jnp.zeros_like(gm_ref)
    gqk = jnp.zeros((8, 128), F32)
    for d in range(n):
        tile = slice(d * own // 128 * 128, d * own // 128 * 128 + 128)
        block = gains_n[d]
        ga_ref[0:1, tile] += block[0:1]
        gm_ref[0:1, tile] += block[1:2]
        gqk = gqk + block
    off = bias_ref[0:1, 0:1]
    mask_ref[...] = mask_block(off)
    x.arrive()
    attn_project(x_ref, wqkv_ref, ga_ref, gqk[2:3], gqk[3:4], cos_ref, sin_ref, q_ref, k_ref, v_ref, p_ref, xn_ref)
    third.step(1)
    nk = k_ref.shape[1] // HD

    @pl.loop(0, nk)
    def _(g):
        attn_group(g, off, q_ref, k_ref, v_ref, att_ref, mask_ref)

    third.step(2)
    second.arrive()

    @pl.loop(0, 4)
    def _(i):
        part_ref[i] = dot(att_ref[lanes(i, tok), :], rows_of(wo_ref)).astype(BF)

    red = CtxReduce(at, part_ref, got, s_red)
    red.start()
    red.across()
    middle = x_own[...].astype(F32) + red.result()
    mid_ref[...] = middle
    r = lax.rsqrt(jnp.mean(middle * middle, axis=-1, keepdims=True) + EPS)
    nm_ref[at.ctx] = (middle * r * gm_ref[0:1, :]).astype(BF)
    nm = CtxGather(at, nm_ref, s_nm)
    nm.start()
    for t in range(3, at.line):
        third.step(t)
    nm.forward()
    nm.arrive()
    og.arrive()
    third.arrive()
    for part in (first, second, third, og, x, nm, red):
        part.finish()
    feed_forward(nm_ref, og_all, wgu_ref, wd_ref, hid_ref, dgu_ref, outp_ref, part_ref)
    db_ref, da_ref, dp_ref = x_ref, hid_ref.at[:, : q_ref.shape[1]], dgu_ref.at[:, : wqkv_ref.shape[-1]]
    dnm = CtxReduce(at, part_ref, got_d, s_dnm)
    dnm.start()
    weight_grad(wd_ref, hid_ref, og_all, 384)
    first = Reduce(at, [wgu_ref, wd_ref], [yi0, yi1], [ln0, ln1], s_ra)
    first.start([1])
    dnm.across()
    weight_grad(wgu_ref, nm_ref, dgu_ref)
    first.start([0])
    out = CtxReduce(at, outp_ref, got_o, s_out)
    dk_ref[...] = jnp.zeros_like(dk_ref)
    dv_ref[...] = jnp.zeros_like(dv_ref)
    first.step(at.line - 1, [0, 1])
    gg, d = norm_back(dnm.result(), mid_ref[...], gm_ref[0:1, :])
    ggm_ref[...] = gg
    d = d + og_ref[...].astype(F32)
    dmid_ref[...] = d
    db_ref[at.ctx] = d.astype(BF)
    db = CtxGather(at, db_ref, s_db)
    db.start()
    out.start()
    for t in range(at.line - 2, 1, -1):
        first.step(t, [0, 1])
    db.forward()
    out.across()
    db.arrive()
    tok = db_ref.shape[1]

    @pl.loop(0, 4)
    def _(i):
        da_ref[lanes(i, tok), :] = dot_nt(db_ref[i], rows_of(wo_ref)).astype(BF)

    weight_grad(wo_ref, att_ref, db_ref)
    first.step(1, [0, 1])
    second = Reduce(at, [wo_ref], [yo], [lo], s_rb)
    second.start([0])
    for g in range(k_ref.shape[1] // HD):
        for i in range(q_ref.shape[0] // QB):
            attn_group_back(g, i, off, q_ref, k_ref, v_ref, att_ref, da_ref, dq_ref, dk_ref, dv_ref, mask_ref)
        if g == 0:
            first.result(0, into(yi0.at[at.outer]))
            first.result(1, into(yi1.at[at.outer]))
            gu = Quarters(at, yi0.at[at.outer], gu_out, s_gu_back)
            gd = Slab(at, yi1.at[at.outer], gd_out, s_gd, at.slab_from)
            gu.start()
            gd.start()
            for t in range(at.line - 1, 1, -1):
                second.step(t, [0])
    second.step(1, [0])
    layer_ref[...] = (mid_ref[...] + out.result()).astype(BF)
    second.result(0, into(yo.at[at.outer]))
    o = Slab(at, yo.at[at.outer], o_out, s_o, at.slab_from)
    o.start()
    db.finish()
    dxn_ref = nm_ref
    attn_unproject(gqk[2:3], gqk[3:4], cos_ref, sin_ref, p_ref, dq_ref, dk_ref, dv_ref, dp_ref, wqkv_ref, dxn_ref, ggq_ref, ggk_ref)
    dxn = CtxReduce(at, dxn_ref, got, s_dxn)
    dxn.start()
    weight_grad(wqkv_ref, xn_ref, dp_ref)
    third = Reduce(at, [wqkv_ref, gains], [yq, yg], [lq, lg], s_rc)
    third.start([0])
    dxn.across()
    third.step(at.line - 1, [0])
    gg, d = norm_back(dxn.result(), x_own[...].astype(F32), ga_ref[0:1, :])
    owned = (dmid_ref[...] + d).astype(BF)
    recv[...] = dot_tn(pick_ref[...], owned).astype(BF)
    rows = Exchange(at, recv, recv_back, cap, s_rows_back)
    rows.start()
    own = 4 * gg.shape[1] // (4 * n)
    lines = lax.broadcasted_iota(jnp.int32, (8, 128), 0)
    for j in range(n):
        tile = slice(j * own // 128 * 128, j * own // 128 * 128 + 128)
        gains[j] = (
            jnp.where(lines == 0, gg[:, tile], 0.0) + jnp.where(lines == 1, ggm_ref[0:1, tile], 0.0)
            + jnp.where(lines == 2, ggq_ref[0:1, :], 0.0) + jnp.where(lines == 3, ggk_ref[0:1, :], 0.0)
        )
    third.start([1])
    third.step(at.line - 1, [1])
    for t in range(at.line - 2, 0, -1):
        third.step(t, [0, 1])
    third.result(0, into(yq.at[at.outer]))
    qkv = Quarters(at, yq.at[at.outer], qkv_out, s_qkv_back)
    qkv.start()
    third.result(1, into(gain_sum))
    small = [
        rcopy(gain_sum, gain_all.at[at.ctx], s_gain_back.at[0, k], s_gain_back.at[1, k], ctx=c)
        for k, c in enumerate((at.c_x, at.c_far, at.c_core))
    ]
    for g in small:
        g.start()
    gain_all[at.ctx] = gain_sum[...]
    rows.finish()
    ig_ref[...] = dot(place_ref[...], recv_back[...]).astype(BF)
    for g in small:
        g.wait()
    gain_out[...] = gain_all[0] + gain_all[1] + gain_all[2] + gain_all[3]
    for part in (qkv, o, gu, gd, dxn, out, dnm, first, second, third):
        part.finish()


def shape(*dims, dtype=BF):
    return jax.ShapeDtypeStruct(dims, dtype)


def linked(body, outs, scratch, name, number):
    return pl.pallas_call(
        body,
        out_shape=outs,
        scratch_shapes=scratch,
        compiler_params=pltpu.CompilerParams(vmem_limit_bytes=VMEM_LIMIT, collective_id=number, has_side_effects=True),
        name=name,
    )


def to_quarters(weight):
    rows, cols = weight.shape
    return weight.reshape(rows, 4, cols // 4).transpose(1, 0, 2)


def from_quarters(blocks):
    n, rows, cols = blocks.shape
    return blocks.transpose(1, 0, 2).reshape(rows, n * cols)


def local(
    layer_input, dest_slot, doc_len, out_grad, attn_gain, w_query, w_key, w_value, q_gain, k_gain,
    w_out, mlp_gain, w_gate, w_up, w_down,
):
    tok, width = layer_input.shape
    n = lax.axis_size("dp")
    cap = 2 * tok // n
    rows = 4 * tok
    slabs = n * cap
    rq, ro, rd = w_query.shape[0], w_out.shape[0], w_down.shape[0]
    ff = rd * n
    owner = dest_slot // (4 * tok)
    slot = dest_slot % tok
    hot = (owner[:, None] == jnp.arange(n, dtype=jnp.int32)[None, :]).astype(BF)
    lower = (jnp.arange(tok)[:, None] > jnp.arange(tok)[None, :]).astype(BF)
    rank = jnp.sum(dot(lower, hot) * hot.astype(F32), axis=1).astype(jnp.int32)
    send_slot = owner * cap + rank
    place = send_slot[:, None] == jnp.arange(slabs, dtype=jnp.int32)[None, :]
    labels = jnp.sum(jnp.where(place, slot[:, None] - tok, 0), axis=0, dtype=jnp.int32) + tok
    place = place.astype(BF)
    outgoing = dot_tn(place, layer_input).astype(BF)
    labels = jnp.broadcast_to(jnp.pad(labels.reshape(n, 1, cap), ((0, 0), (0, 0), (0, 128 - cap))), (n, 8, 128)).reshape(n * 8, 128)
    index = lax.axis_index("dp") * 4 + lax.axis_index("ctx")
    g_rows, g_heads = attn_gain.shape[0], q_gain.shape[0]

    def at_lane(values):
        start = (index * values.shape[0]) % 128
        return lax.dynamic_update_slice(jnp.zeros((128,), F32), values.astype(F32), (start,))

    gain_block = jnp.stack([at_lane(attn_gain), at_lane(mlp_gain), at_lane(q_gain), at_lane(k_gain)])
    gain_block = jnp.pad(gain_block, ((0, 4), (0, 0)))
    qkv = jnp.concatenate([to_quarters(w_query), to_quarters(w_key), to_quarters(w_value)], axis=2)
    gu = jnp.concatenate([to_quarters(w_gate), to_quarters(w_up)], axis=2)
    fw = 2 * ff
    cos, sin = rope_tables(rows)
    bias = jnp.where(doc_len[0, 0] > 0, 0.0, MASKED).astype(F32).reshape(1, 1) + jnp.zeros((8, 128), F32)
    blocks = ([((4, rq, fw), BF), ((rd, width), BF)], [((ro, width), BF)], [((4, rq, 1024), BF), ((8, 128), F32)])
    reduces = []
    for red, lines, sems in (Reduce.scratch(n, b) for b in blocks):
        reduces += [*red, *lines, sems]
    vm = pltpu.VMEM
    group = (4, tok, width)
    input_grad, layer_output, g_qkv, g_o, g_gu, g_d, small = linked(
        functools.partial(layer_body, n, cap),
        (shape(tok, width), shape(tok, width), shape(4, rq, 1024), shape(ro, width), shape(4, rq, fw), shape(rd, width), shape(8, 128, dtype=F32)),
        [vm((n, 4, rq, 1024), BF), vm((n, ro, width), BF), vm((n, 4, rq, fw), BF), vm((n, rd, width), BF), vm(group, BF), vm((tok, width), BF),
         vm((tok, slabs), BF), vm((8, width), F32), vm((8, width), F32), vm((rows, 512), BF), vm((rows, 256), BF), vm((rows, 256), BF),
         vm((rows, 768), BF), vm((rows, width), BF), vm((rows, 512), BF), vm(group, BF), vm((tok, width), F32),
         vm((slabs, width), BF), vm((n * 8, 128), jnp.int32), vm((4, 8, 128), F32), vm((n, 8, 128), F32),
         vm(group, BF), vm(group, BF), vm((3, tok, width), BF), vm((QB, QB), F32),
         vm((rows, ff), BF), vm((rows, fw), BF), vm(group, BF), vm((3, tok, width), BF), vm((3, tok, width), BF),
         vm((tok, width), F32), vm((rows, 512), F32), vm((rows, 256), F32), vm((rows, 256), F32),
         vm((8, HD), F32), vm((8, HD), F32), vm((1, width), F32), vm((n, 8, 128), F32), vm((slabs, width), BF),
         *reduces,
         vm((8, 128), F32), vm((4, 8, 128), F32),
         Gather.scratch(n, 2), Gather.scratch(n, 1), Gather.scratch(n, 2), sem_pairs(n), sem_pairs(n), sem_pairs(3), sem_pairs(3),
         sem_pairs(1), sem_pairs(1), sem_pairs(3), sem_pairs(3), sem_pairs(3), sem_pairs(3), sem_pairs(3),
         sem_pairs(3), sem_pairs(3), sem_pairs(3), sem_pairs(3), sem_pairs(n), sem_pairs(3), sem_pairs(1), sem_pairs(3), sem_pairs(1), sem_pairs(3)],
        "layer", 0,
    )(outgoing, labels, qkv, w_out, gu, w_down, gain_block, out_grad, place, cos, sin, bias)

    def own_lanes(row, count):
        return lax.dynamic_slice(small[row], ((index * count) % 128,), (count,))

    g_qkv, g_gu = g_qkv.astype(F32), g_gu.astype(F32)
    return (
        layer_output,
        input_grad,
        own_lanes(0, g_rows),
        from_quarters(g_qkv[:, :, :512]),
        from_quarters(g_qkv[:, :, 512:768]),
        from_quarters(g_qkv[:, :, 768:]),
        own_lanes(2, g_heads),
        own_lanes(3, g_heads),
        g_o.astype(F32),
        own_lanes(1, g_rows),
        from_quarters(g_gu[:, :, :ff]),
        from_quarters(g_gu[:, :, ff:]),
        g_d.astype(F32),
    )


def solution(mesh):
    rows = P(BOTH, None)
    vec = P(BOTH)
    return jax.shard_map(
        local,
        mesh=mesh,
        in_specs=(rows, vec, P("dp", None), rows, vec, rows, rows, rows, vec, vec, rows, vec, rows, rows, rows),
        out_specs=(rows, rows, vec, rows, rows, rows, vec, vec, rows, vec, rows, rows, rows),
        check_vma=False,
    )
```

```python
import functools
import math

import jax
import jax.numpy as jnp
import numpy as np
from jax import lax
from jax.experimental import pallas as pl
from jax.experimental.pallas import tpu as pltpu
from jax.sharding import PartitionSpec as P

H = 16
KVH = 8
HD = 128
EPS = 1e-06
THETA = 1000000.0
MASKED = -1e30
QB = 128
SCALE = HD ** (-0.5)
LOG2E = math.log2(math.e)
BF = jnp.bfloat16
F32 = jnp.float32
BOTH = ("dp", "ctx")
VMEM_LIMIT = 62 << 20


def dot(a, b):
    return lax.dot_general(a, b, (((1,), (0,)), ((), ())), preferred_element_type=F32)


def dot_nt(a, b):
    return lax.dot_general(a, b, (((1,), (1,)), ((), ())), preferred_element_type=F32)


def dot_tn(a, b):
    return lax.dot_general(a, b, (((0,), (0,)), ((), ())), preferred_element_type=F32)


def lanes(start, size):
    return pl.ds(pl.multiple_of(start * size, size), size)


def rope_tables(rows):
    inverse = np.exp(np.arange(HD // 2, dtype=np.float32) * np.float32(-2.0 / HD * math.log(THETA)))
    doubled = np.concatenate([inverse, inverse]).astype(np.float32)
    angles = np.arange(rows, dtype=np.float32)[:, None] * doubled[None, :]
    sign = np.where(np.arange(HD) < HD // 2, -1.0, 1.0).astype(np.float32)
    return np.cos(angles), np.sin(angles) * sign[None, :]


def mask_block(off_bias):
    rows = lax.broadcasted_iota(jnp.int32, (QB, QB), 0)
    cols = lax.broadcasted_iota(jnp.int32, (QB, QB), 1)
    return jnp.where(rows == cols, 0.0, jnp.where(cols < rows, off_bias, MASKED))


def lane_mean(v):
    ones = jnp.full((HD, HD), 1.0 / HD, BF)
    high = v.astype(BF)
    return dot(high, ones) + dot((v - high.astype(F32)).astype(BF), ones)


def rows_of(ref):
    value = ref[...]
    return value.reshape(-1, value.shape[-1])


def attn_project(x_ref, w, ga, gq, gk, cos_ref, sin_ref, q_ref, k_ref, v_ref, p_ref, xn_ref):
    rows = xn_ref.shape[0]
    tok = x_ref.shape[1]
    nq = q_ref.shape[1] // HD
    nk = k_ref.shape[1] // HD

    @pl.loop(0, rows // tok)
    def _(i):
        here = lanes(i, tok)
        x = x_ref[i].astype(F32)
        r = lax.rsqrt(jnp.mean(x * x, axis=-1, keepdims=True) + EPS)
        xn = (x * r * ga[0:1, :]).astype(BF)
        xn_ref[here, :] = xn
        p = dot(xn, rows_of(w))
        p_ref[here, :] = p[:, : (nq + nk) * HD].astype(BF)
        v_ref[here, :] = p[:, (nq + nk) * HD :].astype(BF)
        cos = cos_ref[here, :]
        sin = sin_ref[here, :]
        for h in range(nq + nk):
            ph = p[:, h * HD : (h + 1) * HD]
            g = gq if h < nq else gk
            nv = ph * lax.rsqrt(lane_mean(ph * ph) + EPS) * g
            rot = (nv * cos + pltpu.roll(nv, HD // 2, 1) * sin).astype(BF)
            if h < nq:
                q_ref[here, h * HD : (h + 1) * HD] = rot
            else:
                k_ref[here, (h - nq) * HD : (h - nq + 1) * HD] = rot


def group_rows(ref, here, g, group):
    return jnp.concatenate([ref[here, lanes(g * group + a, HD)] for a in range(group)], axis=0)


def attn_probs(q, k, off, mask_ref, group):
    s = dot_nt(q, k) * (SCALE * LOG2E)
    cut = s.shape[1] - QB
    last = jnp.exp2(s[:, cut:] + jnp.concatenate([mask_ref[...]] * group, axis=0))
    e = last if cut == 0 else jnp.concatenate([jnp.exp2(s[:, :cut] + off), last], axis=1)
    return e * (1.0 / jnp.sum(e, axis=-1, keepdims=True))


def attn_group(g, off, q_ref, k_ref, v_ref, att_ref, mask_ref):
    group = q_ref.shape[1] // k_ref.shape[1]
    hk = lanes(g, HD)
    for i in range(q_ref.shape[0] // QB):
        here, keys = slice(i * QB, (i + 1) * QB), slice(0, (i + 1) * QB)
        probs = attn_probs(group_rows(q_ref, here, g, group), k_ref[keys, hk], off, mask_ref, group)
        o = dot(probs.astype(BF), v_ref[keys, hk]).astype(BF)
        for a in range(group):
            att_ref[here, lanes(g * group + a, HD)] = o[a * QB : (a + 1) * QB]


def attn_group_back(g, i, off, q_ref, k_ref, v_ref, att_ref, da_ref, dq_ref, dk_ref, dv_ref, mask_ref):
    group = q_ref.shape[1] // k_ref.shape[1]
    hk = lanes(g, HD)
    here, keys = slice(i * QB, (i + 1) * QB), slice(0, (i + 1) * QB)
    q, da, att = (group_rows(ref, here, g, group) for ref in (q_ref, da_ref, att_ref))
    inner = jnp.sum(da.astype(F32) * att.astype(F32), axis=-1, keepdims=True)
    probs = attn_probs(q, k_ref[keys, hk], off, mask_ref, group)
    ds = (probs * (dot_nt(da, v_ref[keys, hk]) - inner)).astype(BF)
    dq = dot(ds, k_ref[keys, hk])
    for a in range(group):
        dq_ref[here, lanes(g * group + a, HD)] = dq[a * QB : (a + 1) * QB]
    dk_ref[keys, hk] += dot_tn(ds, q)
    dv_ref[keys, hk] += dot_tn(probs.astype(BF), da)


def attn_unproject(gq, gk, cos_ref, sin_ref, p_ref, dq_ref, dk_ref, dv_ref, dp_ref, w, dxn_ref, ggq_ref, ggk_ref):
    rows = p_ref.shape[0]
    tok = dxn_ref.shape[1]
    nq = dq_ref.shape[1] // HD
    nk = dk_ref.shape[1] // HD
    ggq_ref[...] = jnp.zeros_like(ggq_ref)
    ggk_ref[...] = jnp.zeros_like(ggk_ref)

    @pl.loop(0, rows // tok)
    def _(i):
        here = lanes(i, tok)
        cos = cos_ref[here, :]
        sin = sin_ref[here, :]
        sums = [jnp.zeros((1, HD), F32), jnp.zeros((1, HD), F32)]
        for h in range(nq + nk):
            which = 0 if h < nq else 1
            g = gq if h < nq else gk
            cols = slice(h * HD, (h + 1) * HD)
            if h < nq:
                d = dq_ref[here, cols] * SCALE
            else:
                d = dk_ref[here, (h - nq) * HD : (h - nq + 1) * HD] * SCALE
            dn = d * cos + pltpu.roll(d * sin, HD // 2, 1)
            ph = p_ref[here, cols].astype(F32)
            r = lax.rsqrt(lane_mean(ph * ph) + EPS)
            nh = ph * r
            dnh = dn * nh
            sums[which] += jnp.sum(dnh, axis=0, keepdims=True)
            dp_ref[here, cols] = (r * (dn * g - nh * lane_mean(dnh * g))).astype(BF)
        dp_ref[here, (nq + nk) * HD :] = dv_ref[here, :].astype(BF)
        ggq_ref[0:1, :] += sums[0]
        ggk_ref[0:1, :] += sums[1]
        dxn_ref[i] = dot_nt(dp_ref[here, :], rows_of(w)).astype(BF)


def feed_forward(nm_ref, og_ref, wgu_ref, wd_ref, hid_ref, dgu_ref, out_ref, dnm_ref):
    rows = nm_ref.shape[1]
    ff = hid_ref.shape[1]

    @pl.loop(0, nm_ref.shape[0])
    def _(i):
        here = lanes(i, rows)
        both = dot(nm_ref[i], rows_of(wgu_ref))
        gate, up = both[:, :ff], both[:, ff:]
        s = 1.0 / (1.0 + jnp.exp2(gate * -LOG2E))
        silu = gate * s
        hidden = (silu * up).astype(BF)
        hid_ref[here, :] = hidden
        dh = dot_nt(og_ref[i], rows_of(wd_ref))
        dgu_ref[here, :ff] = (dh * up * (s * (1.0 + gate * (1.0 - s)))).astype(BF)
        dgu_ref[here, ff:] = (dh * silu).astype(BF)
        dnm_ref[i] = dot_nt(dgu_ref[here, :], rows_of(wgu_ref)).astype(BF)
        out_ref[i] = dot(hidden, rows_of(wd_ref)).astype(BF)


def weight_grad(out_ref, left_ref, right, chunk=256):
    size = math.prod(out_ref.shape[1:-1])
    width = out_ref.shape[-1]

    @pl.loop(0, left_ref.shape[-1] // chunk)
    def _(i):
        left = left_ref[..., lanes(i, chunk)].reshape(-1, chunk)
        g = dot_tn(left, rows_of(right)).astype(BF)
        for j in range(chunk // size):
            out_ref[i * (chunk // size) + j] = g[j * size : (j + 1) * size].reshape(out_ref.shape[1:-1] + (width,))


MESH = pl.DeviceIdType.MESH


def rcopy(src, dst, send, recv, **device):
    return pltpu.make_async_remote_copy(
        src_ref=src, dst_ref=dst, send_sem=send, recv_sem=recv, device_id=device, device_id_type=MESH
    )


class Place:
    def __init__(self, n):
        self.n, self.line = n, n // 2
        self.dp, self.ctx = lax.axis_index("dp"), lax.axis_index("ctx")
        self.outer, self.inner = self.dp // 2, self.dp % 2
        self.dp_inner = self.outer * 2 + 1 - self.inner
        self.dp_up, self.dp_down = self.dp + 2, self.dp - 2
        self.has_up, self.has_down = self.outer < self.line - 1, self.outer > 0
        core = self.ctx % 2
        self.c_core = self.ctx + 1 - 2 * core
        self.c_x = (self.ctx + 2) % 4
        self.c_far = 3 - self.ctx
        mine = self.dp * 4 + self.ctx
        self.slab_to = {"dp": mine % n, "ctx": mine // n}
        source = self.ctx * n + self.dp
        self.slab_from = {"dp": source // 4, "ctx": source % 4}
        self.slab_stays = source == mine


def greet(place, slabs):
    barrier = pltpu.get_barrier_semaphore()

    def signal(**device):
        pl.semaphore_signal(barrier, inc=1, device_id=device, device_id_type=MESH)

    for c in (place.c_core, place.c_x, place.c_far):
        signal(ctx=c)
    for k in range(1, place.n):
        signal(dp=(place.dp + k) % place.n)
    count = place.n + 2
    for slab in slabs:

        @pl.when(jnp.logical_not(place.slab_stays))
        def _():
            signal(**slab)

        count = count + jnp.where(place.slab_stays, 0, 1)
    pl.semaphore_wait(barrier, count)


class Gather:
    def __init__(self, place, bufs, sems):
        self.at, self.bufs, self.sems = place, bufs, sems

    @staticmethod
    def scratch(n, bufs):
        return pltpu.SemaphoreType.DMA((5, bufs, n // 2))

    def copy(self, b, p, way):
        at = self.at
        block = self.bufs[b].at[p * 2 + at.inner]
        device = (at.dp_up, at.dp_down, at.dp_inner)[way]
        recv = self.sems.at[4 if way == 2 else 3, b, p]
        return rcopy(block, block, self.sems.at[way, b, p], recv, dp=device)

    def send(self, p, up, down, inner=True):
        at = self.at
        for b in range(len(self.bufs)):
            if up:

                @pl.when(at.has_up)
                def _():
                    self.copy(b, p, 0).start()

            if down:

                @pl.when(at.has_down)
                def _():
                    self.copy(b, p, 1).start()

            if inner:
                self.copy(b, p, 2).start()

    def start(self):
        self.send(self.at.outer, True, True)

    def start_inner(self):
        self.send(self.at.outer, False, False)

    def start_line(self):
        self.send(self.at.outer, True, True, False)

    def step(self, t):
        at = self.at
        for p, there, up in ((at.outer - t, at.outer >= t, True), (at.outer + t, at.outer + t < at.line, False)):

            @pl.when(there)
            def _():
                for b in range(len(self.bufs)):
                    self.copy(b, p, 0).wait_recv()
                self.send(p, up, not up)

    def arrive(self):
        at = self.at
        for b in range(len(self.bufs)):
            for p in range(at.line):
                block = self.bufs[b].at[p * 2 + 1 - at.inner]
                rcopy(block, block, self.sems.at[2, b, p], self.sems.at[4, b, p], dp=at.dp_inner).wait_recv()

    def finish(self):
        at = self.at
        for b in range(len(self.bufs)):
            for p in range(at.line):
                self.copy(b, p, 2).wait_send()

                @pl.when(jnp.logical_and(at.has_up, p <= at.outer))
                def _():
                    self.copy(b, p, 0).wait_send()

                @pl.when(jnp.logical_and(at.has_down, p >= at.outer))
                def _():
                    self.copy(b, p, 1).wait_send()


class Reduce:
    def __init__(self, place, parts, from_inner, from_line, sems):
        self.at, self.parts, self.from_inner, self.from_line, self.sems = place, parts, from_inner, from_line, sems

    @staticmethod
    def scratch(n, blocks):
        line = n // 2
        return (
            [pltpu.VMEM((line, *dims), dtype) for dims, dtype in blocks],
            [pltpu.VMEM((line + 1, *dims), dtype) for dims, dtype in blocks],
            pltpu.SemaphoreType.DMA((4, len(blocks), line + 1)),
        )

    def inner_copy(self, b, p):
        at = self.at
        return rcopy(
            self.parts[b].at[p * 2 + 1 - at.inner], self.from_inner[b].at[p],
            self.sems.at[0, b, p], self.sems.at[1, b, p], dp=at.dp_inner,
        )

    def line_copy(self, b, p, slot, up):
        at = self.at
        return rcopy(
            self.from_inner[b].at[p], self.from_line[b].at[slot],
            self.sems.at[2, b, p], self.sems.at[3, b, slot], dp=at.dp_up if up else at.dp_down,
        )

    def start(self, which):
        at = self.at
        for d in range(at.line - 1, -1, -1):
            for p, there in ((at.outer + d, at.outer + d < at.line), (at.outer - d, at.outer >= d))[: 2 if d else 1]:

                @pl.when(there)
                def _():
                    for b in which:
                        self.inner_copy(b, p).start()

    def total(self, b, p, slots):
        s = self.parts[b][p * 2 + self.at.inner].astype(F32) + self.from_inner[b][p].astype(F32)
        for slot in slots:
            s = s + self.from_line[b][slot].astype(F32)
        return s

    def step(self, d, which):
        at = self.at
        for p, there, more, up in (
            (at.outer + d, at.outer + d < at.line, at.has_down, True),
            (at.outer - d, at.outer >= d, at.has_up, False),
        ):
            for b in which:

                @pl.when(there)
                def _():
                    self.inner_copy(b, p).wait_recv()
                    into = self.from_inner[b].at[p]

                    @pl.when(more)
                    def _():
                        self.line_copy(b, p, p, up).wait_recv()
                        into[...] = self.total(b, p, [p]).astype(into.dtype)

                    @pl.when(jnp.logical_not(more))
                    def _():
                        into[...] = self.total(b, p, []).astype(into.dtype)

                    slot = p if up or d > 1 else at.line
                    self.line_copy(b, p, slot, up).start()

    def result(self, b, store):
        at = self.at
        p = at.outer
        self.inner_copy(b, p).wait_recv()
        lo, hi = at.has_down, at.has_up

        @pl.when(lo)
        def _():
            self.line_copy(b, p, p, True).wait_recv()

        @pl.when(hi)
        def _():
            self.line_copy(b, p, at.line, False).wait_recv()

        @pl.when(jnp.logical_and(lo, hi))
        def _():
            store(self.total(b, p, [p, at.line]))

        @pl.when(jnp.logical_and(lo, jnp.logical_not(hi)))
        def _():
            store(self.total(b, p, [p]))

        @pl.when(jnp.logical_and(hi, jnp.logical_not(lo)))
        def _():
            store(self.total(b, p, [at.line]))

    def finish(self):
        at = self.at
        for b in range(len(self.parts)):
            for p in range(at.line):
                self.inner_copy(b, p).wait_send()

                @pl.when(p != at.outer)
                def _():
                    self.line_copy(b, p, p, True).wait_send()


class CtxGather:
    def __init__(self, place, buf, sems):
        self.at, self.buf, self.sems = place, buf, sems

    def copy(self, k, owner):
        block = self.buf.at[owner]
        ctx = self.at.c_x if k == 1 else self.at.c_core
        return rcopy(block, block, self.sems.at[0, k], self.sems.at[1, k], ctx=ctx)

    def start(self):
        self.copy(1, self.at.ctx).start()
        self.copy(0, self.at.ctx).start()

    def forward(self):
        self.copy(1, self.at.c_x).wait_recv()
        self.copy(2, self.at.c_x).start()

    def arrive(self):
        self.copy(0, self.at.c_core).wait_recv()
        self.copy(2, self.at.c_far).wait_recv()

    def finish(self):
        for k in range(3):
            self.copy(k, self.at.ctx).wait_send()


class CtxReduce:
    def __init__(self, place, part, got, sems):
        self.at, self.part, self.got, self.sems = place, part, got, sems

    def copy(self, k):
        at = self.at
        block = self.got.at[1] if k == 2 else self.part.at[(at.c_core, at.c_far)[k]]
        return rcopy(block, self.got.at[k], self.sems.at[0, k], self.sems.at[1, k], ctx=at.c_x if k == 2 else at.c_core)

    def start(self):
        self.copy(1).start()
        self.copy(0).start()

    def across(self):
        self.copy(1).wait_recv()
        into = self.got.at[1]
        into[...] = (self.part[self.at.c_x].astype(F32) + into[...].astype(F32)).astype(into.dtype)
        self.copy(2).start()

    def result(self):
        self.copy(0).wait_recv()
        self.copy(2).wait_recv()
        return self.part[self.at.ctx].astype(F32) + self.got[0].astype(F32) + self.got[2].astype(F32)

    def finish(self):
        for k in range(3):
            self.copy(k).wait_send()


class Quarters:
    def __init__(self, place, src, dst, sems):
        self.at, self.src, self.dst, self.sems = place, src, dst, sems

    def copies(self):
        at = self.at
        return [
            rcopy(self.src.at[c], self.dst.at[at.ctx], self.sems.at[0, k], self.sems.at[1, k], ctx=c)
            for k, c in enumerate((at.c_x, at.c_far, at.c_core))
        ]

    def start(self):
        for c in self.copies():
            c.start()
        self.dst[self.at.ctx] = self.src[self.at.ctx]

    def finish(self):
        for c in self.copies():
            c.wait()


class Slab:
    def __init__(self, place, src, dst, sems, to):
        self.at, self.src, self.dst, self.sems, self.to = place, src, dst, sems, to

    def copy(self):
        return rcopy(self.src, self.dst, self.sems.at[0, 0], self.sems.at[1, 0], **self.to)

    def start(self):
        @pl.when(self.at.slab_stays)
        def _():
            self.dst[...] = self.src[...]

        @pl.when(jnp.logical_not(self.at.slab_stays))
        def _():
            self.copy().start()

    def finish(self):
        @pl.when(jnp.logical_not(self.at.slab_stays))
        def _():
            self.copy().wait()


class Exchange:
    def __init__(self, place, src, dst, cap, sems):
        self.at, self.src, self.dst, self.cap, self.sems = place, src, dst, cap, sems

    def rows(self, ref, j):
        return ref.at[pl.ds(pl.multiple_of(j * self.cap, self.cap), self.cap)]

    def copy(self, k):
        at = self.at
        to = (at.dp + k) % at.n
        return rcopy(self.rows(self.src, to), self.rows(self.dst, at.dp), self.sems.at[0, k], self.sems.at[1, k], dp=to)

    def start(self):
        for k in range(1, self.at.n):
            self.copy(k).start()
        self.rows(self.dst, self.at.dp)[...] = self.rows(self.src, self.at.dp)[...]

    def finish(self):
        for k in range(1, self.at.n):
            self.copy(k).wait()


def sem_pairs(count):
    return pltpu.SemaphoreType.DMA((2, count))


def norm_back(c, v, gain):
    r = lax.rsqrt(jnp.mean(v * v, axis=-1, keepdims=True) + EPS)
    nv = v * r
    cg = c * gain
    return jnp.sum(c * nv, axis=0, keepdims=True), r * (cg - nv * jnp.mean(cg * nv, axis=-1, keepdims=True))


def into(ref):
    def store(v):
        ref[...] = v.astype(ref.dtype)

    return store


def layer_body(
    n, cap,
    out_ref, lab_ref, qkv_ref, wo_src, gu_ref, wd_src, gain_ref, og_ref, place_ref, cos_ref, sin_ref, bias_ref,
    ig_ref, layer_ref, qkv_out, o_out, gu_out, gd_out, gain_out,
    wqkv_ref, wo_ref, wgu_ref, wd_ref, og_all, x_own, pick_ref, ga_ref, gm_ref, q_ref, k_ref, v_ref, p_ref, xn_ref, att_ref, nm_ref, mid_ref,
    recv, labels, gains_c, gains_n, x_ref, part_ref, got, mask_ref,
    hid_ref, dgu_ref, outp_ref, got_d, got_o, dmid_ref, dq_ref, dk_ref, dv_ref, ggq_ref, ggk_ref, ggm_ref, gains, recv_back,
    yi0, yi1, ln0, ln1, s_ra, yo, lo, s_rb, yq, yg, lq, lg, s_rc,
    gain_sum, gain_all,
    s_ga, s_gb, s_gc, s_gd4, s_rows, s_labs, s_qkv, s_gu, s_wo, s_wd, s_gain, s_x, s_og, s_red, s_nm,
    s_dnm, s_out, s_db, s_dxn, s_rows_back, s_gu_back, s_gd, s_qkv_back, s_o, s_gain_back,
):
    at = Place(n)
    greet(at, (at.slab_from, at.slab_to))
    qkv = Quarters(at, qkv_ref, wqkv_ref.at[at.dp], s_qkv)
    rows = Exchange(at, out_ref, recv, cap, s_rows)
    labs = Exchange(at, lab_ref, labels, 8, s_labs)
    qkv.start()
    gain_copies = [
        rcopy(gain_ref, gains_c.at[at.ctx], s_gain.at[0, k], s_gain.at[1, k], ctx=c)
        for k, c in enumerate((at.c_x, at.c_far, at.c_core))
    ]
    for g in gain_copies:
        g.start()
    gains_c[at.ctx] = gain_ref[...]
    wo = Slab(at, wo_src, wo_ref.at[at.slab_to["dp"]], s_wo, at.slab_to)
    wd = Slab(at, wd_src, wd_ref.at[at.slab_to["dp"]], s_wd, at.slab_to)
    gu = Quarters(at, gu_ref, wgu_ref.at[at.dp], s_gu)
    labs.start()
    rows.start()
    gu.start()
    wo.start()
    wd.start()
    for g in gain_copies:
        g.wait()
    gains_n[at.dp] = gains_c[0] + gains_c[1] + gains_c[2] + gains_c[3]
    qkv.finish()
    first = Gather(at, [wqkv_ref, gains_n], s_ga)
    first.start()
    og_all[at.ctx] = og_ref[...]
    og = CtxGather(at, og_all, s_og)
    gu.finish()
    og.start()
    third = Gather(at, [wgu_ref], s_gc)
    third.start_inner()
    labs.finish()
    tok = x_ref.shape[1]
    slots = lax.broadcasted_iota(jnp.int32, (tok, cap), 0)
    for j in range(n):
        pick_ref[:, j * cap : (j + 1) * cap] = (slots == labels[j * 8 : j * 8 + 1, :cap]).astype(BF)
    first.step(1)
    rows.finish()
    owned = dot(pick_ref[...], recv[...]).astype(BF)
    x_ref[at.ctx] = owned
    x_own[...] = owned
    x = CtxGather(at, x_ref, s_x)
    x.start()
    first.step(2)
    third.start_line()
    wo.finish()
    second = Gather(at, [wo_ref], s_gb)
    second.start()
    for t in range(3, at.line):
        first.step(t)
    second.step(1)
    og.forward()
    x.forward()
    first.arrive()
    own = 4 * ga_ref.shape[1] // (4 * n)
    ga_ref[...] = jnp.zeros_like(ga_ref)
    gm_ref[...] = jnp.zeros_like(gm_ref)
    gqk = jnp.zeros((8, 128), F32)
    for d in range(n):
        tile = slice(d * own // 128 * 128, d * own // 128 * 128 + 128)
        block = gains_n[d]
        ga_ref[0:1, tile] += block[0:1]
        gm_ref[0:1, tile] += block[1:2]
        gqk = gqk + block
    off = bias_ref[0:1, 0:1]
    mask_ref[...] = mask_block(off)
    x.arrive()
    second.step(2)
    attn_project(x_ref, wqkv_ref, ga_ref, gqk[2:3], gqk[3:4], cos_ref, sin_ref, q_ref, k_ref, v_ref, p_ref, xn_ref)
    for t in range(3, at.line):
        second.step(t)
    third.step(1)
    wd.finish()
    fourth = Gather(at, [wd_ref], s_gd4)
    fourth.start()
    nk = k_ref.shape[1] // HD

    @pl.loop(0, nk)
    def _(g):
        attn_group(g, off, q_ref, k_ref, v_ref, att_ref, mask_ref)

    third.step(2)
    fourth.step(1)
    second.arrive()

    @pl.loop(0, 4)
    def _(i):
        part_ref[i] = dot(att_ref[lanes(i, tok), :], rows_of(wo_ref)).astype(BF)

    red = CtxReduce(at, part_ref, got, s_red)
    red.start()
    red.across()
    for t in range(3, at.line):
        third.step(t)
        fourth.step(t - 1)
    middle = x_own[...].astype(F32) + red.result()
    mid_ref[...] = middle
    r = lax.rsqrt(jnp.mean(middle * middle, axis=-1, keepdims=True) + EPS)
    nm_ref[at.ctx] = (middle * r * gm_ref[0:1, :]).astype(BF)
    nm = CtxGather(at, nm_ref, s_nm)
    nm.start()
    fourth.step(at.line - 1)
    nm.forward()
    nm.arrive()
    og.arrive()
    third.arrive()
    fourth.arrive()
    for part in (first, second, third, fourth, og, x, nm, red):
        part.finish()
    feed_forward(nm_ref, og_all, wgu_ref, wd_ref, hid_ref, dgu_ref, outp_ref, part_ref)
    db_ref, da_ref, dp_ref = x_ref, hid_ref.at[:, : q_ref.shape[1]], dgu_ref.at[:, : wqkv_ref.shape[-1]]
    last = at.line - 1
    dnm = CtxReduce(at, part_ref, got_d, s_dnm)
    dnm.start()
    weight_grad(wd_ref, hid_ref, og_all, 384)
    first = Reduce(at, [wgu_ref, wd_ref], [yi0, yi1], [ln0, ln1], s_ra)
    first.start([1])
    dnm.across()
    weight_grad(wgu_ref, nm_ref, dgu_ref)
    first.start([0])
    out = CtxReduce(at, outp_ref, got_o, s_out)
    dk_ref[...] = jnp.zeros_like(dk_ref)
    dv_ref[...] = jnp.zeros_like(dv_ref)
    first.step(last, [1])
    gg, d = norm_back(dnm.result(), mid_ref[...], gm_ref[0:1, :])
    ggm_ref[...] = gg
    d = d + og_ref[...].astype(F32)
    dmid_ref[...] = d
    db_ref[at.ctx] = d.astype(BF)
    db = CtxGather(at, db_ref, s_db)
    db.start()
    out.start()
    for t in range(last - 1, 0, -1):
        first.step(t, [1])
    db.forward()
    out.across()
    db.arrive()
    tok = db_ref.shape[1]

    @pl.loop(0, 4)
    def _(i):
        da_ref[lanes(i, tok), :] = dot_nt(db_ref[i], rows_of(wo_ref)).astype(BF)

    first.step(last, [0])
    for g in range(k_ref.shape[1] // HD):
        for i in range(q_ref.shape[0] // QB):
            attn_group_back(g, i, off, q_ref, k_ref, v_ref, att_ref, da_ref, dq_ref, dk_ref, dv_ref, mask_ref)
        if g == 0:
            for t in range(last - 1, 1, -1):
                first.step(t, [0])
    dxn_ref = nm_ref
    attn_unproject(gqk[2:3], gqk[3:4], cos_ref, sin_ref, p_ref, dq_ref, dk_ref, dv_ref, dp_ref, wqkv_ref, dxn_ref, ggq_ref, ggk_ref)
    dxn = CtxReduce(at, dxn_ref, got, s_dxn)
    dxn.start()
    first.step(1, [0])
    weight_grad(wqkv_ref, xn_ref, dp_ref)
    third = Reduce(at, [wqkv_ref, gains], [yq, yg], [lq, lg], s_rc)
    third.start([0])
    dxn.across()
    weight_grad(wo_ref, att_ref, db_ref)
    second = Reduce(at, [wo_ref], [yo], [lo], s_rb)
    second.start([0])
    first.result(1, into(yi1.at[at.outer]))
    gd = Slab(at, yi1.at[at.outer], gd_out, s_gd, at.slab_from)
    gd.start()
    first.result(0, into(yi0.at[at.outer]))
    gu = Quarters(at, yi0.at[at.outer], gu_out, s_gu_back)
    gu.start()
    third.step(last, [0])
    gg, d = norm_back(dxn.result(), x_own[...].astype(F32), ga_ref[0:1, :])
    owned = (dmid_ref[...] + d).astype(BF)
    recv[...] = dot_tn(pick_ref[...], owned).astype(BF)
    rows = Exchange(at, recv, recv_back, cap, s_rows_back)
    rows.start()
    own = 4 * gg.shape[1] // (4 * n)
    lines = lax.broadcasted_iota(jnp.int32, (8, 128), 0)
    for j in range(n):
        tile = slice(j * own // 128 * 128, j * own // 128 * 128 + 128)
        gains[j] = (
            jnp.where(lines == 0, gg[:, tile], 0.0) + jnp.where(lines == 1, ggm_ref[0:1, tile], 0.0)
            + jnp.where(lines == 2, ggq_ref[0:1, :], 0.0) + jnp.where(lines == 3, ggk_ref[0:1, :], 0.0)
        )
    third.start([1])
    second.step(last, [0])
    for t in range(last - 1, 0, -1):
        third.step(t, [0])
        second.step(t, [0])
    layer_ref[...] = (mid_ref[...] + out.result()).astype(BF)
    for t in range(last, 0, -1):
        third.step(t, [1])
    second.result(0, into(yo.at[at.outer]))
    o = Slab(at, yo.at[at.outer], o_out, s_o, at.slab_from)
    o.start()
    third.result(0, into(yq.at[at.outer]))
    qkv = Quarters(at, yq.at[at.outer], qkv_out, s_qkv_back)
    qkv.start()
    third.result(1, into(gain_sum))
    small = [
        rcopy(gain_sum, gain_all.at[at.ctx], s_gain_back.at[0, k], s_gain_back.at[1, k], ctx=c)
        for k, c in enumerate((at.c_x, at.c_far, at.c_core))
    ]
    for g in small:
        g.start()
    gain_all[at.ctx] = gain_sum[...]
    rows.finish()
    ig_ref[...] = dot(place_ref[...], recv_back[...]).astype(BF)
    for g in small:
        g.wait()
    gain_out[...] = gain_all[0] + gain_all[1] + gain_all[2] + gain_all[3]
    for part in (qkv, o, gu, gd, dxn, db, out, dnm, first, second, third):
        part.finish()


def shape(*dims, dtype=BF):
    return jax.ShapeDtypeStruct(dims, dtype)


def linked(body, outs, scratch, name, number):
    return pl.pallas_call(
        body,
        out_shape=outs,
        scratch_shapes=scratch,
        compiler_params=pltpu.CompilerParams(vmem_limit_bytes=VMEM_LIMIT, collective_id=number, has_side_effects=True),
        name=name,
    )


def to_quarters(weight):
    rows, cols = weight.shape
    return weight.reshape(rows, 4, cols // 4).transpose(1, 0, 2)


def from_quarters(blocks):
    n, rows, cols = blocks.shape
    return blocks.transpose(1, 0, 2).reshape(rows, n * cols)


def local(
    layer_input, dest_slot, doc_len, out_grad, attn_gain, w_query, w_key, w_value, q_gain, k_gain,
    w_out, mlp_gain, w_gate, w_up, w_down,
):
    tok, width = layer_input.shape
    n = lax.axis_size("dp")
    cap = 2 * tok // n
    rows = 4 * tok
    slabs = n * cap
    rq, ro, rd = w_query.shape[0], w_out.shape[0], w_down.shape[0]
    ff = rd * n
    owner = dest_slot // (4 * tok)
    slot = dest_slot % tok
    hot = (owner[:, None] == jnp.arange(n, dtype=jnp.int32)[None, :]).astype(BF)
    lower = (jnp.arange(tok)[:, None] > jnp.arange(tok)[None, :]).astype(BF)
    rank = jnp.sum(dot(lower, hot) * hot.astype(F32), axis=1).astype(jnp.int32)
    send_slot = owner * cap + rank
    place = send_slot[:, None] == jnp.arange(slabs, dtype=jnp.int32)[None, :]
    labels = jnp.sum(jnp.where(place, slot[:, None] - tok, 0), axis=0, dtype=jnp.int32) + tok
    place = place.astype(BF)
    outgoing = dot_tn(place, layer_input).astype(BF)
    labels = jnp.broadcast_to(jnp.pad(labels.reshape(n, 1, cap), ((0, 0), (0, 0), (0, 128 - cap))), (n, 8, 128)).reshape(n * 8, 128)
    index = lax.axis_index("dp") * 4 + lax.axis_index("ctx")
    g_rows, g_heads = attn_gain.shape[0], q_gain.shape[0]

    def at_lane(values):
        start = (index * values.shape[0]) % 128
        return lax.dynamic_update_slice(jnp.zeros((128,), F32), values.astype(F32), (start,))

    gain_block = jnp.stack([at_lane(attn_gain), at_lane(mlp_gain), at_lane(q_gain), at_lane(k_gain)])
    gain_block = jnp.pad(gain_block, ((0, 4), (0, 0)))
    qkv = jnp.concatenate([to_quarters(w_query), to_quarters(w_key), to_quarters(w_value)], axis=2)
    gu = jnp.concatenate([to_quarters(w_gate), to_quarters(w_up)], axis=2)
    fw = 2 * ff
    cos, sin = rope_tables(rows)
    bias = jnp.where(doc_len[0, 0] > 0, 0.0, MASKED).astype(F32).reshape(1, 1) + jnp.zeros((8, 128), F32)
    blocks = ([((4, rq, fw), BF), ((rd, width), BF)], [((ro, width), BF)], [((4, rq, 1024), BF), ((8, 128), F32)])
    reduces = []
    for red, lines, sems in (Reduce.scratch(n, b) for b in blocks):
        reduces += [*red, *lines, sems]
    vm = pltpu.VMEM
    group = (4, tok, width)
    input_grad, layer_output, g_qkv, g_o, g_gu, g_d, small = linked(
        functools.partial(layer_body, n, cap),
        (shape(tok, width), shape(tok, width), shape(4, rq, 1024), shape(ro, width), shape(4, rq, fw), shape(rd, width), shape(8, 128, dtype=F32)),
        [vm((n, 4, rq, 1024), BF), vm((n, ro, width), BF), vm((n, 4, rq, fw), BF), vm((n, rd, width), BF), vm(group, BF), vm((tok, width), BF),
         vm((tok, slabs), BF), vm((8, width), F32), vm((8, width), F32), vm((rows, 512), BF), vm((rows, 256), BF), vm((rows, 256), BF),
         vm((rows, 768), BF), vm((rows, width), BF), vm((rows, 512), BF), vm(group, BF), vm((tok, width), F32),
         vm((slabs, width), BF), vm((n * 8, 128), jnp.int32), vm((4, 8, 128), F32), vm((n, 8, 128), F32),
         vm(group, BF), vm(group, BF), vm((3, tok, width), BF), vm((QB, QB), F32),
         vm((rows, ff), BF), vm((rows, fw), BF), vm(group, BF), vm((3, tok, width), BF), vm((3, tok, width), BF),
         vm((tok, width), F32), vm((rows, 512), F32), vm((rows, 256), F32), vm((rows, 256), F32),
         vm((8, HD), F32), vm((8, HD), F32), vm((1, width), F32), vm((n, 8, 128), F32), vm((slabs, width), BF),
         *reduces,
         vm((8, 128), F32), vm((4, 8, 128), F32),
         Gather.scratch(n, 2), Gather.scratch(n, 1), Gather.scratch(n, 1), Gather.scratch(n, 1), sem_pairs(n), sem_pairs(n), sem_pairs(3), sem_pairs(3),
         sem_pairs(1), sem_pairs(1), sem_pairs(3), sem_pairs(3), sem_pairs(3), sem_pairs(3), sem_pairs(3),
         sem_pairs(3), sem_pairs(3), sem_pairs(3), sem_pairs(3), sem_pairs(n), sem_pairs(3), sem_pairs(1), sem_pairs(3), sem_pairs(1), sem_pairs(3)],
        "layer", 0,
    )(outgoing, labels, qkv, w_out, gu, w_down, gain_block, out_grad, place, cos, sin, bias)

    def own_lanes(row, count):
        return lax.dynamic_slice(small[row], ((index * count) % 128,), (count,))

    g_qkv, g_gu = g_qkv.astype(F32), g_gu.astype(F32)
    return (
        layer_output,
        input_grad,
        own_lanes(0, g_rows),
        from_quarters(g_qkv[:, :, :512]),
        from_quarters(g_qkv[:, :, 512:768]),
        from_quarters(g_qkv[:, :, 768:]),
        own_lanes(2, g_heads),
        own_lanes(3, g_heads),
        g_o.astype(F32),
        own_lanes(1, g_rows),
        from_quarters(g_gu[:, :, :ff]),
        from_quarters(g_gu[:, :, ff:]),
        g_d.astype(F32),
    )


def solution(mesh):
    rows = P(BOTH, None)
    vec = P(BOTH)
    return jax.shard_map(
        local,
        mesh=mesh,
        in_specs=(rows, vec, P("dp", None), rows, vec, rows, rows, rows, vec, vec, rows, vec, rows, rows, rows),
        out_specs=(rows, rows, vec, rows, rows, rows, vec, vec, rows, vec, rows, rows, rows),
        check_vma=False,
    )
```

```python
import functools
import math

import jax
import jax.numpy as jnp
import numpy as np
from jax import lax
from jax.experimental import pallas as pl
from jax.experimental.pallas import tpu as pltpu
from jax.sharding import PartitionSpec as P

H = 16
KVH = 8
HD = 128
EPS = 1e-06
THETA = 1000000.0
MASKED = -1e30
QB = 128
SCALE = HD ** (-0.5)
LOG2E = math.log2(math.e)
BF = jnp.bfloat16
F32 = jnp.float32
BOTH = ("dp", "ctx")
VMEM_LIMIT = 62 << 20


def dot(a, b):
    return lax.dot_general(a, b, (((1,), (0,)), ((), ())), preferred_element_type=F32)


def dot_nt(a, b):
    return lax.dot_general(a, b, (((1,), (1,)), ((), ())), preferred_element_type=F32)


def dot_tn(a, b):
    return lax.dot_general(a, b, (((0,), (0,)), ((), ())), preferred_element_type=F32)


def lanes(start, size):
    return pl.ds(pl.multiple_of(start * size, size), size)


def rope_tables(rows):
    inverse = np.exp(np.arange(HD // 2, dtype=np.float32) * np.float32(-2.0 / HD * math.log(THETA)))
    doubled = np.concatenate([inverse, inverse]).astype(np.float32)
    angles = np.arange(rows, dtype=np.float32)[:, None] * doubled[None, :]
    sign = np.where(np.arange(HD) < HD // 2, -1.0, 1.0).astype(np.float32)
    return np.cos(angles), np.sin(angles) * sign[None, :]


def mask_block(off_bias):
    rows = lax.broadcasted_iota(jnp.int32, (QB, QB), 0)
    cols = lax.broadcasted_iota(jnp.int32, (QB, QB), 1)
    return jnp.where(rows == cols, 0.0, jnp.where(cols < rows, off_bias, MASKED))


def lane_mean(v):
    ones = jnp.full((HD, HD), 1.0 / HD, BF)
    high = v.astype(BF)
    return dot(high, ones) + dot((v - high.astype(F32)).astype(BF), ones)


def rows_of(ref):
    value = ref[...]
    return value.reshape(-1, value.shape[-1])


def attn_project(x_ref, w, ga, gq, gk, cos_ref, sin_ref, q_ref, k_ref, v_ref, p_ref, xn_ref):
    rows = xn_ref.shape[0]
    tok = x_ref.shape[1]
    nq = q_ref.shape[1] // HD
    nk = k_ref.shape[1] // HD

    @pl.loop(0, rows // tok)
    def _(i):
        here = lanes(i, tok)
        x = x_ref[i].astype(F32)
        r = lax.rsqrt(jnp.mean(x * x, axis=-1, keepdims=True) + EPS)
        xn = (x * r * ga[0:1, :]).astype(BF)
        xn_ref[here, :] = xn
        p = dot(xn, rows_of(w))
        p_ref[here, :] = p[:, : (nq + nk) * HD].astype(BF)
        v_ref[here, :] = p[:, (nq + nk) * HD :].astype(BF)
        cos = cos_ref[here, :]
        sin = sin_ref[here, :]
        for h in range(nq + nk):
            ph = p[:, h * HD : (h + 1) * HD]
            g = gq if h < nq else gk
            nv = ph * lax.rsqrt(lane_mean(ph * ph) + EPS) * g
            rot = (nv * cos + pltpu.roll(nv, HD // 2, 1) * sin).astype(BF)
            if h < nq:
                q_ref[here, h * HD : (h + 1) * HD] = rot
            else:
                k_ref[here, (h - nq) * HD : (h - nq + 1) * HD] = rot


def group_rows(ref, here, g, group):
    return jnp.concatenate([ref[here, lanes(g * group + a, HD)] for a in range(group)], axis=0)


def attn_probs(q, k, off, mask_ref, group):
    s = dot_nt(q, k) * (SCALE * LOG2E)
    cut = s.shape[1] - QB
    last = jnp.exp2(s[:, cut:] + jnp.concatenate([mask_ref[...]] * group, axis=0))
    e = last if cut == 0 else jnp.concatenate([jnp.exp2(s[:, :cut] + off), last], axis=1)
    return e * (1.0 / jnp.sum(e, axis=-1, keepdims=True))


def attn_group(g, off, q_ref, k_ref, v_ref, att_ref, mask_ref):
    group = q_ref.shape[1] // k_ref.shape[1]
    hk = lanes(g, HD)
    for i in range(q_ref.shape[0] // QB):
        here, keys = slice(i * QB, (i + 1) * QB), slice(0, (i + 1) * QB)
        probs = attn_probs(group_rows(q_ref, here, g, group), k_ref[keys, hk], off, mask_ref, group)
        o = dot(probs.astype(BF), v_ref[keys, hk]).astype(BF)
        for a in range(group):
            att_ref[here, lanes(g * group + a, HD)] = o[a * QB : (a + 1) * QB]


def attn_group_back(g, i, off, q_ref, k_ref, v_ref, att_ref, da_ref, dq_ref, dk_ref, dv_ref, mask_ref):
    group = q_ref.shape[1] // k_ref.shape[1]
    hk = lanes(g, HD)
    here, keys = slice(i * QB, (i + 1) * QB), slice(0, (i + 1) * QB)
    q, da, att = (group_rows(ref, here, g, group) for ref in (q_ref, da_ref, att_ref))
    inner = jnp.sum(da.astype(F32) * att.astype(F32), axis=-1, keepdims=True)
    probs = attn_probs(q, k_ref[keys, hk], off, mask_ref, group)
    ds = (probs * (dot_nt(da, v_ref[keys, hk]) - inner)).astype(BF)
    dq = dot(ds, k_ref[keys, hk])
    for a in range(group):
        dq_ref[here, lanes(g * group + a, HD)] = dq[a * QB : (a + 1) * QB]
    dk_ref[keys, hk] += dot_tn(ds, q)
    dv_ref[keys, hk] += dot_tn(probs.astype(BF), da)


def attn_unproject(gq, gk, cos_ref, sin_ref, p_ref, dq_ref, dk_ref, dv_ref, dp_ref, w, dxn_ref, ggq_ref, ggk_ref):
    rows = p_ref.shape[0]
    tok = dxn_ref.shape[1]
    nq = dq_ref.shape[1] // HD
    nk = dk_ref.shape[1] // HD
    ggq_ref[...] = jnp.zeros_like(ggq_ref)
    ggk_ref[...] = jnp.zeros_like(ggk_ref)

    @pl.loop(0, rows // tok)
    def _(i):
        here = lanes(i, tok)
        cos = cos_ref[here, :]
        sin = sin_ref[here, :]
        sums = [jnp.zeros((1, HD), F32), jnp.zeros((1, HD), F32)]
        for h in range(nq + nk):
            which = 0 if h < nq else 1
            g = gq if h < nq else gk
            cols = slice(h * HD, (h + 1) * HD)
            if h < nq:
                d = dq_ref[here, cols] * SCALE
            else:
                d = dk_ref[here, (h - nq) * HD : (h - nq + 1) * HD] * SCALE
            dn = d * cos + pltpu.roll(d * sin, HD // 2, 1)
            ph = p_ref[here, cols].astype(F32)
            r = lax.rsqrt(lane_mean(ph * ph) + EPS)
            nh = ph * r
            dnh = dn * nh
            sums[which] += jnp.sum(dnh, axis=0, keepdims=True)
            dp_ref[here, cols] = (r * (dn * g - nh * lane_mean(dnh * g))).astype(BF)
        dp_ref[here, (nq + nk) * HD :] = dv_ref[here, :].astype(BF)
        ggq_ref[0:1, :] += sums[0]
        ggk_ref[0:1, :] += sums[1]
        dxn_ref[i] = dot_nt(dp_ref[here, :], rows_of(w)).astype(BF)


def feed_forward(nm_ref, og_ref, wgu_ref, wd_ref, hid_ref, dgu_ref, out_ref, dnm_ref):
    rows = nm_ref.shape[1]
    ff = hid_ref.shape[1]

    @pl.loop(0, nm_ref.shape[0])
    def _(i):
        here = lanes(i, rows)
        both = dot(nm_ref[i], rows_of(wgu_ref))
        gate, up = both[:, :ff], both[:, ff:]
        s = 1.0 / (1.0 + jnp.exp2(gate * -LOG2E))
        silu = gate * s
        hidden = (silu * up).astype(BF)
        hid_ref[here, :] = hidden
        dh = dot_nt(og_ref[i], rows_of(wd_ref))
        dgu_ref[here, :ff] = (dh * up * (s * (1.0 + gate * (1.0 - s)))).astype(BF)
        dgu_ref[here, ff:] = (dh * silu).astype(BF)
        dnm_ref[i] = dot_nt(dgu_ref[here, :], rows_of(wgu_ref)).astype(BF)
        out_ref[i] = dot(hidden, rows_of(wd_ref)).astype(BF)


def weight_grad(out_ref, left_ref, right, chunk=256):
    size = math.prod(out_ref.shape[1:-1])
    width = out_ref.shape[-1]

    @pl.loop(0, left_ref.shape[-1] // chunk)
    def _(i):
        left = left_ref[..., lanes(i, chunk)].reshape(-1, chunk)
        g = dot_tn(left, rows_of(right)).astype(BF)
        for j in range(chunk // size):
            out_ref[i * (chunk // size) + j] = g[j * size : (j + 1) * size].reshape(out_ref.shape[1:-1] + (width,))


MESH = pl.DeviceIdType.MESH


def rcopy(src, dst, send, recv, **device):
    return pltpu.make_async_remote_copy(
        src_ref=src, dst_ref=dst, send_sem=send, recv_sem=recv, device_id=device, device_id_type=MESH
    )


class Place:
    def __init__(self, n):
        self.n, self.line = n, n // 2
        self.dp, self.ctx = lax.axis_index("dp"), lax.axis_index("ctx")
        self.outer, self.inner = self.dp // 2, self.dp % 2
        self.dp_inner = self.outer * 2 + 1 - self.inner
        self.dp_up, self.dp_down = self.dp + 2, self.dp - 2
        self.has_up, self.has_down = self.outer < self.line - 1, self.outer > 0
        core = self.ctx % 2
        self.c_core = self.ctx + 1 - 2 * core
        self.c_x = (self.ctx + 2) % 4
        self.c_far = 3 - self.ctx
        mine = self.dp * 4 + self.ctx
        self.slab_to = {"dp": mine % n, "ctx": mine // n}
        source = self.ctx * n + self.dp
        self.slab_from = {"dp": source // 4, "ctx": source % 4}
        self.slab_stays = source == mine


def greet(place, slabs):
    barrier = pltpu.get_barrier_semaphore()

    def signal(**device):
        pl.semaphore_signal(barrier, inc=1, device_id=device, device_id_type=MESH)

    for c in (place.c_core, place.c_x, place.c_far):
        signal(ctx=c)
    for k in range(1, place.n):
        signal(dp=(place.dp + k) % place.n)
    count = place.n + 2
    for slab in slabs:

        @pl.when(jnp.logical_not(place.slab_stays))
        def _():
            signal(**slab)

        count = count + jnp.where(place.slab_stays, 0, 1)
    return barrier, count


class Gather:
    def __init__(self, place, bufs, sems):
        self.at, self.bufs, self.sems = place, bufs, sems

    @staticmethod
    def scratch(n, bufs):
        return pltpu.SemaphoreType.DMA((5, bufs, n // 2))

    def copy(self, b, p, way):
        at = self.at
        block = self.bufs[b].at[p * 2 + at.inner]
        device = (at.dp_up, at.dp_down, at.dp_inner)[way]
        recv = self.sems.at[4 if way == 2 else 3, b, p]
        return rcopy(block, block, self.sems.at[way, b, p], recv, dp=device)

    def send(self, p, up, down, inner=True):
        at = self.at
        for b in range(len(self.bufs)):
            if up:

                @pl.when(at.has_up)
                def _():
                    self.copy(b, p, 0).start()

            if down:

                @pl.when(at.has_down)
                def _():
                    self.copy(b, p, 1).start()

            if inner:
                self.copy(b, p, 2).start()

    def start(self):
        self.send(self.at.outer, True, True)

    def start_inner(self):
        self.send(self.at.outer, False, False)

    def start_line(self):
        self.send(self.at.outer, True, True, False)

    def step(self, t):
        at = self.at
        for p, there, up in ((at.outer - t, at.outer >= t, True), (at.outer + t, at.outer + t < at.line, False)):

            @pl.when(there)
            def _():
                for b in range(len(self.bufs)):
                    self.copy(b, p, 0).wait_recv()
                self.send(p, up, not up)

    def arrive(self):
        at = self.at
        for b in range(len(self.bufs)):
            for p in range(at.line):
                block = self.bufs[b].at[p * 2 + 1 - at.inner]
                rcopy(block, block, self.sems.at[2, b, p], self.sems.at[4, b, p], dp=at.dp_inner).wait_recv()

    def finish(self):
        at = self.at
        for b in range(len(self.bufs)):
            for p in range(at.line):
                self.copy(b, p, 2).wait_send()

                @pl.when(jnp.logical_and(at.has_up, p <= at.outer))
                def _():
                    self.copy(b, p, 0).wait_send()

                @pl.when(jnp.logical_and(at.has_down, p >= at.outer))
                def _():
                    self.copy(b, p, 1).wait_send()


class Reduce:
    def __init__(self, place, parts, from_inner, from_line, sems):
        self.at, self.parts, self.from_inner, self.from_line, self.sems = place, parts, from_inner, from_line, sems

    @staticmethod
    def scratch(n, blocks):
        line = n // 2
        return (
            [pltpu.VMEM((line, *dims), dtype) for dims, dtype in blocks],
            [pltpu.VMEM((line + 1, *dims), dtype) for dims, dtype in blocks],
            pltpu.SemaphoreType.DMA((4, len(blocks), line + 1)),
        )

    def inner_copy(self, b, p):
        at = self.at
        return rcopy(
            self.parts[b].at[p * 2 + 1 - at.inner], self.from_inner[b].at[p],
            self.sems.at[0, b, p], self.sems.at[1, b, p], dp=at.dp_inner,
        )

    def line_copy(self, b, p, slot, up):
        at = self.at
        return rcopy(
            self.from_inner[b].at[p], self.from_line[b].at[slot],
            self.sems.at[2, b, p], self.sems.at[3, b, slot], dp=at.dp_up if up else at.dp_down,
        )

    def start(self, which):
        at = self.at
        for d in range(at.line - 1, -1, -1):
            for p, there in ((at.outer + d, at.outer + d < at.line), (at.outer - d, at.outer >= d))[: 2 if d else 1]:

                @pl.when(there)
                def _():
                    for b in which:
                        self.inner_copy(b, p).start()

    def total(self, b, p, slots):
        s = self.parts[b][p * 2 + self.at.inner].astype(F32) + self.from_inner[b][p].astype(F32)
        for slot in slots:
            s = s + self.from_line[b][slot].astype(F32)
        return s

    def step(self, d, which):
        at = self.at
        for p, there, more, up in (
            (at.outer + d, at.outer + d < at.line, at.has_down, True),
            (at.outer - d, at.outer >= d, at.has_up, False),
        ):
            for b in which:

                @pl.when(there)
                def _():
                    self.inner_copy(b, p).wait_recv()
                    into = self.from_inner[b].at[p]

                    @pl.when(more)
                    def _():
                        self.line_copy(b, p, p, up).wait_recv()
                        into[...] = self.total(b, p, [p]).astype(into.dtype)

                    @pl.when(jnp.logical_not(more))
                    def _():
                        into[...] = self.total(b, p, []).astype(into.dtype)

                    slot = p if up or d > 1 else at.line
                    self.line_copy(b, p, slot, up).start()

    def result(self, b, store):
        at = self.at
        p = at.outer
        self.inner_copy(b, p).wait_recv()
        lo, hi = at.has_down, at.has_up

        @pl.when(lo)
        def _():
            self.line_copy(b, p, p, True).wait_recv()

        @pl.when(hi)
        def _():
            self.line_copy(b, p, at.line, False).wait_recv()

        @pl.when(jnp.logical_and(lo, hi))
        def _():
            store(self.total(b, p, [p, at.line]))

        @pl.when(jnp.logical_and(lo, jnp.logical_not(hi)))
        def _():
            store(self.total(b, p, [p]))

        @pl.when(jnp.logical_and(hi, jnp.logical_not(lo)))
        def _():
            store(self.total(b, p, [at.line]))

    def finish(self):
        at = self.at
        for b in range(len(self.parts)):
            for p in range(at.line):
                self.inner_copy(b, p).wait_send()

                @pl.when(p != at.outer)
                def _():
                    self.line_copy(b, p, p, True).wait_send()


class CtxGather:
    def __init__(self, place, buf, sems):
        self.at, self.buf, self.sems = place, buf, sems

    def copy(self, k, owner):
        block = self.buf.at[owner]
        ctx = self.at.c_x if k == 1 else self.at.c_core
        return rcopy(block, block, self.sems.at[0, k], self.sems.at[1, k], ctx=ctx)

    def start(self):
        self.copy(1, self.at.ctx).start()
        self.copy(0, self.at.ctx).start()

    def forward(self):
        self.copy(1, self.at.c_x).wait_recv()
        self.copy(2, self.at.c_x).start()

    def arrive(self):
        self.copy(0, self.at.c_core).wait_recv()
        self.copy(2, self.at.c_far).wait_recv()

    def finish(self):
        for k in range(3):
            self.copy(k, self.at.ctx).wait_send()


class CtxReduce:
    def __init__(self, place, part, got, sems):
        self.at, self.part, self.got, self.sems = place, part, got, sems

    def copy(self, k):
        at = self.at
        block = self.got.at[1] if k == 2 else self.part.at[(at.c_core, at.c_far)[k]]
        return rcopy(block, self.got.at[k], self.sems.at[0, k], self.sems.at[1, k], ctx=at.c_x if k == 2 else at.c_core)

    def start(self):
        self.copy(1).start()
        self.copy(0).start()

    def across(self):
        self.copy(1).wait_recv()
        into = self.got.at[1]
        into[...] = (self.part[self.at.c_x].astype(F32) + into[...].astype(F32)).astype(into.dtype)
        self.copy(2).start()

    def result(self):
        self.copy(0).wait_recv()
        self.copy(2).wait_recv()
        return self.part[self.at.ctx].astype(F32) + self.got[0].astype(F32) + self.got[2].astype(F32)

    def finish(self):
        for k in range(3):
            self.copy(k).wait_send()


class Quarters:
    def __init__(self, place, src, dst, sems):
        self.at, self.src, self.dst, self.sems = place, src, dst, sems

    def copies(self):
        at = self.at
        return [
            rcopy(self.src.at[c], self.dst.at[at.ctx], self.sems.at[0, k], self.sems.at[1, k], ctx=c)
            for k, c in enumerate((at.c_x, at.c_far, at.c_core))
        ]

    def start(self):
        for c in self.copies():
            c.start()
        self.dst[self.at.ctx] = self.src[self.at.ctx]

    def finish(self):
        for c in self.copies():
            c.wait()


class Slab:
    def __init__(self, place, src, dst, sems, to):
        self.at, self.src, self.dst, self.sems, self.to = place, src, dst, sems, to

    def copy(self):
        return rcopy(self.src, self.dst, self.sems.at[0, 0], self.sems.at[1, 0], **self.to)

    def start(self):
        @pl.when(self.at.slab_stays)
        def _():
            self.dst[...] = self.src[...]

        @pl.when(jnp.logical_not(self.at.slab_stays))
        def _():
            self.copy().start()

    def finish(self):
        @pl.when(jnp.logical_not(self.at.slab_stays))
        def _():
            self.copy().wait()


class Exchange:
    def __init__(self, place, src, dst, cap, sems):
        self.at, self.src, self.dst, self.cap, self.sems = place, src, dst, cap, sems

    def rows(self, ref, j):
        if len(ref.shape) == 3:
            size = ref.shape[1]
            start = j * self.cap
            return ref.at[start // size, pl.ds(pl.multiple_of(start % size, self.cap), self.cap)]
        return ref.at[pl.ds(pl.multiple_of(j * self.cap, self.cap), self.cap)]

    def copy(self, k):
        at = self.at
        to = (at.dp + k) % at.n
        return rcopy(self.rows(self.src, to), self.rows(self.dst, at.dp), self.sems.at[0, k], self.sems.at[1, k], dp=to)

    def start(self):
        for k in range(1, self.at.n):
            self.copy(k).start()
        self.rows(self.dst, self.at.dp)[...] = self.rows(self.src, self.at.dp)[...]

    def finish(self):
        for k in range(1, self.at.n):
            self.copy(k).wait()


def sem_pairs(count):
    return pltpu.SemaphoreType.DMA((2, count))


def norm_back(c, v, gain):
    r = lax.rsqrt(jnp.mean(v * v, axis=-1, keepdims=True) + EPS)
    nv = v * r
    cg = c * gain
    return jnp.sum(c * nv, axis=0, keepdims=True), r * (cg - nv * jnp.mean(cg * nv, axis=-1, keepdims=True))


def into(ref):
    def store(v):
        ref[...] = v.astype(ref.dtype)

    return store


def quarter_columns(dst_ref, weights):
    for c in range(4):
        start = 0
        for w in weights:
            size = w.shape[1] // 4
            dst_ref[c, :, start : start + size] = w[:, c * size : (c + 1) * size]
            start += size


def route(n, cap, dest_ref, place_ref, labs_ref):
    tok = dest_ref.shape[1]
    dest = dest_ref[...]
    owner = jnp.right_shift(dest, (4 * tok).bit_length() - 1)
    slot = jnp.bitwise_and(dest, tok - 1)
    lines = lax.broadcasted_iota(jnp.int32, (n, tok), 0)
    hot = (lines == owner).astype(F32)
    before = lax.broadcasted_iota(jnp.int32, (tok, tok), 0) < lax.broadcasted_iota(jnp.int32, (tok, tok), 1)
    rank = dot(hot.astype(BF), before.astype(BF))
    send = jnp.sum(hot * (rank + (lines * cap).astype(F32)), axis=0, keepdims=True).astype(jnp.int32)
    place = (lax.broadcasted_iota(jnp.int32, (n * cap, tok), 0) == send).astype(BF)
    place_ref[...] = place
    labels = dot_nt(jnp.broadcast_to((slot + 1).astype(F32), (8, tok)).astype(BF), place)
    labs_ref[...] = jnp.zeros_like(labs_ref)
    for j in range(n):
        labs_ref[j * 8 : j * 8 + 8, :cap] = labels[:, j * cap : (j + 1) * cap]


def gain_tile(at, raw_ref, counts):
    index = at.dp * 4 + at.ctx
    raw = jnp.broadcast_to(raw_ref[...], (8, 128)).astype(BF)
    source = lax.broadcasted_iota(jnp.int32, (128, 128), 0)
    target = lax.broadcasted_iota(jnp.int32, (128, 128), 1)
    lines = lax.broadcasted_iota(jnp.int32, (8, 128), 0)
    total, start = jnp.zeros((8, 128), F32), 0
    for k, count in enumerate(counts):
        move = (target - (index * count) % 128 == source - start) & (source >= start) & (source < start + count)
        total = total + jnp.where(lines == k, dot(raw, move.astype(BF)), 0.0)
        start += count
    return total


def final_body(counts, ig, layer, qkv, o, gu, gd, small, layer_out, ig_out, ga, gq, gk, gv, gqg, gkg, go, gm, gg, gup, gdn):
    index = lax.axis_index("dp") * 4 + lax.axis_index("ctx")
    layer_out[...] = layer[...]
    ig_out[...] = ig[...]
    for blocks, outs in ((qkv, (gq, gk, gv)), (gu, (gg, gup))):
        for c in range(4):
            start = 0
            for out in outs:
                size = out.shape[1] // 4
                out[:, c * size : (c + 1) * size] = blocks[c, :, start : start + size].astype(F32)
                start += size
    go[...] = o[...].astype(F32)
    gdn[...] = gd[...].astype(F32)
    for k, (out, count) in enumerate(zip((ga, gm, gqg, gkg), counts)):
        row = pltpu.roll(small[...], (128 - (index * count) % 128) % 128, 1)
        out[...] = row[k : k + 1, :count]


def layer_body(
    n, cap, counts,
    in_ref, dest_ref, doc_ref, raw_ref, og_ref, wq_src, wk_src, wv_src, wo_src, wg_src, wu_src, wd_src, cos_ref, sin_ref,
    ig_ref, layer_ref, qkv_out, o_out, gu_out, gd_out, gain_out,
    wqkv_ref, wo_ref, wgu_ref, wd_ref, og_all, x_own, pick_ref, ga_ref, gm_ref, q_ref, k_ref, v_ref, p_ref, xn_ref, att_ref, nm_ref, mid_ref,
    recv, labels, gains_c, gains_n, x_ref, part_ref, got, mask_ref,
    hid_ref, dgu_ref, outp_ref, got_d, got_o, dmid_ref, dq_ref, dk_ref, dv_ref, ggq_ref, ggk_ref, ggm_ref, gains, recv_back,
    yi0, yi1, ln0, ln1, s_ra, yo, lo, s_rb, yq, yg, lq, lg, s_rc,
    gain_sum, gain_all, qkv_ref, gu_ref, place_ref, lab_ref,
    s_ga, s_gb, s_gc, s_gd4, s_rows, s_labs, s_qkv, s_gu, s_wo, s_wd, s_gain, s_x, s_og, s_red, s_nm,
    s_dnm, s_out, s_db, s_dxn, s_rows_back, s_gu_back, s_gd, s_qkv_back, s_o, s_gain_back,
):
    at = Place(n)
    barrier, count = greet(at, (at.slab_from, at.slab_to))
    quarter_columns(qkv_ref, (wq_src, wk_src, wv_src))
    gains_c[at.ctx] = gain_tile(at, raw_ref, counts)
    route(n, cap, dest_ref, place_ref, lab_ref)
    tok = in_ref.shape[0]
    for half in range(n * cap // tok):
        part_ref[half] = dot(place_ref[half * tok : (half + 1) * tok, :], in_ref[...]).astype(BF)
    pl.semaphore_wait(barrier, count)
    qkv = Quarters(at, qkv_ref, wqkv_ref.at[at.dp], s_qkv)
    rows = Exchange(at, part_ref, recv, cap, s_rows)
    labs = Exchange(at, lab_ref, labels, 8, s_labs)
    qkv.start()
    gain_copies = [
        rcopy(gains_c.at[at.ctx], gains_c.at[at.ctx], s_gain.at[0, k], s_gain.at[1, k], ctx=c)
        for k, c in enumerate((at.c_x, at.c_far, at.c_core))
    ]
    for g in gain_copies:
        g.start()
    quarter_columns(gu_ref, (wg_src, wu_src))
    wo = Slab(at, wo_src, wo_ref.at[at.slab_to["dp"]], s_wo, at.slab_to)
    wd = Slab(at, wd_src, wd_ref.at[at.slab_to["dp"]], s_wd, at.slab_to)
    gu = Quarters(at, gu_ref, wgu_ref.at[at.dp], s_gu)
    labs.start()
    rows.start()
    gu.start()
    wo.start()
    wd.start()
    for g in gain_copies:
        g.wait()
    gains_n[at.dp] = gains_c[0] + gains_c[1] + gains_c[2] + gains_c[3]
    qkv.finish()
    first = Gather(at, [wqkv_ref, gains_n], s_ga)
    first.start()
    og_all[at.ctx] = og_ref[...]
    og = CtxGather(at, og_all, s_og)
    gu.finish()
    og.start()
    third = Gather(at, [wgu_ref], s_gc)
    third.start_inner()
    labs.finish()
    slots = lax.broadcasted_iota(jnp.int32, (tok, cap), 0).astype(F32) + 1.0
    for j in range(n):
        pick_ref[:, j * cap : (j + 1) * cap] = (slots == labels[j * 8 : j * 8 + 1, :cap]).astype(BF)
    first.step(1)
    rows.finish()
    owned = dot(pick_ref[...], recv[...]).astype(BF)
    x_ref[at.ctx] = owned
    x_own[...] = owned
    x = CtxGather(at, x_ref, s_x)
    x.start()
    first.step(2)
    third.start_line()
    wo.finish()
    second = Gather(at, [wo_ref], s_gb)
    second.start()
    for t in range(3, at.line):
        first.step(t)
    second.step(1)
    og.forward()
    x.forward()
    first.arrive()
    own = 4 * ga_ref.shape[1] // (4 * n)
    ga_ref[...] = jnp.zeros_like(ga_ref)
    gm_ref[...] = jnp.zeros_like(gm_ref)
    gqk = jnp.zeros((8, 128), F32)
    for d in range(n):
        tile = slice(d * own // 128 * 128, d * own // 128 * 128 + 128)
        block = gains_n[d]
        ga_ref[0:1, tile] += block[0:1]
        gm_ref[0:1, tile] += block[1:2]
        gqk = gqk + block
    off = jnp.where(doc_ref[0:1, 0:1] > 0, 0.0, MASKED).astype(F32)
    mask_ref[...] = mask_block(off)
    x.arrive()
    second.step(2)
    attn_project(x_ref, wqkv_ref, ga_ref, gqk[2:3], gqk[3:4], cos_ref, sin_ref, q_ref, k_ref, v_ref, p_ref, xn_ref)
    for t in range(3, at.line):
        second.step(t)
    third.step(1)
    wd.finish()
    fourth = Gather(at, [wd_ref], s_gd4)
    fourth.start()
    nk = k_ref.shape[1] // HD

    @pl.loop(0, nk)
    def _(g):
        attn_group(g, off, q_ref, k_ref, v_ref, att_ref, mask_ref)

    third.step(2)
    fourth.step(1)
    second.arrive()

    @pl.loop(0, 4)
    def _(i):
        part_ref[i] = dot(att_ref[lanes(i, tok), :], rows_of(wo_ref)).astype(BF)

    red = CtxReduce(at, part_ref, got, s_red)
    red.start()
    red.across()
    for t in range(3, at.line):
        third.step(t)
        fourth.step(t - 1)
    middle = x_own[...].astype(F32) + red.result()
    mid_ref[...] = middle
    r = lax.rsqrt(jnp.mean(middle * middle, axis=-1, keepdims=True) + EPS)
    nm_ref[at.ctx] = (middle * r * gm_ref[0:1, :]).astype(BF)
    nm = CtxGather(at, nm_ref, s_nm)
    nm.start()
    fourth.step(at.line - 1)
    nm.forward()
    nm.arrive()
    og.arrive()
    third.arrive()
    fourth.arrive()
    for part in (first, second, third, fourth, og, x, nm, red):
        part.finish()
    feed_forward(nm_ref, og_all, wgu_ref, wd_ref, hid_ref, dgu_ref, outp_ref, part_ref)
    db_ref, da_ref, dp_ref = x_ref, hid_ref.at[:, : q_ref.shape[1]], dgu_ref.at[:, : wqkv_ref.shape[-1]]
    last = at.line - 1
    dnm = CtxReduce(at, part_ref, got_d, s_dnm)
    dnm.start()
    weight_grad(wd_ref, hid_ref, og_all, 384)
    first = Reduce(at, [wgu_ref, wd_ref], [yi0, yi1], [ln0, ln1], s_ra)
    first.start([1])
    dnm.across()
    weight_grad(wgu_ref, nm_ref, dgu_ref)
    first.start([0])
    out = CtxReduce(at, outp_ref, got_o, s_out)
    dk_ref[...] = jnp.zeros_like(dk_ref)
    dv_ref[...] = jnp.zeros_like(dv_ref)
    first.step(last, [1])
    gg, d = norm_back(dnm.result(), mid_ref[...], gm_ref[0:1, :])
    ggm_ref[...] = gg
    d = d + og_ref[...].astype(F32)
    dmid_ref[...] = d
    db_ref[at.ctx] = d.astype(BF)
    db = CtxGather(at, db_ref, s_db)
    db.start()
    out.start()
    for t in range(last - 1, 0, -1):
        first.step(t, [1])
    db.forward()
    out.across()
    db.arrive()
    tok = db_ref.shape[1]

    @pl.loop(0, 4)
    def _(i):
        da_ref[lanes(i, tok), :] = dot_nt(db_ref[i], rows_of(wo_ref)).astype(BF)

    first.step(last, [0])
    for g in range(k_ref.shape[1] // HD):
        for i in range(q_ref.shape[0] // QB):
            attn_group_back(g, i, off, q_ref, k_ref, v_ref, att_ref, da_ref, dq_ref, dk_ref, dv_ref, mask_ref)
        if g == 0:
            for t in range(last - 1, 1, -1):
                first.step(t, [0])
    dxn_ref = nm_ref
    attn_unproject(gqk[2:3], gqk[3:4], cos_ref, sin_ref, p_ref, dq_ref, dk_ref, dv_ref, dp_ref, wqkv_ref, dxn_ref, ggq_ref, ggk_ref)
    dxn = CtxReduce(at, dxn_ref, got, s_dxn)
    dxn.start()
    first.step(1, [0])
    weight_grad(wqkv_ref, xn_ref, dp_ref)
    third = Reduce(at, [wqkv_ref, gains], [yq, yg], [lq, lg], s_rc)
    third.start([0])
    dxn.across()
    weight_grad(wo_ref, att_ref, db_ref)
    second = Reduce(at, [wo_ref], [yo], [lo], s_rb)
    second.start([0])
    first.result(1, into(yi1.at[at.outer]))
    gd = Slab(at, yi1.at[at.outer], gd_out, s_gd, at.slab_from)
    gd.start()
    first.result(0, into(yi0.at[at.outer]))
    gu = Quarters(at, yi0.at[at.outer], gu_out, s_gu_back)
    gu.start()
    third.step(last, [0])
    gg, d = norm_back(dxn.result(), x_own[...].astype(F32), ga_ref[0:1, :])
    owned = (dmid_ref[...] + d).astype(BF)
    recv[...] = dot_tn(pick_ref[...], owned).astype(BF)
    rows = Exchange(at, recv, recv_back, cap, s_rows_back)
    rows.start()
    own = 4 * gg.shape[1] // (4 * n)
    lines = lax.broadcasted_iota(jnp.int32, (8, 128), 0)
    for j in range(n):
        tile = slice(j * own // 128 * 128, j * own // 128 * 128 + 128)
        gains[j] = (
            jnp.where(lines == 0, gg[:, tile], 0.0) + jnp.where(lines == 1, ggm_ref[0:1, tile], 0.0)
            + jnp.where(lines == 2, ggq_ref[0:1, :], 0.0) + jnp.where(lines == 3, ggk_ref[0:1, :], 0.0)
        )
    third.start([1])
    second.step(last, [0])
    for t in range(last - 1, 0, -1):
        third.step(t, [0])
        second.step(t, [0])
    layer_ref[...] = (mid_ref[...] + out.result()).astype(BF)
    for t in range(last, 0, -1):
        third.step(t, [1])
    second.result(0, into(yo.at[at.outer]))
    o = Slab(at, yo.at[at.outer], o_out, s_o, at.slab_from)
    o.start()
    third.result(0, into(yq.at[at.outer]))
    qkv = Quarters(at, yq.at[at.outer], qkv_out, s_qkv_back)
    qkv.start()
    third.result(1, into(gain_sum))
    small = [
        rcopy(gain_sum, gain_all.at[at.ctx], s_gain_back.at[0, k], s_gain_back.at[1, k], ctx=c)
        for k, c in enumerate((at.c_x, at.c_far, at.c_core))
    ]
    for g in small:
        g.start()
    gain_all[at.ctx] = gain_sum[...]
    rows.finish()
    ig_ref[...] = dot_tn(place_ref[...], recv_back[...]).astype(BF)
    for g in small:
        g.wait()
    gain_out[...] = gain_all[0] + gain_all[1] + gain_all[2] + gain_all[3]
    for part in (qkv, o, gu, gd, dxn, db, out, dnm, first, second, third):
        part.finish()


def shape(*dims, dtype=BF):
    return jax.ShapeDtypeStruct(dims, dtype)


def linked(body, outs, scratch, name, number):
    return pl.pallas_call(
        body,
        out_shape=outs,
        scratch_shapes=scratch,
        compiler_params=pltpu.CompilerParams(vmem_limit_bytes=VMEM_LIMIT, collective_id=number, has_side_effects=True),
        name=name,
    )


def local(
    layer_input, dest_slot, doc_len, out_grad, attn_gain, w_query, w_key, w_value, q_gain, k_gain,
    w_out, mlp_gain, w_gate, w_up, w_down,
):
    tok, width = layer_input.shape
    n = lax.axis_size("dp")
    cap = 2 * tok // n
    rows = 4 * tok
    slabs = n * cap
    rq, ro, rd = w_query.shape[0], w_out.shape[0], w_down.shape[0]
    ff = rd * n
    counts = (attn_gain.shape[0], mlp_gain.shape[0], q_gain.shape[0], k_gain.shape[0])
    raw = jnp.pad(jnp.concatenate([attn_gain, mlp_gain, q_gain, k_gain]), (0, 128 - sum(counts))).astype(F32).reshape(1, 128)
    fw = 2 * ff
    cos, sin = rope_tables(rows)
    blocks = ([((4, rq, fw), BF), ((rd, width), BF)], [((ro, width), BF)], [((4, rq, 1024), BF), ((8, 128), F32)])
    reduces = []
    for red, lines, sems in (Reduce.scratch(n, b) for b in blocks):
        reduces += [*red, *lines, sems]
    vm = pltpu.VMEM
    group = (4, tok, width)
    input_grad, layer_output, g_qkv, g_o, g_gu, g_d, small = linked(
        functools.partial(layer_body, n, cap, counts),
        (shape(tok, width), shape(tok, width), shape(4, rq, 1024), shape(ro, width), shape(4, rq, fw), shape(rd, width), shape(8, 128, dtype=F32)),
        [vm((n, 4, rq, 1024), BF), vm((n, ro, width), BF), vm((n, 4, rq, fw), BF), vm((n, rd, width), BF), vm(group, BF), vm((tok, width), BF),
         vm((tok, slabs), BF), vm((8, width), F32), vm((8, width), F32), vm((rows, 512), BF), vm((rows, 256), BF), vm((rows, 256), BF),
         vm((rows, 768), BF), vm((rows, width), BF), vm((rows, 512), BF), vm(group, BF), vm((tok, width), F32),
         vm((slabs, width), BF), vm((n * 8, 128), F32), vm((4, 8, 128), F32), vm((n, 8, 128), F32),
         vm(group, BF), vm(group, BF), vm((3, tok, width), BF), vm((QB, QB), F32),
         vm((rows, ff), BF), vm((rows, fw), BF), vm(group, BF), vm((3, tok, width), BF), vm((3, tok, width), BF),
         vm((tok, width), F32), vm((rows, 512), F32), vm((rows, 256), F32), vm((rows, 256), F32),
         vm((8, HD), F32), vm((8, HD), F32), vm((1, width), F32), vm((n, 8, 128), F32), vm((slabs, width), BF),
         *reduces,
         vm((8, 128), F32), vm((4, 8, 128), F32), vm((4, rq, 1024), BF), vm((4, rq, fw), BF), vm((slabs, tok), BF), vm((n * 8, 128), F32),
         Gather.scratch(n, 2), Gather.scratch(n, 1), Gather.scratch(n, 1), Gather.scratch(n, 1), sem_pairs(n), sem_pairs(n), sem_pairs(3), sem_pairs(3),
         sem_pairs(1), sem_pairs(1), sem_pairs(3), sem_pairs(3), sem_pairs(3), sem_pairs(3), sem_pairs(3),
         sem_pairs(3), sem_pairs(3), sem_pairs(3), sem_pairs(3), sem_pairs(n), sem_pairs(3), sem_pairs(1), sem_pairs(3), sem_pairs(1), sem_pairs(3)],
        "layer", 0,
    )(layer_input, dest_slot.reshape(1, tok), doc_len, raw, out_grad, w_query, w_key, w_value, w_out, w_gate, w_up, w_down, cos, sin)
    grads = [shape(*w.shape, dtype=F32) for w in (w_query, w_key, w_value, w_out, w_gate, w_up, w_down)]
    gains = [shape(1, c, dtype=F32) for c in counts]
    outs = (shape(tok, width), shape(tok, width), gains[0], *grads[:3], gains[2], gains[3], grads[3], gains[1], *grads[4:])
    outs = pl.pallas_call(functools.partial(final_body, counts), out_shape=outs, name="final")(
        input_grad, layer_output, g_qkv, g_o, g_gu, g_d, small
    )
    return tuple(o.reshape(-1) if o.shape[0] == 1 else o for o in outs)


def solution(mesh):
    rows = P(BOTH, None)
    vec = P(BOTH)
    return jax.shard_map(
        local,
        mesh=mesh,
        in_specs=(rows, vec, P("dp", None), rows, vec, rows, rows, rows, vec, vec, rows, vec, rows, rows, rows),
        out_specs=(rows, rows, vec, rows, rows, rows, vec, vec, rows, vec, rows, rows, rows),
        check_vma=False,
    )
```

```python
import functools
import math

import jax
import jax.numpy as jnp
import numpy as np
from jax import lax
from jax.experimental import pallas as pl
from jax.experimental.pallas import tpu as pltpu
from jax.sharding import PartitionSpec as P

H = 16
KVH = 8
HD = 128
EPS = 1e-06
THETA = 1000000.0
MASKED = -1e30
QB = 128
SCALE = HD ** (-0.5)
LOG2E = math.log2(math.e)
BF = jnp.bfloat16
F32 = jnp.float32
BOTH = ("dp", "ctx")
VMEM_LIMIT = 62 << 20


def dot(a, b):
    return lax.dot_general(a, b, (((1,), (0,)), ((), ())), preferred_element_type=F32)


def dot_nt(a, b):
    return lax.dot_general(a, b, (((1,), (1,)), ((), ())), preferred_element_type=F32)


def dot_tn(a, b):
    return lax.dot_general(a, b, (((0,), (0,)), ((), ())), preferred_element_type=F32)


def lanes(start, size):
    return pl.ds(pl.multiple_of(start * size, size), size)


def rope_tables(rows):
    inverse = np.exp(np.arange(HD // 2, dtype=np.float32) * np.float32(-2.0 / HD * math.log(THETA)))
    doubled = np.concatenate([inverse, inverse]).astype(np.float32)
    angles = np.arange(rows, dtype=np.float32)[:, None] * doubled[None, :]
    sign = np.where(np.arange(HD) < HD // 2, -1.0, 1.0).astype(np.float32)
    return np.cos(angles), np.sin(angles) * sign[None, :]


def mask_block(off_bias):
    rows = lax.broadcasted_iota(jnp.int32, (QB, QB), 0)
    cols = lax.broadcasted_iota(jnp.int32, (QB, QB), 1)
    return jnp.where(rows == cols, 0.0, jnp.where(cols < rows, off_bias, MASKED))


def lane_mean(v):
    ones = jnp.full((HD, HD), 1.0 / HD, BF)
    high = v.astype(BF)
    return dot(high, ones) + dot((v - high.astype(F32)).astype(BF), ones)


def rows_of(ref):
    value = ref[...]
    return value.reshape(-1, value.shape[-1])


def attn_project(x_ref, w, ga, gq, gk, cos_ref, sin_ref, q_ref, k_ref, v_ref, p_ref, xn_ref):
    rows = xn_ref.shape[0]
    tok = x_ref.shape[1]
    nq = q_ref.shape[1] // HD
    nk = k_ref.shape[1] // HD

    @pl.loop(0, rows // tok)
    def _(i):
        here = lanes(i, tok)
        x = x_ref[i].astype(F32)
        r = lax.rsqrt(jnp.mean(x * x, axis=-1, keepdims=True) + EPS)
        xn = (x * r * ga[0:1, :]).astype(BF)
        xn_ref[here, :] = xn
        p = dot(xn, rows_of(w))
        p_ref[here, :] = p[:, : (nq + nk) * HD].astype(BF)
        v_ref[here, :] = p[:, (nq + nk) * HD :].astype(BF)
        cos = cos_ref[here, :]
        sin = sin_ref[here, :]
        for h in range(nq + nk):
            ph = p[:, h * HD : (h + 1) * HD]
            g = gq if h < nq else gk
            nv = ph * lax.rsqrt(lane_mean(ph * ph) + EPS) * g
            rot = (nv * cos + pltpu.roll(nv, HD // 2, 1) * sin).astype(BF)
            if h < nq:
                q_ref[here, h * HD : (h + 1) * HD] = rot
            else:
                k_ref[here, (h - nq) * HD : (h - nq + 1) * HD] = rot


def group_rows(ref, here, g, group):
    return jnp.concatenate([ref[here, lanes(g * group + a, HD)] for a in range(group)], axis=0)


def attn_probs(q, k, off, mask_ref, group):
    s = dot_nt(q, k) * (SCALE * LOG2E)
    cut = s.shape[1] - QB
    last = jnp.exp2(s[:, cut:] + jnp.concatenate([mask_ref[...]] * group, axis=0))
    e = last if cut == 0 else jnp.concatenate([jnp.exp2(s[:, :cut] + off), last], axis=1)
    return e * (1.0 / jnp.sum(e, axis=-1, keepdims=True))


def attn_group(g, off, q_ref, k_ref, v_ref, att_ref, mask_ref):
    group = q_ref.shape[1] // k_ref.shape[1]
    hk = lanes(g, HD)
    for i in range(q_ref.shape[0] // QB):
        here, keys = slice(i * QB, (i + 1) * QB), slice(0, (i + 1) * QB)
        probs = attn_probs(group_rows(q_ref, here, g, group), k_ref[keys, hk], off, mask_ref, group)
        o = dot(probs.astype(BF), v_ref[keys, hk]).astype(BF)
        for a in range(group):
            att_ref[here, lanes(g * group + a, HD)] = o[a * QB : (a + 1) * QB]


def attn_group_back(g, i, off, q_ref, k_ref, v_ref, att_ref, da_ref, dq_ref, dk_ref, dv_ref, mask_ref):
    group = q_ref.shape[1] // k_ref.shape[1]
    hk = lanes(g, HD)
    here, keys = slice(i * QB, (i + 1) * QB), slice(0, (i + 1) * QB)
    q, da, att = (group_rows(ref, here, g, group) for ref in (q_ref, da_ref, att_ref))
    inner = jnp.sum(da.astype(F32) * att.astype(F32), axis=-1, keepdims=True)
    probs = attn_probs(q, k_ref[keys, hk], off, mask_ref, group)
    ds = (probs * (dot_nt(da, v_ref[keys, hk]) - inner)).astype(BF)
    dq = dot(ds, k_ref[keys, hk])
    for a in range(group):
        dq_ref[here, lanes(g * group + a, HD)] = dq[a * QB : (a + 1) * QB]
    dk_ref[keys, hk] += dot_tn(ds, q)
    dv_ref[keys, hk] += dot_tn(probs.astype(BF), da)


def attn_unproject(gq, gk, cos_ref, sin_ref, p_ref, dq_ref, dk_ref, dv_ref, dp_ref, w, dxn_ref, ggq_ref, ggk_ref):
    rows = p_ref.shape[0]
    tok = dxn_ref.shape[1]
    nq = dq_ref.shape[1] // HD
    nk = dk_ref.shape[1] // HD
    ggq_ref[...] = jnp.zeros_like(ggq_ref)
    ggk_ref[...] = jnp.zeros_like(ggk_ref)

    @pl.loop(0, rows // tok)
    def _(i):
        here = lanes(i, tok)
        cos = cos_ref[here, :]
        sin = sin_ref[here, :]
        sums = [jnp.zeros((1, HD), F32), jnp.zeros((1, HD), F32)]
        for h in range(nq + nk):
            which = 0 if h < nq else 1
            g = gq if h < nq else gk
            cols = slice(h * HD, (h + 1) * HD)
            if h < nq:
                d = dq_ref[here, cols] * SCALE
            else:
                d = dk_ref[here, (h - nq) * HD : (h - nq + 1) * HD] * SCALE
            dn = d * cos + pltpu.roll(d * sin, HD // 2, 1)
            ph = p_ref[here, cols].astype(F32)
            r = lax.rsqrt(lane_mean(ph * ph) + EPS)
            nh = ph * r
            dnh = dn * nh
            sums[which] += jnp.sum(dnh, axis=0, keepdims=True)
            dp_ref[here, cols] = (r * (dn * g - nh * lane_mean(dnh * g))).astype(BF)
        dp_ref[here, (nq + nk) * HD :] = dv_ref[here, :].astype(BF)
        ggq_ref[0:1, :] += sums[0]
        ggk_ref[0:1, :] += sums[1]
        dxn_ref[i] = dot_nt(dp_ref[here, :], rows_of(w)).astype(BF)


def feed_forward(nm_ref, og_ref, wgu_ref, wd_ref, hid_ref, dgu_ref, out_ref, dnm_ref):
    rows = nm_ref.shape[1]
    ff = hid_ref.shape[1]

    @pl.loop(0, nm_ref.shape[0])
    def _(i):
        here = lanes(i, rows)
        both = dot(nm_ref[i], rows_of(wgu_ref))
        gate, up = both[:, :ff], both[:, ff:]
        s = 1.0 / (1.0 + jnp.exp2(gate * -LOG2E))
        silu = gate * s
        hidden = (silu * up).astype(BF)
        hid_ref[here, :] = hidden
        dh = dot_nt(og_ref[i], rows_of(wd_ref))
        dgu_ref[here, :ff] = (dh * up * (s * (1.0 + gate * (1.0 - s)))).astype(BF)
        dgu_ref[here, ff:] = (dh * silu).astype(BF)
        dnm_ref[i] = dot_nt(dgu_ref[here, :], rows_of(wgu_ref)).astype(BF)
        out_ref[i] = dot(hidden, rows_of(wd_ref)).astype(BF)


def weight_grad(out_ref, left_ref, right, chunk=256):
    size = math.prod(out_ref.shape[1:-1])
    width = out_ref.shape[-1]

    @pl.loop(0, left_ref.shape[-1] // chunk)
    def _(i):
        left = left_ref[..., lanes(i, chunk)].reshape(-1, chunk)
        g = dot_tn(left, rows_of(right)).astype(BF)
        for j in range(chunk // size):
            out_ref[i * (chunk // size) + j] = g[j * size : (j + 1) * size].reshape(out_ref.shape[1:-1] + (width,))


MESH = pl.DeviceIdType.MESH


def rcopy(src, dst, send, recv, **device):
    return pltpu.make_async_remote_copy(
        src_ref=src, dst_ref=dst, send_sem=send, recv_sem=recv, device_id=device, device_id_type=MESH
    )


class Place:
    def __init__(self, n):
        self.n, self.line = n, n // 2
        self.dp, self.ctx = lax.axis_index("dp"), lax.axis_index("ctx")
        self.outer, self.inner = self.dp // 2, self.dp % 2
        self.dp_inner = self.outer * 2 + 1 - self.inner
        self.dp_up, self.dp_down = self.dp + 2, self.dp - 2
        self.has_up, self.has_down = self.outer < self.line - 1, self.outer > 0
        core = self.ctx % 2
        self.c_core = self.ctx + 1 - 2 * core
        self.c_x = (self.ctx + 2) % 4
        self.c_far = 3 - self.ctx
        mine = self.dp * 4 + self.ctx
        self.slab_to = {"dp": mine % n, "ctx": mine // n}
        source = self.ctx * n + self.dp
        self.slab_from = {"dp": source // 4, "ctx": source % 4}
        self.slab_stays = source == mine


def greet(place, slabs):
    barrier = pltpu.get_barrier_semaphore()

    def signal(**device):
        pl.semaphore_signal(barrier, inc=1, device_id=device, device_id_type=MESH)

    for c in (place.c_core, place.c_x, place.c_far):
        signal(ctx=c)
    for k in range(1, place.n):
        signal(dp=(place.dp + k) % place.n)
    count = place.n + 2
    for slab in slabs:

        @pl.when(jnp.logical_not(place.slab_stays))
        def _():
            signal(**slab)

        count = count + jnp.where(place.slab_stays, 0, 1)
    return barrier, count


class Gather:
    def __init__(self, place, bufs, sems):
        self.at, self.bufs, self.sems = place, bufs, sems

    @staticmethod
    def scratch(n, bufs):
        return pltpu.SemaphoreType.DMA((5, bufs, n // 2))

    def copy(self, b, p, way):
        at = self.at
        block = self.bufs[b].at[p * 2 + at.inner]
        device = (at.dp_up, at.dp_down, at.dp_inner)[way]
        recv = self.sems.at[4 if way == 2 else 3, b, p]
        return rcopy(block, block, self.sems.at[way, b, p], recv, dp=device)

    def send(self, p, up, down, inner=True):
        at = self.at
        for b in range(len(self.bufs)):
            if up:

                @pl.when(at.has_up)
                def _():
                    self.copy(b, p, 0).start()

            if down:

                @pl.when(at.has_down)
                def _():
                    self.copy(b, p, 1).start()

            if inner:
                self.copy(b, p, 2).start()

    def start(self):
        self.send(self.at.outer, True, True)

    def start_inner(self):
        self.send(self.at.outer, False, False)

    def start_line(self):
        self.send(self.at.outer, True, True, False)

    def step(self, t):
        at = self.at
        for p, there, up in ((at.outer - t, at.outer >= t, True), (at.outer + t, at.outer + t < at.line, False)):

            @pl.when(there)
            def _():
                for b in range(len(self.bufs)):
                    self.copy(b, p, 0).wait_recv()
                self.send(p, up, not up)

    def arrive(self):
        at = self.at
        for b in range(len(self.bufs)):
            for p in range(at.line):
                block = self.bufs[b].at[p * 2 + 1 - at.inner]
                rcopy(block, block, self.sems.at[2, b, p], self.sems.at[4, b, p], dp=at.dp_inner).wait_recv()

    def finish(self):
        at = self.at
        for b in range(len(self.bufs)):
            for p in range(at.line):
                self.copy(b, p, 2).wait_send()

                @pl.when(jnp.logical_and(at.has_up, p <= at.outer))
                def _():
                    self.copy(b, p, 0).wait_send()

                @pl.when(jnp.logical_and(at.has_down, p >= at.outer))
                def _():
                    self.copy(b, p, 1).wait_send()


class Reduce:
    def __init__(self, place, parts, from_inner, from_line, sems):
        self.at, self.parts, self.from_inner, self.from_line, self.sems = place, parts, from_inner, from_line, sems

    @staticmethod
    def scratch(n, blocks):
        line = n // 2
        return (
            [pltpu.VMEM((line, *dims), dtype) for dims, dtype in blocks],
            [pltpu.VMEM((line + 1, *dims), dtype) for dims, dtype in blocks],
            pltpu.SemaphoreType.DMA((4, len(blocks), line + 1)),
        )

    def inner_copy(self, b, p):
        at = self.at
        return rcopy(
            self.parts[b].at[p * 2 + 1 - at.inner], self.from_inner[b].at[p],
            self.sems.at[0, b, p], self.sems.at[1, b, p], dp=at.dp_inner,
        )

    def line_copy(self, b, p, slot, up):
        at = self.at
        return rcopy(
            self.from_inner[b].at[p], self.from_line[b].at[slot],
            self.sems.at[2, b, p], self.sems.at[3, b, slot], dp=at.dp_up if up else at.dp_down,
        )

    def start(self, which):
        at = self.at
        for d in range(at.line - 1, -1, -1):
            for p, there in ((at.outer + d, at.outer + d < at.line), (at.outer - d, at.outer >= d))[: 2 if d else 1]:

                @pl.when(there)
                def _():
                    for b in which:
                        self.inner_copy(b, p).start()

    def total(self, b, p, slots):
        s = self.parts[b][p * 2 + self.at.inner].astype(F32) + self.from_inner[b][p].astype(F32)
        for slot in slots:
            s = s + self.from_line[b][slot].astype(F32)
        return s

    def step(self, d, which):
        at = self.at
        for p, there, more, up in (
            (at.outer + d, at.outer + d < at.line, at.has_down, True),
            (at.outer - d, at.outer >= d, at.has_up, False),
        ):
            for b in which:

                @pl.when(there)
                def _():
                    self.inner_copy(b, p).wait_recv()
                    into = self.from_inner[b].at[p]

                    @pl.when(more)
                    def _():
                        self.line_copy(b, p, p, up).wait_recv()
                        into[...] = self.total(b, p, [p]).astype(into.dtype)

                    @pl.when(jnp.logical_not(more))
                    def _():
                        into[...] = self.total(b, p, []).astype(into.dtype)

                    slot = p if up or d > 1 else at.line
                    self.line_copy(b, p, slot, up).start()

    def result(self, b, store):
        at = self.at
        p = at.outer
        self.inner_copy(b, p).wait_recv()
        lo, hi = at.has_down, at.has_up

        @pl.when(lo)
        def _():
            self.line_copy(b, p, p, True).wait_recv()

        @pl.when(hi)
        def _():
            self.line_copy(b, p, at.line, False).wait_recv()

        @pl.when(jnp.logical_and(lo, hi))
        def _():
            store(self.total(b, p, [p, at.line]))

        @pl.when(jnp.logical_and(lo, jnp.logical_not(hi)))
        def _():
            store(self.total(b, p, [p]))

        @pl.when(jnp.logical_and(hi, jnp.logical_not(lo)))
        def _():
            store(self.total(b, p, [at.line]))

    def finish(self):
        at = self.at
        for b in range(len(self.parts)):
            for p in range(at.line):
                self.inner_copy(b, p).wait_send()

                @pl.when(p != at.outer)
                def _():
                    self.line_copy(b, p, p, True).wait_send()


class CtxGather:
    def __init__(self, place, buf, sems):
        self.at, self.buf, self.sems = place, buf, sems

    def copy(self, k, owner):
        block = self.buf.at[owner]
        ctx = self.at.c_x if k == 1 else self.at.c_core
        return rcopy(block, block, self.sems.at[0, k], self.sems.at[1, k], ctx=ctx)

    def start(self):
        self.copy(1, self.at.ctx).start()
        self.copy(0, self.at.ctx).start()

    def forward(self):
        self.copy(1, self.at.c_x).wait_recv()
        self.copy(2, self.at.c_x).start()

    def arrive(self):
        self.copy(0, self.at.c_core).wait_recv()
        self.copy(2, self.at.c_far).wait_recv()

    def finish(self):
        for k in range(3):
            self.copy(k, self.at.ctx).wait_send()


class CtxReduce:
    def __init__(self, place, part, got, sems):
        self.at, self.part, self.got, self.sems = place, part, got, sems

    def copy(self, k):
        at = self.at
        block = self.got.at[1] if k == 2 else self.part.at[(at.c_core, at.c_far)[k]]
        return rcopy(block, self.got.at[k], self.sems.at[0, k], self.sems.at[1, k], ctx=at.c_x if k == 2 else at.c_core)

    def start(self):
        self.copy(1).start()
        self.copy(0).start()

    def across(self):
        self.copy(1).wait_recv()
        into = self.got.at[1]
        into[...] = (self.part[self.at.c_x].astype(F32) + into[...].astype(F32)).astype(into.dtype)
        self.copy(2).start()

    def result(self):
        self.copy(0).wait_recv()
        self.copy(2).wait_recv()
        return self.part[self.at.ctx].astype(F32) + self.got[0].astype(F32) + self.got[2].astype(F32)

    def finish(self):
        for k in range(3):
            self.copy(k).wait_send()


class Quarters:
    def __init__(self, place, src, dst, sems):
        self.at, self.src, self.dst, self.sems = place, src, dst, sems

    def copies(self):
        at = self.at
        return [
            rcopy(self.src.at[c], self.dst.at[at.ctx], self.sems.at[0, k], self.sems.at[1, k], ctx=c)
            for k, c in enumerate((at.c_x, at.c_far, at.c_core))
        ]

    def start(self):
        for c in self.copies():
            c.start()
        self.dst[self.at.ctx] = self.src[self.at.ctx]

    def finish(self):
        for c in self.copies():
            c.wait()


class Slab:
    def __init__(self, place, src, dst, sems, to):
        self.at, self.src, self.dst, self.sems, self.to = place, src, dst, sems, to

    def copy(self):
        return rcopy(self.src, self.dst, self.sems.at[0, 0], self.sems.at[1, 0], **self.to)

    def start(self):
        @pl.when(self.at.slab_stays)
        def _():
            self.dst[...] = self.src[...]

        @pl.when(jnp.logical_not(self.at.slab_stays))
        def _():
            self.copy().start()

    def finish(self):
        @pl.when(jnp.logical_not(self.at.slab_stays))
        def _():
            self.copy().wait()


class Exchange:
    def __init__(self, place, src, dst, cap, sems):
        self.at, self.src, self.dst, self.cap, self.sems = place, src, dst, cap, sems

    def rows(self, ref, j):
        if len(ref.shape) == 3:
            size = ref.shape[1]
            start = j * self.cap
            return ref.at[start // size, pl.ds(pl.multiple_of(start % size, self.cap), self.cap)]
        return ref.at[pl.ds(pl.multiple_of(j * self.cap, self.cap), self.cap)]

    def copy(self, k):
        at = self.at
        to = (at.dp + k) % at.n
        return rcopy(self.rows(self.src, to), self.rows(self.dst, at.dp), self.sems.at[0, k], self.sems.at[1, k], dp=to)

    def start(self):
        for k in range(1, self.at.n):
            self.copy(k).start()
        self.rows(self.dst, self.at.dp)[...] = self.rows(self.src, self.at.dp)[...]

    def finish(self):
        for k in range(1, self.at.n):
            self.copy(k).wait()


def sem_pairs(count):
    return pltpu.SemaphoreType.DMA((2, count))


def norm_back(c, v, gain):
    r = lax.rsqrt(jnp.mean(v * v, axis=-1, keepdims=True) + EPS)
    nv = v * r
    cg = c * gain
    return jnp.sum(c * nv, axis=0, keepdims=True), r * (cg - nv * jnp.mean(cg * nv, axis=-1, keepdims=True))


def into(ref):
    def store(v):
        ref[...] = v.astype(ref.dtype)

    return store


def quarter_columns(dst_ref, weights):
    for c in range(4):
        start = 0
        for w in weights:
            size = w.shape[1] // 4
            dst_ref[c, :, start : start + size] = w[:, c * size : (c + 1) * size]
            start += size


def unit_columns(n, dst_ref, weights):
    size = weights[0].shape[1] // (4 * n)
    for c in range(4):
        for k, w in enumerate(weights):
            for d in range(n):
                start = (k * n + d) * size
                dst_ref[c, :, start : start + size] = w[:, (d * 4 + c) * size : (d * 4 + c + 1) * size]


def route(n, cap, dest_ref, place_ref, labs_ref):
    tok = dest_ref.shape[1]
    dest = dest_ref[...]
    owner = jnp.right_shift(dest, (4 * tok).bit_length() - 1)
    slot = jnp.bitwise_and(dest, tok - 1)
    lines = lax.broadcasted_iota(jnp.int32, (n, tok), 0)
    hot = (lines == owner).astype(F32)
    before = lax.broadcasted_iota(jnp.int32, (tok, tok), 0) < lax.broadcasted_iota(jnp.int32, (tok, tok), 1)
    rank = dot(hot.astype(BF), before.astype(BF))
    send = jnp.sum(hot * (rank + (lines * cap).astype(F32)), axis=0, keepdims=True).astype(jnp.int32)
    place = (lax.broadcasted_iota(jnp.int32, (n * cap, tok), 0) == send).astype(BF)
    place_ref[...] = place
    labels = dot_nt(jnp.broadcast_to((slot + 1).astype(F32), (8, tok)).astype(BF), place)
    labs_ref[...] = jnp.zeros_like(labs_ref)
    for j in range(n):
        labs_ref[j * 8 : j * 8 + 8, :cap] = labels[:, j * cap : (j + 1) * cap]


def gain_tile(at, raw_ref, counts):
    index = at.dp * 4 + at.ctx
    raw = jnp.broadcast_to(raw_ref[...], (8, 128)).astype(BF)
    source = lax.broadcasted_iota(jnp.int32, (128, 128), 0)
    target = lax.broadcasted_iota(jnp.int32, (128, 128), 1)
    lines = lax.broadcasted_iota(jnp.int32, (8, 128), 0)
    total, start = jnp.zeros((8, 128), F32), 0
    for k, count in enumerate(counts):
        move = (target - (index * count) % 128 == source - start) & (source >= start) & (source < start + count)
        total = total + jnp.where(lines == k, dot(raw, move.astype(BF)), 0.0)
        start += count
    return total


def final_body(counts, ig, layer, qkv, o, gu, gd, small, layer_out, ig_out, ga, gq, gk, gv, gqg, gkg, go, gm, gg, gup, gdn):
    index = lax.axis_index("dp") * 4 + lax.axis_index("ctx")
    layer_out[...] = layer[...]
    ig_out[...] = ig[...]
    for c in range(4):
        start = 0
        for out in (gq, gk, gv):
            size = out.shape[1] // 4
            out[:, c * size : (c + 1) * size] = qkv[c, :, start : start + size].astype(F32)
            start += size
        size = gdn.shape[0]
        n = gg.shape[1] // (4 * size)
        for k, out in enumerate((gg, gup)):
            for d in range(n):
                start = (k * n + d) * size
                out[:, (d * 4 + c) * size : (d * 4 + c + 1) * size] = gu[c, :, start : start + size].astype(F32)
    go[...] = o[...].astype(F32)
    gdn[...] = gd[...].astype(F32)
    for k, (out, count) in enumerate(zip((ga, gm, gqg, gkg), counts)):
        row = pltpu.roll(small[...], (128 - (index * count) % 128) % 128, 1)
        out[...] = row[k : k + 1, :count]


def layer_body(
    n, cap, counts,
    in_ref, dest_ref, doc_ref, raw_ref, og_ref, wq_src, wk_src, wv_src, wo_src, wg_src, wu_src, wd_src, cos_ref, sin_ref,
    ig_ref, layer_ref, qkv_out, o_out, gu_out, gd_out, gain_out,
    wqkv_ref, wo_ref, wgu_ref, wd_ref, og_all, x_own, pick_ref, ga_ref, gm_ref, q_ref, k_ref, v_ref, p_ref, xn_ref, att_ref, nm_ref, mid_ref,
    recv, labels, gains_c, gains_n, x_ref, part_ref, got, mask_ref,
    hid_ref, dgu_ref, outp_ref, got_d, got_o, dmid_ref, dq_ref, dk_ref, dv_ref, ggq_ref, ggk_ref, ggm_ref, gains, recv_back,
    yi0, yi1, ln0, ln1, s_ra, yo, lo, s_rb, yq, yg, lq, lg, s_rc,
    gain_sum, gain_all, qkv_ref, gu_ref, place_ref, lab_ref,
    s_ga, s_gb, s_gc, s_gd4, s_rows, s_labs, s_qkv, s_gu, s_wo, s_gain, s_x, s_og, s_red, s_nm,
    s_dnm, s_out, s_db, s_dxn, s_rows_back, s_gu_back, s_qkv_back, s_o, s_gain_back,
):
    at = Place(n)
    barrier, count = greet(at, (at.slab_from, at.slab_to))
    quarter_columns(qkv_ref, (wq_src, wk_src, wv_src))
    gains_c[at.ctx] = gain_tile(at, raw_ref, counts)
    route(n, cap, dest_ref, place_ref, lab_ref)
    tok = in_ref.shape[0]
    for half in range(n * cap // tok):
        part_ref[half] = dot(place_ref[half * tok : (half + 1) * tok, :], in_ref[...]).astype(BF)
    pl.semaphore_wait(barrier, count)
    qkv = Quarters(at, qkv_ref, wqkv_ref.at[at.dp], s_qkv)
    rows = Exchange(at, part_ref, recv, cap, s_rows)
    labs = Exchange(at, lab_ref, labels, 8, s_labs)
    qkv.start()
    gain_copies = [
        rcopy(gains_c.at[at.ctx], gains_c.at[at.ctx], s_gain.at[0, k], s_gain.at[1, k], ctx=c)
        for k, c in enumerate((at.c_x, at.c_far, at.c_core))
    ]
    for g in gain_copies:
        g.start()
    unit_columns(n, gu_ref, (wg_src, wu_src))
    wo = Slab(at, wo_src, wo_ref.at[at.slab_to["dp"]], s_wo, at.slab_to)
    wd_ref[at.dp] = wd_src[...]
    gu = Quarters(at, gu_ref, wgu_ref.at[at.dp], s_gu)
    labs.start()
    rows.start()
    gu.start()
    wo.start()
    for g in gain_copies:
        g.wait()
    gains_n[at.dp] = gains_c[0] + gains_c[1] + gains_c[2] + gains_c[3]
    qkv.finish()
    first = Gather(at, [wqkv_ref, gains_n], s_ga)
    first.start()
    og_all[at.ctx] = og_ref[...]
    og = CtxGather(at, og_all, s_og)
    gu.finish()
    og.start()
    third = Gather(at, [wgu_ref], s_gc)
    third.start_inner()
    labs.finish()
    slots = lax.broadcasted_iota(jnp.int32, (tok, cap), 0).astype(F32) + 1.0
    for j in range(n):
        pick_ref[:, j * cap : (j + 1) * cap] = (slots == labels[j * 8 : j * 8 + 1, :cap]).astype(BF)
    first.step(1)
    rows.finish()
    owned = dot(pick_ref[...], recv[...]).astype(BF)
    x_ref[at.ctx] = owned
    x_own[...] = owned
    x = CtxGather(at, x_ref, s_x)
    x.start()
    first.step(2)
    third.start_line()
    wo.finish()
    second = Gather(at, [wo_ref], s_gb)
    second.start()
    for t in range(3, at.line):
        first.step(t)
    second.step(1)
    og.forward()
    x.forward()
    first.arrive()
    own = 4 * ga_ref.shape[1] // (4 * n)
    ga_ref[...] = jnp.zeros_like(ga_ref)
    gm_ref[...] = jnp.zeros_like(gm_ref)
    gqk = jnp.zeros((8, 128), F32)
    for d in range(n):
        tile = slice(d * own // 128 * 128, d * own // 128 * 128 + 128)
        block = gains_n[d]
        ga_ref[0:1, tile] += block[0:1]
        gm_ref[0:1, tile] += block[1:2]
        gqk = gqk + block
    off = jnp.where(doc_ref[0:1, 0:1] > 0, 0.0, MASKED).astype(F32)
    mask_ref[...] = mask_block(off)
    x.arrive()
    second.step(2)
    attn_project(x_ref, wqkv_ref, ga_ref, gqk[2:3], gqk[3:4], cos_ref, sin_ref, q_ref, k_ref, v_ref, p_ref, xn_ref)
    for t in range(3, at.line):
        second.step(t)
    third.step(1)
    fourth = Gather(at, [wd_ref], s_gd4)
    fourth.start()
    nk = k_ref.shape[1] // HD

    @pl.loop(0, nk)
    def _(g):
        attn_group(g, off, q_ref, k_ref, v_ref, att_ref, mask_ref)

    third.step(2)
    fourth.step(1)
    second.arrive()

    @pl.loop(0, 4)
    def _(i):
        part_ref[i] = dot(att_ref[lanes(i, tok), :], rows_of(wo_ref)).astype(BF)

    red = CtxReduce(at, part_ref, got, s_red)
    red.start()
    red.across()
    for t in range(3, at.line):
        third.step(t)
        fourth.step(t - 1)
    middle = x_own[...].astype(F32) + red.result()
    mid_ref[...] = middle
    r = lax.rsqrt(jnp.mean(middle * middle, axis=-1, keepdims=True) + EPS)
    nm_ref[at.ctx] = (middle * r * gm_ref[0:1, :]).astype(BF)
    nm = CtxGather(at, nm_ref, s_nm)
    nm.start()
    fourth.step(at.line - 1)
    nm.forward()
    nm.arrive()
    og.arrive()
    third.arrive()
    fourth.arrive()
    for part in (first, second, third, fourth, og, x, nm, red):
        part.finish()
    feed_forward(nm_ref, og_all, wgu_ref, wd_ref, hid_ref, dgu_ref, outp_ref, part_ref)
    db_ref, da_ref, dp_ref = x_ref, hid_ref.at[:, : q_ref.shape[1]], dgu_ref.at[:, : wqkv_ref.shape[-1]]
    last = at.line - 1
    dnm = CtxReduce(at, part_ref, got_d, s_dnm)
    dnm.start()
    weight_grad(wd_ref, hid_ref, og_all, 384)
    first = Reduce(at, [wgu_ref, wd_ref], [yi0, yi1], [ln0, ln1], s_ra)
    first.start([1])
    dnm.across()
    weight_grad(wgu_ref, nm_ref, dgu_ref)
    first.start([0])
    out = CtxReduce(at, outp_ref, got_o, s_out)
    dk_ref[...] = jnp.zeros_like(dk_ref)
    dv_ref[...] = jnp.zeros_like(dv_ref)
    first.step(last, [1])
    gg, d = norm_back(dnm.result(), mid_ref[...], gm_ref[0:1, :])
    ggm_ref[...] = gg
    d = d + og_ref[...].astype(F32)
    dmid_ref[...] = d
    db_ref[at.ctx] = d.astype(BF)
    db = CtxGather(at, db_ref, s_db)
    db.start()
    out.start()
    for t in range(last - 1, 0, -1):
        first.step(t, [1])
    db.forward()
    out.across()
    db.arrive()
    tok = db_ref.shape[1]

    @pl.loop(0, 4)
    def _(i):
        da_ref[lanes(i, tok), :] = dot_nt(db_ref[i], rows_of(wo_ref)).astype(BF)

    first.step(last, [0])
    for g in range(k_ref.shape[1] // HD):
        for i in range(q_ref.shape[0] // QB):
            attn_group_back(g, i, off, q_ref, k_ref, v_ref, att_ref, da_ref, dq_ref, dk_ref, dv_ref, mask_ref)
        if g == 0:
            for t in range(last - 1, 1, -1):
                first.step(t, [0])
    dxn_ref = nm_ref
    attn_unproject(gqk[2:3], gqk[3:4], cos_ref, sin_ref, p_ref, dq_ref, dk_ref, dv_ref, dp_ref, wqkv_ref, dxn_ref, ggq_ref, ggk_ref)
    dxn = CtxReduce(at, dxn_ref, got, s_dxn)
    dxn.start()
    first.step(1, [0])
    weight_grad(wqkv_ref, xn_ref, dp_ref)
    third = Reduce(at, [wqkv_ref, gains], [yq, yg], [lq, lg], s_rc)
    third.start([0])
    dxn.across()
    weight_grad(wo_ref, att_ref, db_ref)
    second = Reduce(at, [wo_ref], [yo], [lo], s_rb)
    second.start([0])
    first.result(1, into(gd_out))
    first.result(0, into(yi0.at[at.outer]))
    gu = Quarters(at, yi0.at[at.outer], gu_out, s_gu_back)
    gu.start()
    third.step(last, [0])
    gg, d = norm_back(dxn.result(), x_own[...].astype(F32), ga_ref[0:1, :])
    owned = (dmid_ref[...] + d).astype(BF)
    recv[...] = dot_tn(pick_ref[...], owned).astype(BF)
    rows = Exchange(at, recv, recv_back, cap, s_rows_back)
    rows.start()
    own = 4 * gg.shape[1] // (4 * n)
    lines = lax.broadcasted_iota(jnp.int32, (8, 128), 0)
    for j in range(n):
        tile = slice(j * own // 128 * 128, j * own // 128 * 128 + 128)
        gains[j] = (
            jnp.where(lines == 0, gg[:, tile], 0.0) + jnp.where(lines == 1, ggm_ref[0:1, tile], 0.0)
            + jnp.where(lines == 2, ggq_ref[0:1, :], 0.0) + jnp.where(lines == 3, ggk_ref[0:1, :], 0.0)
        )
    third.start([1])
    second.step(last, [0])
    for t in range(last - 1, 0, -1):
        third.step(t, [0])
        second.step(t, [0])
    layer_ref[...] = (mid_ref[...] + out.result()).astype(BF)
    for t in range(last, 0, -1):
        third.step(t, [1])
    second.result(0, into(yo.at[at.outer]))
    o = Slab(at, yo.at[at.outer], o_out, s_o, at.slab_from)
    o.start()
    third.result(0, into(yq.at[at.outer]))
    qkv = Quarters(at, yq.at[at.outer], qkv_out, s_qkv_back)
    qkv.start()
    third.result(1, into(gain_sum))
    small = [
        rcopy(gain_sum, gain_all.at[at.ctx], s_gain_back.at[0, k], s_gain_back.at[1, k], ctx=c)
        for k, c in enumerate((at.c_x, at.c_far, at.c_core))
    ]
    for g in small:
        g.start()
    gain_all[at.ctx] = gain_sum[...]
    rows.finish()
    ig_ref[...] = dot_tn(place_ref[...], recv_back[...]).astype(BF)
    for g in small:
        g.wait()
    gain_out[...] = gain_all[0] + gain_all[1] + gain_all[2] + gain_all[3]
    for part in (qkv, o, gu, dxn, db, out, dnm, first, second, third):
        part.finish()


def shape(*dims, dtype=BF):
    return jax.ShapeDtypeStruct(dims, dtype)


def linked(body, outs, scratch, name, number):
    return pl.pallas_call(
        body,
        out_shape=outs,
        scratch_shapes=scratch,
        compiler_params=pltpu.CompilerParams(vmem_limit_bytes=VMEM_LIMIT, collective_id=number, has_side_effects=True),
        name=name,
    )


def local(
    layer_input, dest_slot, doc_len, out_grad, attn_gain, w_query, w_key, w_value, q_gain, k_gain,
    w_out, mlp_gain, w_gate, w_up, w_down,
):
    tok, width = layer_input.shape
    n = lax.axis_size("dp")
    cap = 2 * tok // n
    rows = 4 * tok
    slabs = n * cap
    rq, ro, rd = w_query.shape[0], w_out.shape[0], w_down.shape[0]
    ff = rd * n
    counts = (attn_gain.shape[0], mlp_gain.shape[0], q_gain.shape[0], k_gain.shape[0])
    raw = jnp.pad(jnp.concatenate([attn_gain, mlp_gain, q_gain, k_gain]), (0, 128 - sum(counts))).astype(F32).reshape(1, 128)
    fw = 2 * ff
    cos, sin = rope_tables(rows)
    blocks = ([((4, rq, fw), BF), ((rd, width), BF)], [((ro, width), BF)], [((4, rq, 1024), BF), ((8, 128), F32)])
    reduces = []
    for red, lines, sems in (Reduce.scratch(n, b) for b in blocks):
        reduces += [*red, *lines, sems]
    vm = pltpu.VMEM
    group = (4, tok, width)
    input_grad, layer_output, g_qkv, g_o, g_gu, g_d, small = linked(
        functools.partial(layer_body, n, cap, counts),
        (shape(tok, width), shape(tok, width), shape(4, rq, 1024), shape(ro, width), shape(4, rq, fw), shape(rd, width), shape(8, 128, dtype=F32)),
        [vm((n, 4, rq, 1024), BF), vm((n, ro, width), BF), vm((n, 4, rq, fw), BF), vm((n, rd, width), BF), vm(group, BF), vm((tok, width), BF),
         vm((tok, slabs), BF), vm((8, width), F32), vm((8, width), F32), vm((rows, 512), BF), vm((rows, 256), BF), vm((rows, 256), BF),
         vm((rows, 768), BF), vm((rows, width), BF), vm((rows, 512), BF), vm(group, BF), vm((tok, width), F32),
         vm((slabs, width), BF), vm((n * 8, 128), F32), vm((4, 8, 128), F32), vm((n, 8, 128), F32),
         vm(group, BF), vm(group, BF), vm((3, tok, width), BF), vm((QB, QB), F32),
         vm((rows, ff), BF), vm((rows, fw), BF), vm(group, BF), vm((3, tok, width), BF), vm((3, tok, width), BF),
         vm((tok, width), F32), vm((rows, 512), F32), vm((rows, 256), F32), vm((rows, 256), F32),
         vm((8, HD), F32), vm((8, HD), F32), vm((1, width), F32), vm((n, 8, 128), F32), vm((slabs, width), BF),
         *reduces,
         vm((8, 128), F32), vm((4, 8, 128), F32), vm((4, rq, 1024), BF), vm((4, rq, fw), BF), vm((slabs, tok), BF), vm((n * 8, 128), F32),
         Gather.scratch(n, 2), Gather.scratch(n, 1), Gather.scratch(n, 1), Gather.scratch(n, 1), sem_pairs(n), sem_pairs(n), sem_pairs(3), sem_pairs(3),
         sem_pairs(1), sem_pairs(3), sem_pairs(3), sem_pairs(3), sem_pairs(3), sem_pairs(3),
         sem_pairs(3), sem_pairs(3), sem_pairs(3), sem_pairs(3), sem_pairs(n), sem_pairs(3), sem_pairs(3), sem_pairs(1), sem_pairs(3)],
        "layer", 0,
    )(layer_input, dest_slot.reshape(1, tok), doc_len, raw, out_grad, w_query, w_key, w_value, w_out, w_gate, w_up, w_down, cos, sin)
    grads = [shape(*w.shape, dtype=F32) for w in (w_query, w_key, w_value, w_out, w_gate, w_up, w_down)]
    gains = [shape(1, c, dtype=F32) for c in counts]
    outs = (shape(tok, width), shape(tok, width), gains[0], *grads[:3], gains[2], gains[3], grads[3], gains[1], *grads[4:])
    outs = pl.pallas_call(functools.partial(final_body, counts), out_shape=outs, name="final")(
        input_grad, layer_output, g_qkv, g_o, g_gu, g_d, small
    )
    return tuple(o.reshape(-1) if o.shape[0] == 1 else o for o in outs)


def solution(mesh):
    rows = P(BOTH, None)
    vec = P(BOTH)
    return jax.shard_map(
        local,
        mesh=mesh,
        in_specs=(rows, vec, P("dp", None), rows, vec, rows, rows, rows, vec, vec, rows, vec, rows, rows, rows),
        out_specs=(rows, rows, vec, rows, rows, rows, vec, vec, rows, vec, rows, rows, rows),
        check_vma=False,
    )
```

```python
import functools
import math

import jax
import jax.numpy as jnp
import numpy as np
from jax import lax
from jax.experimental import pallas as pl
from jax.experimental.pallas import tpu as pltpu
from jax.sharding import PartitionSpec as P

H = 16
KVH = 8
HD = 128
EPS = 1e-06
THETA = 1000000.0
MASKED = -1e30
QB = 128
SCALE = HD ** (-0.5)
LOG2E = math.log2(math.e)
BF = jnp.bfloat16
F32 = jnp.float32
BOTH = ("dp", "ctx")
VMEM_LIMIT = 63 << 20


def dot(a, b):
    return lax.dot_general(a, b, (((1,), (0,)), ((), ())), preferred_element_type=F32)


def dot_nt(a, b):
    return lax.dot_general(a, b, (((1,), (1,)), ((), ())), preferred_element_type=F32)


def dot_tn(a, b):
    return lax.dot_general(a, b, (((0,), (0,)), ((), ())), preferred_element_type=F32)


def lanes(start, size):
    return pl.ds(pl.multiple_of(start * size, size), size)


def rope_tables(rows):
    inverse = np.exp(np.arange(HD // 2, dtype=np.float32) * np.float32(-2.0 / HD * math.log(THETA)))
    doubled = np.concatenate([inverse, inverse]).astype(np.float32)
    angles = np.arange(rows, dtype=np.float32)[:, None] * doubled[None, :]
    sign = np.where(np.arange(HD) < HD // 2, -1.0, 1.0).astype(np.float32)
    return np.cos(angles), np.sin(angles) * sign[None, :]


def mask_block(off_bias):
    rows = lax.broadcasted_iota(jnp.int32, (QB, QB), 0)
    cols = lax.broadcasted_iota(jnp.int32, (QB, QB), 1)
    return jnp.where(rows == cols, 0.0, jnp.where(cols < rows, off_bias, MASKED))


def lane_mean(v):
    ones = jnp.full((HD, HD), 1.0 / HD, BF)
    high = v.astype(BF)
    return dot(high, ones) + dot((v - high.astype(F32)).astype(BF), ones)


def rows_of(ref):
    value = ref[...]
    return value.reshape(-1, value.shape[-1])


def attn_project(x_ref, w, ga, gq, gk, cos_ref, sin_ref, q_ref, k_ref, v_ref, p_ref, xn_ref):
    rows = xn_ref.shape[0]
    tok = x_ref.shape[1]
    nq = q_ref.shape[1] // HD
    nk = k_ref.shape[1] // HD

    @pl.loop(0, rows // tok)
    def _(i):
        here = lanes(i, tok)
        x = x_ref[i].astype(F32)
        r = lax.rsqrt(jnp.mean(x * x, axis=-1, keepdims=True) + EPS)
        xn = (x * r * ga[0:1, :]).astype(BF)
        xn_ref[here, :] = xn
        p = dot(xn, rows_of(w))
        p_ref[here, :] = p[:, : (nq + nk) * HD].astype(BF)
        v_ref[here, :] = p[:, (nq + nk) * HD :].astype(BF)
        cos = cos_ref[here, :]
        sin = sin_ref[here, :]
        for h in range(nq + nk):
            ph = p[:, h * HD : (h + 1) * HD]
            g = gq if h < nq else gk
            nv = ph * lax.rsqrt(lane_mean(ph * ph) + EPS) * g
            rot = (nv * cos + pltpu.roll(nv, HD // 2, 1) * sin).astype(BF)
            if h < nq:
                q_ref[here, h * HD : (h + 1) * HD] = rot
            else:
                k_ref[here, (h - nq) * HD : (h - nq + 1) * HD] = rot


def group_rows(ref, here, g, group):
    return jnp.concatenate([ref[here, lanes(g * group + a, HD)] for a in range(group)], axis=0)


def attn_probs(q, k, off, mask_ref, group):
    s = dot_nt(q, k) * (SCALE * LOG2E)
    cut = s.shape[1] - QB
    last = jnp.exp2(s[:, cut:] + jnp.concatenate([mask_ref[...]] * group, axis=0))
    e = last if cut == 0 else jnp.concatenate([jnp.exp2(s[:, :cut] + off), last], axis=1)
    return e * (1.0 / jnp.sum(e, axis=-1, keepdims=True))


def attn_group(g, off, q_ref, k_ref, v_ref, att_ref, mask_ref):
    group = q_ref.shape[1] // k_ref.shape[1]
    hk = lanes(g, HD)
    for i in range(q_ref.shape[0] // QB):
        here, keys = slice(i * QB, (i + 1) * QB), slice(0, (i + 1) * QB)
        probs = attn_probs(group_rows(q_ref, here, g, group), k_ref[keys, hk], off, mask_ref, group)
        o = dot(probs.astype(BF), v_ref[keys, hk]).astype(BF)
        for a in range(group):
            att_ref[here, lanes(g * group + a, HD)] = o[a * QB : (a + 1) * QB]


def attn_group_back(g, i, off, q_ref, k_ref, v_ref, att_ref, da_ref, dq_ref, dk_ref, dv_ref, mask_ref):
    group = q_ref.shape[1] // k_ref.shape[1]
    hk = lanes(g, HD)
    here, keys = slice(i * QB, (i + 1) * QB), slice(0, (i + 1) * QB)
    q, da, att = (group_rows(ref, here, g, group) for ref in (q_ref, da_ref, att_ref))
    inner = jnp.sum(da.astype(F32) * att.astype(F32), axis=-1, keepdims=True)
    probs = attn_probs(q, k_ref[keys, hk], off, mask_ref, group)
    ds = (probs * (dot_nt(da, v_ref[keys, hk]) - inner)).astype(BF)
    dq = dot(ds, k_ref[keys, hk])
    for a in range(group):
        dq_ref[here, lanes(g * group + a, HD)] = dq[a * QB : (a + 1) * QB]
    dk_ref[keys, hk] += dot_tn(ds, q)
    dv_ref[keys, hk] += dot_tn(probs.astype(BF), da)


def attn_unproject(gq, gk, cos_ref, sin_ref, p_ref, dq_ref, dk_ref, dv_ref, dp_ref, w, dxn_ref, ggq_ref, ggk_ref):
    rows = p_ref.shape[0]
    tok = dxn_ref.shape[1]
    nq = dq_ref.shape[1] // HD
    nk = dk_ref.shape[1] // HD
    ggq_ref[...] = jnp.zeros_like(ggq_ref)
    ggk_ref[...] = jnp.zeros_like(ggk_ref)

    @pl.loop(0, rows // tok)
    def _(i):
        here = lanes(i, tok)
        cos = cos_ref[here, :]
        sin = sin_ref[here, :]
        sums = [jnp.zeros((1, HD), F32), jnp.zeros((1, HD), F32)]
        for h in range(nq + nk):
            which = 0 if h < nq else 1
            g = gq if h < nq else gk
            cols = slice(h * HD, (h + 1) * HD)
            if h < nq:
                d = dq_ref[here, cols] * SCALE
            else:
                d = dk_ref[here, (h - nq) * HD : (h - nq + 1) * HD] * SCALE
            dn = d * cos + pltpu.roll(d * sin, HD // 2, 1)
            ph = p_ref[here, cols].astype(F32)
            r = lax.rsqrt(lane_mean(ph * ph) + EPS)
            nh = ph * r
            dnh = dn * nh
            sums[which] += jnp.sum(dnh, axis=0, keepdims=True)
            dp_ref[here, cols] = (r * (dn * g - nh * lane_mean(dnh * g))).astype(BF)
        dp_ref[here, (nq + nk) * HD :] = dv_ref[here, :].astype(BF)
        ggq_ref[0:1, :] += sums[0]
        ggk_ref[0:1, :] += sums[1]
        dxn_ref[i] = dot_nt(dp_ref[here, :], rows_of(w)).astype(BF)


def feed_up(nm_ref, wgu_ref, hid_ref, dgu_ref):
    rows = nm_ref.shape[1]
    ff = hid_ref.shape[1]

    @pl.loop(0, nm_ref.shape[0])
    def _(i):
        here = lanes(i, rows)
        both = dot(nm_ref[i], rows_of(wgu_ref))
        gate, up = both[:, :ff], both[:, ff:]
        dgu_ref[here, :] = both.astype(BF)
        hid_ref[here, :] = (gate / (1.0 + jnp.exp2(gate * -LOG2E)) * up).astype(BF)


def feed_down(og_ref, wgu_ref, wd_ref, hid_ref, dgu_ref, out_ref, dnm_ref):
    rows = og_ref.shape[1]
    ff = hid_ref.shape[1]

    @pl.loop(0, og_ref.shape[0])
    def _(i):
        here = lanes(i, rows)
        gate, up = dgu_ref[here, :ff].astype(F32), dgu_ref[here, ff:].astype(F32)
        s = 1.0 / (1.0 + jnp.exp2(gate * -LOG2E))
        dh = dot_nt(og_ref[i], rows_of(wd_ref))
        dgu_ref[here, :ff] = (dh * up * (s * (1.0 + gate * (1.0 - s)))).astype(BF)
        dgu_ref[here, ff:] = (dh * (gate * s)).astype(BF)
        dnm_ref[i] = dot_nt(dgu_ref[here, :], rows_of(wgu_ref)).astype(BF)
        out_ref[i] = dot(hid_ref[here, :], rows_of(wd_ref)).astype(BF)


def weight_grad(out_ref, left_ref, right, chunk=256):
    size = math.prod(out_ref.shape[1:-1])
    width = out_ref.shape[-1]

    @pl.loop(0, left_ref.shape[-1] // chunk)
    def _(i):
        left = left_ref[..., lanes(i, chunk)].reshape(-1, chunk)
        g = dot_tn(left, rows_of(right)).astype(BF)
        for j in range(chunk // size):
            out_ref[i * (chunk // size) + j] = g[j * size : (j + 1) * size].reshape(out_ref.shape[1:-1] + (width,))


MESH = pl.DeviceIdType.MESH


def rcopy(src, dst, send, recv, **device):
    return pltpu.make_async_remote_copy(
        src_ref=src, dst_ref=dst, send_sem=send, recv_sem=recv, device_id=device, device_id_type=MESH
    )


class Place:
    def __init__(self, n):
        self.n, self.line = n, n // 2
        self.dp, self.ctx = lax.axis_index("dp"), lax.axis_index("ctx")
        self.outer, self.inner = self.dp // 2, self.dp % 2
        self.dp_inner = self.outer * 2 + 1 - self.inner
        self.dp_up, self.dp_down = self.dp + 2, self.dp - 2
        self.has_up, self.has_down = self.outer < self.line - 1, self.outer > 0
        core = self.ctx % 2
        self.c_core = self.ctx + 1 - 2 * core
        self.c_x = (self.ctx + 2) % 4
        self.c_far = 3 - self.ctx
        mine = self.dp * 4 + self.ctx
        self.slab_to = {"dp": mine % n, "ctx": mine // n}
        source = self.ctx * n + self.dp
        self.slab_from = {"dp": source // 4, "ctx": source % 4}
        self.slab_stays = source == mine


def greet(place, slabs):
    barrier = pltpu.get_barrier_semaphore()

    def signal(**device):
        pl.semaphore_signal(barrier, inc=1, device_id=device, device_id_type=MESH)

    for c in (place.c_core, place.c_x, place.c_far):
        signal(ctx=c)
    for k in range(1, place.n):
        signal(dp=(place.dp + k) % place.n)
    count = place.n + 2
    for slab in slabs:

        @pl.when(jnp.logical_not(place.slab_stays))
        def _():
            signal(**slab)

        count = count + jnp.where(place.slab_stays, 0, 1)
    return barrier, count


class Gather:
    def __init__(self, place, bufs, sems):
        self.at, self.bufs, self.sems = place, bufs, sems

    @staticmethod
    def scratch(n, bufs):
        return pltpu.SemaphoreType.DMA((5, bufs, n // 2))

    def copy(self, b, p, way):
        at = self.at
        block = self.bufs[b].at[p * 2 + at.inner]
        device = (at.dp_up, at.dp_down, at.dp_inner)[way]
        recv = self.sems.at[4 if way == 2 else 3, b, p]
        return rcopy(block, block, self.sems.at[way, b, p], recv, dp=device)

    def send(self, p, up, down, inner=True):
        at = self.at
        for b in range(len(self.bufs)):
            if up:

                @pl.when(at.has_up)
                def _():
                    self.copy(b, p, 0).start()

            if down:

                @pl.when(at.has_down)
                def _():
                    self.copy(b, p, 1).start()

            if inner:
                self.copy(b, p, 2).start()

    def start(self):
        self.send(self.at.outer, True, True)

    def start_inner(self):
        self.send(self.at.outer, False, False)

    def start_line(self):
        self.send(self.at.outer, True, True, False)

    def step(self, t):
        at = self.at
        for p, there, up in ((at.outer - t, at.outer >= t, True), (at.outer + t, at.outer + t < at.line, False)):

            @pl.when(there)
            def _():
                for b in range(len(self.bufs)):
                    self.copy(b, p, 0).wait_recv()
                self.send(p, up, not up)

    def arrive(self):
        at = self.at
        for b in range(len(self.bufs)):
            for p in range(at.line):
                block = self.bufs[b].at[p * 2 + 1 - at.inner]
                rcopy(block, block, self.sems.at[2, b, p], self.sems.at[4, b, p], dp=at.dp_inner).wait_recv()

    def finish(self):
        at = self.at
        for b in range(len(self.bufs)):
            for p in range(at.line):
                self.copy(b, p, 2).wait_send()

                @pl.when(jnp.logical_and(at.has_up, p <= at.outer))
                def _():
                    self.copy(b, p, 0).wait_send()

                @pl.when(jnp.logical_and(at.has_down, p >= at.outer))
                def _():
                    self.copy(b, p, 1).wait_send()


class Reduce:
    def __init__(self, place, parts, from_inner, from_line, sems):
        self.at, self.parts, self.from_inner, self.from_line, self.sems = place, parts, from_inner, from_line, sems

    @staticmethod
    def scratch(n, blocks):
        line = n // 2
        return (
            [pltpu.VMEM((line, *dims), dtype) for dims, dtype in blocks],
            [pltpu.VMEM((line + 1, *dims), dtype) for dims, dtype in blocks],
            pltpu.SemaphoreType.DMA((4, len(blocks), line + 1)),
        )

    def inner_copy(self, b, p):
        at = self.at
        return rcopy(
            self.parts[b].at[p * 2 + 1 - at.inner], self.from_inner[b].at[p],
            self.sems.at[0, b, p], self.sems.at[1, b, p], dp=at.dp_inner,
        )

    def line_copy(self, b, p, slot, up):
        at = self.at
        return rcopy(
            self.from_inner[b].at[p], self.from_line[b].at[slot],
            self.sems.at[2, b, p], self.sems.at[3, b, slot], dp=at.dp_up if up else at.dp_down,
        )

    def start(self, which):
        at = self.at
        for d in range(at.line - 1, -1, -1):
            for p, there in ((at.outer + d, at.outer + d < at.line), (at.outer - d, at.outer >= d))[: 2 if d else 1]:

                @pl.when(there)
                def _():
                    for b in which:
                        self.inner_copy(b, p).start()

    def total(self, b, p, slots):
        s = self.parts[b][p * 2 + self.at.inner].astype(F32) + self.from_inner[b][p].astype(F32)
        for slot in slots:
            s = s + self.from_line[b][slot].astype(F32)
        return s

    def step(self, d, which):
        at = self.at
        for p, there, more, up in (
            (at.outer + d, at.outer + d < at.line, at.has_down, True),
            (at.outer - d, at.outer >= d, at.has_up, False),
        ):
            for b in which:

                @pl.when(there)
                def _():
                    self.inner_copy(b, p).wait_recv()
                    into = self.from_inner[b].at[p]

                    @pl.when(more)
                    def _():
                        self.line_copy(b, p, p, up).wait_recv()
                        into[...] = self.total(b, p, [p]).astype(into.dtype)

                    @pl.when(jnp.logical_not(more))
                    def _():
                        into[...] = self.total(b, p, []).astype(into.dtype)

                    slot = p if up or d > 1 else at.line
                    self.line_copy(b, p, slot, up).start()

    def result(self, b, store):
        at = self.at
        p = at.outer
        self.inner_copy(b, p).wait_recv()
        lo, hi = at.has_down, at.has_up

        @pl.when(lo)
        def _():
            self.line_copy(b, p, p, True).wait_recv()

        @pl.when(hi)
        def _():
            self.line_copy(b, p, at.line, False).wait_recv()

        @pl.when(jnp.logical_and(lo, hi))
        def _():
            store(self.total(b, p, [p, at.line]))

        @pl.when(jnp.logical_and(lo, jnp.logical_not(hi)))
        def _():
            store(self.total(b, p, [p]))

        @pl.when(jnp.logical_and(hi, jnp.logical_not(lo)))
        def _():
            store(self.total(b, p, [at.line]))

    def finish(self):
        at = self.at
        for b in range(len(self.parts)):
            for p in range(at.line):
                self.inner_copy(b, p).wait_send()

                @pl.when(p != at.outer)
                def _():
                    self.line_copy(b, p, p, True).wait_send()


class CtxGather:
    def __init__(self, place, buf, sems):
        self.at, self.buf, self.sems = place, buf, sems

    def copy(self, k, owner):
        block = self.buf.at[owner]
        ctx = self.at.c_x if k == 1 else self.at.c_core
        return rcopy(block, block, self.sems.at[0, k], self.sems.at[1, k], ctx=ctx)

    def start(self):
        self.copy(1, self.at.ctx).start()
        self.copy(0, self.at.ctx).start()

    def forward(self):
        self.copy(1, self.at.c_x).wait_recv()
        self.copy(2, self.at.c_x).start()

    def arrive(self):
        self.copy(0, self.at.c_core).wait_recv()
        self.copy(2, self.at.c_far).wait_recv()

    def finish(self):
        for k in range(3):
            self.copy(k, self.at.ctx).wait_send()


class CtxReduce:
    def __init__(self, place, part, got, sems):
        self.at, self.part, self.got, self.sems = place, part, got, sems

    def copy(self, k):
        at = self.at
        block = self.got.at[1] if k == 2 else self.part.at[(at.c_core, at.c_far)[k]]
        return rcopy(block, self.got.at[k], self.sems.at[0, k], self.sems.at[1, k], ctx=at.c_x if k == 2 else at.c_core)

    def start(self):
        self.copy(1).start()
        self.copy(0).start()

    def across(self):
        self.copy(1).wait_recv()
        into = self.got.at[1]
        into[...] = (self.part[self.at.c_x].astype(F32) + into[...].astype(F32)).astype(into.dtype)
        self.copy(2).start()

    def result(self):
        self.copy(0).wait_recv()
        self.copy(2).wait_recv()
        return self.part[self.at.ctx].astype(F32) + self.got[0].astype(F32) + self.got[2].astype(F32)

    def finish(self):
        for k in range(3):
            self.copy(k).wait_send()


class Quarters:
    def __init__(self, place, src, dst, sems):
        self.at, self.src, self.dst, self.sems = place, src, dst, sems

    def copies(self):
        at = self.at
        return [
            rcopy(self.src.at[c], self.dst.at[at.ctx], self.sems.at[0, k], self.sems.at[1, k], ctx=c)
            for k, c in enumerate((at.c_x, at.c_far, at.c_core))
        ]

    def start(self):
        for c in self.copies():
            c.start()
        self.dst[self.at.ctx] = self.src[self.at.ctx]

    def finish(self):
        for c in self.copies():
            c.wait()


class Slab:
    def __init__(self, place, src, dst, sems, to):
        self.at, self.src, self.dst, self.sems, self.to = place, src, dst, sems, to

    def copy(self):
        return rcopy(self.src, self.dst, self.sems.at[0, 0], self.sems.at[1, 0], **self.to)

    def start(self):
        @pl.when(self.at.slab_stays)
        def _():
            self.dst[...] = self.src[...]

        @pl.when(jnp.logical_not(self.at.slab_stays))
        def _():
            self.copy().start()

    def finish(self):
        @pl.when(jnp.logical_not(self.at.slab_stays))
        def _():
            self.copy().wait()


class Exchange:
    def __init__(self, place, src, dst, cap, sems):
        self.at, self.src, self.dst, self.cap, self.sems = place, src, dst, cap, sems

    def rows(self, ref, j):
        if len(ref.shape) == 3:
            size = ref.shape[1]
            start = j * self.cap
            return ref.at[start // size, pl.ds(pl.multiple_of(start % size, self.cap), self.cap)]
        return ref.at[pl.ds(pl.multiple_of(j * self.cap, self.cap), self.cap)]

    def copy(self, k):
        at = self.at
        to = (at.dp + k) % at.n
        return rcopy(self.rows(self.src, to), self.rows(self.dst, at.dp), self.sems.at[0, k], self.sems.at[1, k], dp=to)

    def start(self):
        for k in range(1, self.at.n):
            self.copy(k).start()
        self.rows(self.dst, self.at.dp)[...] = self.rows(self.src, self.at.dp)[...]

    def finish(self):
        for k in range(1, self.at.n):
            self.copy(k).wait()


def sem_pairs(count):
    return pltpu.SemaphoreType.DMA((2, count))


def norm_back(c, v, gain):
    r = lax.rsqrt(jnp.mean(v * v, axis=-1, keepdims=True) + EPS)
    nv = v * r
    cg = c * gain
    return jnp.sum(c * nv, axis=0, keepdims=True), r * (cg - nv * jnp.mean(cg * nv, axis=-1, keepdims=True))


def into(ref):
    def store(v):
        ref[...] = v.astype(ref.dtype)

    return store


def quarter_columns(dst_ref, weights):
    for c in range(4):
        start = 0
        for w in weights:
            size = w.shape[1] // 4
            dst_ref[c, :, start : start + size] = w[:, c * size : (c + 1) * size]
            start += size


def unit_columns(n, dst_ref, weights):
    size = weights[0].shape[1] // (4 * n)
    for c in range(4):
        for k, w in enumerate(weights):
            for d in range(n):
                start = (k * n + d) * size
                dst_ref[c, :, start : start + size] = w[:, (d * 4 + c) * size : (d * 4 + c + 1) * size]


def route(n, cap, dest_ref, place_ref, labs_ref):
    tok = dest_ref.shape[1]
    dest = dest_ref[...]
    owner = jnp.right_shift(dest, (4 * tok).bit_length() - 1)
    slot = jnp.bitwise_and(dest, tok - 1)
    lines = lax.broadcasted_iota(jnp.int32, (n, tok), 0)
    hot = (lines == owner).astype(F32)
    before = lax.broadcasted_iota(jnp.int32, (tok, tok), 0) < lax.broadcasted_iota(jnp.int32, (tok, tok), 1)
    rank = dot(hot.astype(BF), before.astype(BF))
    send = jnp.sum(hot * (rank + (lines * cap).astype(F32)), axis=0, keepdims=True).astype(jnp.int32)
    place = (lax.broadcasted_iota(jnp.int32, (n * cap, tok), 0) == send).astype(BF)
    place_ref[...] = place
    labels = dot_nt(jnp.broadcast_to((slot + 1).astype(F32), (8, tok)).astype(BF), place)
    labs_ref[...] = jnp.zeros_like(labs_ref)
    for j in range(n):
        labs_ref[j * 8 : j * 8 + 8, :cap] = labels[:, j * cap : (j + 1) * cap]


def gain_tile(at, raw_ref, counts):
    index = at.dp * 4 + at.ctx
    raw = jnp.broadcast_to(raw_ref[...], (8, 128)).astype(BF)
    source = lax.broadcasted_iota(jnp.int32, (128, 128), 0)
    target = lax.broadcasted_iota(jnp.int32, (128, 128), 1)
    lines = lax.broadcasted_iota(jnp.int32, (8, 128), 0)
    total, start = jnp.zeros((8, 128), F32), 0
    for k, count in enumerate(counts):
        move = (target - (index * count) % 128 == source - start) & (source >= start) & (source < start + count)
        total = total + jnp.where(lines == k, dot(raw, move.astype(BF)), 0.0)
        start += count
    return total


def final_body(counts, ig, layer, qkv, o, gu, gd, small, layer_out, ig_out, ga, gq, gk, gv, gqg, gkg, go, gm, gg, gup, gdn):
    index = lax.axis_index("dp") * 4 + lax.axis_index("ctx")
    layer_out[...] = layer[...]
    ig_out[...] = ig[...]
    for c in range(4):
        start = 0
        for out in (gq, gk, gv):
            size = out.shape[1] // 4
            out[:, c * size : (c + 1) * size] = qkv[c, :, start : start + size].astype(F32)
            start += size
        size = gdn.shape[0]
        n = gg.shape[1] // (4 * size)
        for k, out in enumerate((gg, gup)):
            for d in range(n):
                start = (k * n + d) * size
                out[:, (d * 4 + c) * size : (d * 4 + c + 1) * size] = gu[c, :, start : start + size].astype(F32)
    go[...] = o[...].astype(F32)
    gdn[...] = gd[...].astype(F32)
    for k, (out, count) in enumerate(zip((ga, gm, gqg, gkg), counts)):
        row = pltpu.roll(small[...], (128 - (index * count) % 128) % 128, 1)
        out[...] = row[k : k + 1, :count]


def layer_body(
    n, cap, counts,
    in_ref, dest_ref, doc_ref, raw_ref, og_ref, wq_src, wk_src, wv_src, wo_src, wg_src, wu_src, wd_src, cos_ref, sin_ref,
    ig_ref, layer_ref, qkv_out, o_out, gu_out, gd_out, gain_out,
    wqkv_ref, wo_ref, wgu_ref, wd_ref, og_all, x_own, pick_ref, ga_ref, gm_ref, q_ref, k_ref, v_ref, p_ref, xn_ref, att_ref, nm_ref, mid_ref,
    recv, labels, gains_c, gains_n, x_ref, part_ref, got, mask_ref,
    hid_ref, dgu_ref, outp_ref, got_d, got_o, dmid_ref, dq_ref, dk_ref, dv_ref, ggq_ref, ggk_ref, ggm_ref, gains, recv_back,
    yi0, yi1, ln0, ln1, s_ra, yo, lo, s_rb, yq, yg, lq, lg, s_rc,
    gain_sum, gain_all, qkv_ref, gu_ref, place_ref, lab_ref, gwd_ref,
    s_ga, s_gb, s_gc, s_gd4, s_rows, s_labs, s_qkv, s_gu, s_wo, s_gain, s_x, s_og, s_red, s_nm,
    s_dnm, s_out, s_db, s_dxn, s_rows_back, s_gu_back, s_qkv_back, s_o, s_gain_back,
):
    at = Place(n)
    barrier, count = greet(at, (at.slab_from, at.slab_to))
    quarter_columns(qkv_ref, (wq_src, wk_src, wv_src))
    gains_c[at.ctx] = gain_tile(at, raw_ref, counts)
    route(n, cap, dest_ref, place_ref, lab_ref)
    tok = in_ref.shape[0]
    for half in range(n * cap // tok):
        part_ref[half] = dot(place_ref[half * tok : (half + 1) * tok, :], in_ref[...]).astype(BF)
    pl.semaphore_wait(barrier, count)
    qkv = Quarters(at, qkv_ref, wqkv_ref.at[at.dp], s_qkv)
    rows = Exchange(at, part_ref, recv, cap, s_rows)
    labs = Exchange(at, lab_ref, labels, 8, s_labs)
    qkv.start()
    gain_copies = [
        rcopy(gains_c.at[at.ctx], gains_c.at[at.ctx], s_gain.at[0, k], s_gain.at[1, k], ctx=c)
        for k, c in enumerate((at.c_x, at.c_far, at.c_core))
    ]
    for g in gain_copies:
        g.start()
    unit_columns(n, gu_ref, (wg_src, wu_src))
    wo = Slab(at, wo_src, wo_ref.at[at.slab_to["dp"]], s_wo, at.slab_to)
    wd_ref[at.dp] = wd_src[...]
    gu = Quarters(at, gu_ref, wgu_ref.at[at.dp], s_gu)
    labs.start()
    rows.start()
    gu.start()
    wo.start()
    for g in gain_copies:
        g.wait()
    gains_n[at.dp] = gains_c[0] + gains_c[1] + gains_c[2] + gains_c[3]
    qkv.finish()
    first = Gather(at, [wqkv_ref, gains_n], s_ga)
    first.start()
    og_all[at.ctx] = og_ref[...]
    og = CtxGather(at, og_all, s_og)
    gu.finish()
    og.start()
    third = Gather(at, [wgu_ref], s_gc)
    third.start_inner()
    labs.finish()
    slots = lax.broadcasted_iota(jnp.int32, (tok, cap), 0).astype(F32) + 1.0
    for j in range(n):
        pick_ref[:, j * cap : (j + 1) * cap] = (slots == labels[j * 8 : j * 8 + 1, :cap]).astype(BF)
    first.step(1)
    rows.finish()
    owned = dot(pick_ref[...], recv[...]).astype(BF)
    x_ref[at.ctx] = owned
    x_own[...] = owned
    x = CtxGather(at, x_ref, s_x)
    x.start()
    first.step(2)
    third.start_line()
    wo.finish()
    second = Gather(at, [wo_ref], s_gb)
    second.start()
    for t in range(3, at.line):
        first.step(t)
    second.step(1)
    og.forward()
    x.forward()
    first.arrive()
    own = 4 * ga_ref.shape[1] // (4 * n)
    ga_ref[...] = jnp.zeros_like(ga_ref)
    gm_ref[...] = jnp.zeros_like(gm_ref)
    gqk = jnp.zeros((8, 128), F32)
    for d in range(n):
        tile = slice(d * own // 128 * 128, d * own // 128 * 128 + 128)
        block = gains_n[d]
        ga_ref[0:1, tile] += block[0:1]
        gm_ref[0:1, tile] += block[1:2]
        gqk = gqk + block
    off = jnp.where(doc_ref[0:1, 0:1] > 0, 0.0, MASKED).astype(F32)
    mask_ref[...] = mask_block(off)
    x.arrive()
    second.step(2)
    attn_project(x_ref, wqkv_ref, ga_ref, gqk[2:3], gqk[3:4], cos_ref, sin_ref, q_ref, k_ref, v_ref, p_ref, xn_ref)
    for t in range(3, at.line):
        second.step(t)
    third.step(1)
    nk = k_ref.shape[1] // HD

    @pl.loop(0, nk)
    def _(g):
        attn_group(g, off, q_ref, k_ref, v_ref, att_ref, mask_ref)

    third.step(2)
    second.arrive()

    @pl.loop(0, 4)
    def _(i):
        part_ref[i] = dot(att_ref[lanes(i, tok), :], rows_of(wo_ref)).astype(BF)

    red = CtxReduce(at, part_ref, got, s_red)
    red.start()
    red.across()
    for t in range(3, at.line):
        third.step(t)
    fourth = Gather(at, [wd_ref], s_gd4)
    fourth.start()
    middle = x_own[...].astype(F32) + red.result()
    mid_ref[...] = middle
    r = lax.rsqrt(jnp.mean(middle * middle, axis=-1, keepdims=True) + EPS)
    nm_ref[at.ctx] = (middle * r * gm_ref[0:1, :]).astype(BF)
    nm = CtxGather(at, nm_ref, s_nm)
    nm.start()
    fourth.step(1)
    nm.forward()
    fourth.step(2)
    nm.arrive()
    og.arrive()
    for t in range(3, at.line):
        fourth.step(t)
    third.arrive()
    feed_up(nm_ref, wgu_ref, hid_ref, dgu_ref)
    weight_grad(gwd_ref, hid_ref, og_all, 384)
    grads = Reduce(at, [wgu_ref, gwd_ref], [yi0, yi1], [ln0, ln1], s_ra)
    grads.start([1])
    fourth.arrive()
    for part in (first, second, third, fourth, og, x, nm, red):
        part.finish()
    first = grads
    feed_down(og_all, wgu_ref, wd_ref, hid_ref, dgu_ref, outp_ref, part_ref)
    db_ref, da_ref, dp_ref = x_ref, hid_ref.at[:, : q_ref.shape[1]], dgu_ref.at[:, : wqkv_ref.shape[-1]]
    last = at.line - 1
    dnm = CtxReduce(at, part_ref, got_d, s_dnm)
    dnm.start()
    first.step(last, [1])
    dnm.across()
    weight_grad(wgu_ref, nm_ref, dgu_ref)
    first.start([0])
    out = CtxReduce(at, outp_ref, got_o, s_out)
    dk_ref[...] = jnp.zeros_like(dk_ref)
    dv_ref[...] = jnp.zeros_like(dv_ref)
    first.step(last - 1, [1])
    gg, d = norm_back(dnm.result(), mid_ref[...], gm_ref[0:1, :])
    ggm_ref[...] = gg
    d = d + og_ref[...].astype(F32)
    dmid_ref[...] = d
    db_ref[at.ctx] = d.astype(BF)
    db = CtxGather(at, db_ref, s_db)
    db.start()
    out.start()
    for t in range(last - 2, 0, -1):
        first.step(t, [1])
    db.forward()
    out.across()
    db.arrive()
    tok = db_ref.shape[1]

    @pl.loop(0, 4)
    def _(i):
        da_ref[lanes(i, tok), :] = dot_nt(db_ref[i], rows_of(wo_ref)).astype(BF)

    first.step(last, [0])
    for g in range(k_ref.shape[1] // HD):
        for i in range(q_ref.shape[0] // QB):
            attn_group_back(g, i, off, q_ref, k_ref, v_ref, att_ref, da_ref, dq_ref, dk_ref, dv_ref, mask_ref)
        if g == 0:
            for t in range(last - 1, 1, -1):
                first.step(t, [0])
    dxn_ref = nm_ref
    attn_unproject(gqk[2:3], gqk[3:4], cos_ref, sin_ref, p_ref, dq_ref, dk_ref, dv_ref, dp_ref, wqkv_ref, dxn_ref, ggq_ref, ggk_ref)
    dxn = CtxReduce(at, dxn_ref, got, s_dxn)
    dxn.start()
    first.step(1, [0])
    weight_grad(wqkv_ref, xn_ref, dp_ref)
    third = Reduce(at, [wqkv_ref, gains], [yq, yg], [lq, lg], s_rc)
    third.start([0])
    dxn.across()
    weight_grad(wo_ref, att_ref, db_ref)
    second = Reduce(at, [wo_ref], [yo], [lo], s_rb)
    second.start([0])
    first.result(1, into(gd_out))
    first.result(0, into(yi0.at[at.outer]))
    gu = Quarters(at, yi0.at[at.outer], gu_out, s_gu_back)
    gu.start()
    third.step(last, [0])
    gg, d = norm_back(dxn.result(), x_own[...].astype(F32), ga_ref[0:1, :])
    owned = (dmid_ref[...] + d).astype(BF)
    recv[...] = dot_tn(pick_ref[...], owned).astype(BF)
    rows = Exchange(at, recv, recv_back, cap, s_rows_back)
    rows.start()
    own = 4 * gg.shape[1] // (4 * n)
    lines = lax.broadcasted_iota(jnp.int32, (8, 128), 0)
    for j in range(n):
        tile = slice(j * own // 128 * 128, j * own // 128 * 128 + 128)
        gains[j] = (
            jnp.where(lines == 0, gg[:, tile], 0.0) + jnp.where(lines == 1, ggm_ref[0:1, tile], 0.0)
            + jnp.where(lines == 2, ggq_ref[0:1, :], 0.0) + jnp.where(lines == 3, ggk_ref[0:1, :], 0.0)
        )
    third.start([1])
    second.step(last, [0])
    for t in range(last - 1, 0, -1):
        third.step(t, [0])
        second.step(t, [0])
    layer_ref[...] = (mid_ref[...] + out.result()).astype(BF)
    for t in range(last, 0, -1):
        third.step(t, [1])
    second.result(0, into(yo.at[at.outer]))
    o = Slab(at, yo.at[at.outer], o_out, s_o, at.slab_from)
    o.start()
    third.result(0, into(yq.at[at.outer]))
    qkv = Quarters(at, yq.at[at.outer], qkv_out, s_qkv_back)
    qkv.start()
    third.result(1, into(gain_sum))
    small = [
        rcopy(gain_sum, gain_all.at[at.ctx], s_gain_back.at[0, k], s_gain_back.at[1, k], ctx=c)
        for k, c in enumerate((at.c_x, at.c_far, at.c_core))
    ]
    for g in small:
        g.start()
    gain_all[at.ctx] = gain_sum[...]
    rows.finish()
    ig_ref[...] = dot_tn(place_ref[...], recv_back[...]).astype(BF)
    for g in small:
        g.wait()
    gain_out[...] = gain_all[0] + gain_all[1] + gain_all[2] + gain_all[3]
    for part in (qkv, o, gu, dxn, db, out, dnm, first, second, third):
        part.finish()


def shape(*dims, dtype=BF):
    return jax.ShapeDtypeStruct(dims, dtype)


def linked(body, outs, scratch, name, number):
    return pl.pallas_call(
        body,
        out_shape=outs,
        scratch_shapes=scratch,
        compiler_params=pltpu.CompilerParams(vmem_limit_bytes=VMEM_LIMIT, collective_id=number, has_side_effects=True),
        name=name,
    )


def local(
    layer_input, dest_slot, doc_len, out_grad, attn_gain, w_query, w_key, w_value, q_gain, k_gain,
    w_out, mlp_gain, w_gate, w_up, w_down,
):
    tok, width = layer_input.shape
    n = lax.axis_size("dp")
    cap = 2 * tok // n
    rows = 4 * tok
    slabs = n * cap
    rq, ro, rd = w_query.shape[0], w_out.shape[0], w_down.shape[0]
    ff = rd * n
    counts = (attn_gain.shape[0], mlp_gain.shape[0], q_gain.shape[0], k_gain.shape[0])
    raw = jnp.pad(jnp.concatenate([attn_gain, mlp_gain, q_gain, k_gain]), (0, 128 - sum(counts))).astype(F32).reshape(1, 128)
    fw = 2 * ff
    cos, sin = rope_tables(rows)
    blocks = ([((4, rq, fw), BF), ((rd, width), BF)], [((ro, width), BF)], [((4, rq, 1024), BF), ((8, 128), F32)])
    reduces = []
    for red, lines, sems in (Reduce.scratch(n, b) for b in blocks):
        reduces += [*red, *lines, sems]
    vm = pltpu.VMEM
    group = (4, tok, width)
    input_grad, layer_output, g_qkv, g_o, g_gu, g_d, small = linked(
        functools.partial(layer_body, n, cap, counts),
        (shape(tok, width), shape(tok, width), shape(4, rq, 1024), shape(ro, width), shape(4, rq, fw), shape(rd, width), shape(8, 128, dtype=F32)),
        [vm((n, 4, rq, 1024), BF), vm((n, ro, width), BF), vm((n, 4, rq, fw), BF), vm((n, rd, width), BF), vm(group, BF), vm((tok, width), BF),
         vm((tok, slabs), BF), vm((8, width), F32), vm((8, width), F32), vm((rows, 512), BF), vm((rows, 256), BF), vm((rows, 256), BF),
         vm((rows, 768), BF), vm((rows, width), BF), vm((rows, 512), BF), vm(group, BF), vm((tok, width), F32),
         vm((slabs, width), BF), vm((n * 8, 128), F32), vm((4, 8, 128), F32), vm((n, 8, 128), F32),
         vm(group, BF), vm(group, BF), vm((3, tok, width), BF), vm((QB, QB), F32),
         vm((rows, ff), BF), vm((rows, fw), BF), vm(group, BF), vm((3, tok, width), BF), vm((3, tok, width), BF),
         vm((tok, width), F32), vm((rows, 512), F32), vm((rows, 256), F32), vm((rows, 256), F32),
         vm((8, HD), F32), vm((8, HD), F32), vm((1, width), F32), vm((n, 8, 128), F32), vm((slabs, width), BF),
         *reduces,
         vm((8, 128), F32), vm((4, 8, 128), F32), vm((4, rq, 1024), BF), vm((4, rq, fw), BF), vm((slabs, tok), BF), vm((n * 8, 128), F32), vm((n, rd, width), BF),
         Gather.scratch(n, 2), Gather.scratch(n, 1), Gather.scratch(n, 1), Gather.scratch(n, 1), sem_pairs(n), sem_pairs(n), sem_pairs(3), sem_pairs(3),
         sem_pairs(1), sem_pairs(3), sem_pairs(3), sem_pairs(3), sem_pairs(3), sem_pairs(3),
         sem_pairs(3), sem_pairs(3), sem_pairs(3), sem_pairs(3), sem_pairs(n), sem_pairs(3), sem_pairs(3), sem_pairs(1), sem_pairs(3)],
        "layer", 0,
    )(layer_input, dest_slot.reshape(1, tok), doc_len, raw, out_grad, w_query, w_key, w_value, w_out, w_gate, w_up, w_down, cos, sin)
    grads = [shape(*w.shape, dtype=F32) for w in (w_query, w_key, w_value, w_out, w_gate, w_up, w_down)]
    gains = [shape(1, c, dtype=F32) for c in counts]
    outs = (shape(tok, width), shape(tok, width), gains[0], *grads[:3], gains[2], gains[3], grads[3], gains[1], *grads[4:])
    outs = pl.pallas_call(functools.partial(final_body, counts), out_shape=outs, name="final")(
        input_grad, layer_output, g_qkv, g_o, g_gu, g_d, small
    )
    return tuple(o.reshape(-1) if o.shape[0] == 1 else o for o in outs)


def solution(mesh):
    rows = P(BOTH, None)
    vec = P(BOTH)
    return jax.shard_map(
        local,
        mesh=mesh,
        in_specs=(rows, vec, P("dp", None), rows, vec, rows, rows, rows, vec, vec, rows, vec, rows, rows, rows),
        out_specs=(rows, rows, vec, rows, rows, rows, vec, vec, rows, vec, rows, rows, rows),
        check_vma=False,
    )
```

```python
import functools
import math

import jax
import jax.numpy as jnp
import numpy as np
from jax import lax
from jax.experimental import pallas as pl
from jax.experimental.pallas import tpu as pltpu
from jax.sharding import PartitionSpec as P

H = 16
KVH = 8
HD = 128
EPS = 1e-06
THETA = 1000000.0
MASKED = -1e30
QB = 128
SCALE = HD ** (-0.5)
LOG2E = math.log2(math.e)
BF = jnp.bfloat16
F32 = jnp.float32
BOTH = ("dp", "ctx")
VMEM_LIMIT = 63 << 20


def dot(a, b):
    return lax.dot_general(a, b, (((1,), (0,)), ((), ())), preferred_element_type=F32)


def dot_nt(a, b):
    return lax.dot_general(a, b, (((1,), (1,)), ((), ())), preferred_element_type=F32)


def dot_tn(a, b):
    return lax.dot_general(a, b, (((0,), (0,)), ((), ())), preferred_element_type=F32)


def lanes(start, size):
    return pl.ds(pl.multiple_of(start * size, size), size)


def rope_tables(rows):
    inverse = np.exp(np.arange(HD // 2, dtype=np.float32) * np.float32(-2.0 / HD * math.log(THETA)))
    doubled = np.concatenate([inverse, inverse]).astype(np.float32)
    angles = np.arange(rows, dtype=np.float32)[:, None] * doubled[None, :]
    sign = np.where(np.arange(HD) < HD // 2, -1.0, 1.0).astype(np.float32)
    return np.cos(angles), np.sin(angles) * sign[None, :]


def mask_block(off_bias):
    rows = lax.broadcasted_iota(jnp.int32, (QB, QB), 0)
    cols = lax.broadcasted_iota(jnp.int32, (QB, QB), 1)
    return jnp.where(rows == cols, 0.0, jnp.where(cols < rows, off_bias, MASKED))


def lane_mean(v):
    ones = jnp.full((HD, HD), 1.0 / HD, BF)
    high = v.astype(BF)
    return dot(high, ones) + dot((v - high.astype(F32)).astype(BF), ones)


def rows_of(ref):
    value = ref[...]
    return value.reshape(-1, value.shape[-1])


def attn_project(x_ref, w, ga, gq, gk, cos_ref, sin_ref, q_ref, k_ref, v_ref, p_ref, xn_ref):
    rows = xn_ref.shape[0]
    tok = x_ref.shape[1]
    nq = q_ref.shape[1] // HD
    nk = k_ref.shape[1] // HD

    @pl.loop(0, rows // tok)
    def _(i):
        here = lanes(i, tok)
        x = x_ref[i].astype(F32)
        r = lax.rsqrt(jnp.mean(x * x, axis=-1, keepdims=True) + EPS)
        xn = (x * r * ga[0:1, :]).astype(BF)
        xn_ref[here, :] = xn
        p = dot(xn, rows_of(w))
        p_ref[here, :] = p[:, : (nq + nk) * HD].astype(BF)
        v_ref[here, :] = p[:, (nq + nk) * HD :].astype(BF)
        cos = cos_ref[here, :]
        sin = sin_ref[here, :]
        for h in range(nq + nk):
            ph = p[:, h * HD : (h + 1) * HD]
            g = gq if h < nq else gk
            nv = ph * lax.rsqrt(lane_mean(ph * ph) + EPS) * g
            rot = (nv * cos + pltpu.roll(nv, HD // 2, 1) * sin).astype(BF)
            if h < nq:
                q_ref[here, h * HD : (h + 1) * HD] = rot
            else:
                k_ref[here, (h - nq) * HD : (h - nq + 1) * HD] = rot


def group_rows(ref, here, g, group):
    return jnp.concatenate([ref[here, lanes(g * group + a, HD)] for a in range(group)], axis=0)


def attn_probs(q, k, off, mask_ref, group):
    s = dot_nt(q, k) * (SCALE * LOG2E)
    cut = s.shape[1] - QB
    last = jnp.exp2(s[:, cut:] + jnp.concatenate([mask_ref[...]] * group, axis=0))
    e = last if cut == 0 else jnp.concatenate([jnp.exp2(s[:, :cut] + off), last], axis=1)
    return e * (1.0 / jnp.sum(e, axis=-1, keepdims=True))


def attn_group(g, off, q_ref, k_ref, v_ref, att_ref, mask_ref):
    group = q_ref.shape[1] // k_ref.shape[1]
    hk = lanes(g, HD)
    for i in range(q_ref.shape[0] // QB):
        here, keys = slice(i * QB, (i + 1) * QB), slice(0, (i + 1) * QB)
        probs = attn_probs(group_rows(q_ref, here, g, group), k_ref[keys, hk], off, mask_ref, group)
        o = dot(probs.astype(BF), v_ref[keys, hk]).astype(BF)
        for a in range(group):
            att_ref[here, lanes(g * group + a, HD)] = o[a * QB : (a + 1) * QB]


def attn_group_back(g, i, off, q_ref, k_ref, v_ref, att_ref, da_ref, dq_ref, dk_ref, dv_ref, mask_ref):
    group = q_ref.shape[1] // k_ref.shape[1]
    hk = lanes(g, HD)
    here, keys = slice(i * QB, (i + 1) * QB), slice(0, (i + 1) * QB)
    q, da, att = (group_rows(ref, here, g, group) for ref in (q_ref, da_ref, att_ref))
    inner = jnp.sum(da.astype(F32) * att.astype(F32), axis=-1, keepdims=True)
    probs = attn_probs(q, k_ref[keys, hk], off, mask_ref, group)
    ds = (probs * (dot_nt(da, v_ref[keys, hk]) - inner)).astype(BF)
    dq = dot(ds, k_ref[keys, hk])
    for a in range(group):
        dq_ref[here, lanes(g * group + a, HD)] = dq[a * QB : (a + 1) * QB]
    dk_ref[keys, hk] += dot_tn(ds, q)
    dv_ref[keys, hk] += dot_tn(probs.astype(BF), da)


def attn_unproject(gq, gk, cos_ref, sin_ref, p_ref, dq_ref, dk_ref, dv_ref, dp_ref, w, dxn_ref, ggq_ref, ggk_ref):
    rows = p_ref.shape[0]
    tok = dxn_ref.shape[1]
    nq = dq_ref.shape[1] // HD
    nk = dk_ref.shape[1] // HD
    ggq_ref[...] = jnp.zeros_like(ggq_ref)
    ggk_ref[...] = jnp.zeros_like(ggk_ref)

    @pl.loop(0, rows // tok)
    def _(i):
        here = lanes(i, tok)
        cos = cos_ref[here, :]
        sin = sin_ref[here, :]
        sums = [jnp.zeros((1, HD), F32), jnp.zeros((1, HD), F32)]
        for h in range(nq + nk):
            which = 0 if h < nq else 1
            g = gq if h < nq else gk
            cols = slice(h * HD, (h + 1) * HD)
            if h < nq:
                d = dq_ref[here, cols] * SCALE
            else:
                d = dk_ref[here, (h - nq) * HD : (h - nq + 1) * HD] * SCALE
            dn = d * cos + pltpu.roll(d * sin, HD // 2, 1)
            ph = p_ref[here, cols].astype(F32)
            r = lax.rsqrt(lane_mean(ph * ph) + EPS)
            nh = ph * r
            dnh = dn * nh
            sums[which] += jnp.sum(dnh, axis=0, keepdims=True)
            dp_ref[here, cols] = (r * (dn * g - nh * lane_mean(dnh * g))).astype(BF)
        dp_ref[here, (nq + nk) * HD :] = dv_ref[here, :].astype(BF)
        ggq_ref[0:1, :] += sums[0]
        ggk_ref[0:1, :] += sums[1]
        dxn_ref[i] = dot_nt(dp_ref[here, :], rows_of(w)).astype(BF)


def feed_up(nm_ref, wgu_ref, hid_ref, dgu_ref):
    rows = nm_ref.shape[1]
    ff = hid_ref.shape[1]

    @pl.loop(0, nm_ref.shape[0])
    def _(i):
        here = lanes(i, rows)
        both = dot(nm_ref[i], rows_of(wgu_ref))
        gate, up = both[:, :ff], both[:, ff:]
        dgu_ref[here, :] = both.astype(BF)
        hid_ref[here, :] = (gate / (1.0 + jnp.exp2(gate * -LOG2E)) * up).astype(BF)


def feed_down(og_ref, wgu_ref, wd_ref, hid_ref, dgu_ref, out_ref, dnm_ref):
    rows = og_ref.shape[1]
    ff = hid_ref.shape[1]

    @pl.loop(0, og_ref.shape[0])
    def _(i):
        here = lanes(i, rows)
        gate, up = dgu_ref[here, :ff].astype(F32), dgu_ref[here, ff:].astype(F32)
        s = 1.0 / (1.0 + jnp.exp2(gate * -LOG2E))
        dh = dot_nt(og_ref[i], rows_of(wd_ref))
        dgu_ref[here, :ff] = (dh * up * (s * (1.0 + gate * (1.0 - s)))).astype(BF)
        dgu_ref[here, ff:] = (dh * (gate * s)).astype(BF)
        dnm_ref[i] = dot_nt(dgu_ref[here, :], rows_of(wgu_ref)).astype(BF)
        out_ref[i] = dot(hid_ref[here, :], rows_of(wd_ref)).astype(BF)


def weight_grad(out_ref, left_ref, right, chunk=256):
    size = math.prod(out_ref.shape[1:-1])
    width = out_ref.shape[-1]

    @pl.loop(0, left_ref.shape[-1] // chunk)
    def _(i):
        left = left_ref[..., lanes(i, chunk)].reshape(-1, chunk)
        g = dot_tn(left, rows_of(right)).astype(BF)
        for j in range(chunk // size):
            out_ref[i * (chunk // size) + j] = g[j * size : (j + 1) * size].reshape(out_ref.shape[1:-1] + (width,))


MESH = pl.DeviceIdType.MESH


def rcopy(src, dst, send, recv, **device):
    return pltpu.make_async_remote_copy(
        src_ref=src, dst_ref=dst, send_sem=send, recv_sem=recv, device_id=device, device_id_type=MESH
    )


class Place:
    def __init__(self, n):
        self.n, self.line = n, n // 2
        self.dp, self.ctx = lax.axis_index("dp"), lax.axis_index("ctx")
        self.outer, self.inner = self.dp // 2, self.dp % 2
        self.dp_inner = self.outer * 2 + 1 - self.inner
        self.dp_up, self.dp_down = self.dp + 2, self.dp - 2
        self.has_up, self.has_down = self.outer < self.line - 1, self.outer > 0
        core = self.ctx % 2
        self.c_core = self.ctx + 1 - 2 * core
        self.c_x = (self.ctx + 2) % 4
        self.c_far = 3 - self.ctx
        mine = self.dp * 4 + self.ctx
        self.slab_to = {"dp": mine % n, "ctx": mine // n}
        source = self.ctx * n + self.dp
        self.slab_from = {"dp": source // 4, "ctx": source % 4}
        self.slab_stays = source == mine


def greet(place, slabs):
    barrier = pltpu.get_barrier_semaphore()

    def signal(**device):
        pl.semaphore_signal(barrier, inc=1, device_id=device, device_id_type=MESH)

    for c in (place.c_core, place.c_x, place.c_far):
        signal(ctx=c)
    for k in range(1, place.n):
        signal(dp=(place.dp + k) % place.n)
    count = place.n + 2
    for slab in slabs:

        @pl.when(jnp.logical_not(place.slab_stays))
        def _():
            signal(**slab)

        count = count + jnp.where(place.slab_stays, 0, 1)
    return barrier, count


class Gather:
    def __init__(self, place, bufs, sems):
        self.at, self.bufs, self.sems = place, bufs, sems

    @staticmethod
    def scratch(n, bufs):
        return pltpu.SemaphoreType.DMA((5, bufs, n // 2))

    def copy(self, b, p, way):
        at = self.at
        block = self.bufs[b].at[p * 2 + at.inner]
        device = (at.dp_up, at.dp_down, at.dp_inner)[way]
        recv = self.sems.at[4 if way == 2 else 3, b, p]
        return rcopy(block, block, self.sems.at[way, b, p], recv, dp=device)

    def send(self, p, up, down, inner=True):
        at = self.at
        for b in range(len(self.bufs)):
            if up:

                @pl.when(at.has_up)
                def _():
                    self.copy(b, p, 0).start()

            if down:

                @pl.when(at.has_down)
                def _():
                    self.copy(b, p, 1).start()

            if inner:
                self.copy(b, p, 2).start()

    def start(self):
        self.send(self.at.outer, True, True)

    def start_inner(self):
        self.send(self.at.outer, False, False)

    def start_line(self):
        self.send(self.at.outer, True, True, False)

    def step(self, t):
        at = self.at
        for p, there, up in ((at.outer - t, at.outer >= t, True), (at.outer + t, at.outer + t < at.line, False)):

            @pl.when(there)
            def _():
                for b in range(len(self.bufs)):
                    self.copy(b, p, 0).wait_recv()
                self.send(p, up, not up)

    def arrive(self):
        at = self.at
        for b in range(len(self.bufs)):
            for p in range(at.line):
                block = self.bufs[b].at[p * 2 + 1 - at.inner]
                rcopy(block, block, self.sems.at[2, b, p], self.sems.at[4, b, p], dp=at.dp_inner).wait_recv()

    def finish(self):
        at = self.at
        for b in range(len(self.bufs)):
            for p in range(at.line):
                self.copy(b, p, 2).wait_send()

                @pl.when(jnp.logical_and(at.has_up, p <= at.outer))
                def _():
                    self.copy(b, p, 0).wait_send()

                @pl.when(jnp.logical_and(at.has_down, p >= at.outer))
                def _():
                    self.copy(b, p, 1).wait_send()


class Reduce:
    def __init__(self, place, parts, from_inner, from_line, sems):
        self.at, self.parts, self.from_inner, self.from_line, self.sems = place, parts, from_inner, from_line, sems

    @staticmethod
    def scratch(n, blocks):
        line = n // 2
        return (
            [pltpu.VMEM((line, *dims), dtype) for dims, dtype in blocks],
            [pltpu.VMEM((line + 1, *dims), dtype) for dims, dtype in blocks],
            pltpu.SemaphoreType.DMA((4, len(blocks), line + 1)),
        )

    def inner_copy(self, b, p):
        at = self.at
        return rcopy(
            self.parts[b].at[p * 2 + 1 - at.inner], self.from_inner[b].at[p],
            self.sems.at[0, b, p], self.sems.at[1, b, p], dp=at.dp_inner,
        )

    def line_copy(self, b, p, slot, up):
        at = self.at
        return rcopy(
            self.from_inner[b].at[p], self.from_line[b].at[slot],
            self.sems.at[2, b, p], self.sems.at[3, b, slot], dp=at.dp_up if up else at.dp_down,
        )

    def start(self, which):
        at = self.at
        for d in range(at.line - 1, -1, -1):
            for p, there in ((at.outer + d, at.outer + d < at.line), (at.outer - d, at.outer >= d))[: 2 if d else 1]:

                @pl.when(there)
                def _():
                    for b in which:
                        self.inner_copy(b, p).start()

    def total(self, b, p, slots):
        s = self.parts[b][p * 2 + self.at.inner].astype(F32) + self.from_inner[b][p].astype(F32)
        for slot in slots:
            s = s + self.from_line[b][slot].astype(F32)
        return s

    def step(self, d, which):
        at = self.at
        for p, there, more, up in (
            (at.outer + d, at.outer + d < at.line, at.has_down, True),
            (at.outer - d, at.outer >= d, at.has_up, False),
        ):
            for b in which:

                @pl.when(there)
                def _():
                    self.inner_copy(b, p).wait_recv()
                    into = self.from_inner[b].at[p]

                    @pl.when(more)
                    def _():
                        self.line_copy(b, p, p, up).wait_recv()
                        into[...] = self.total(b, p, [p]).astype(into.dtype)

                    @pl.when(jnp.logical_not(more))
                    def _():
                        into[...] = self.total(b, p, []).astype(into.dtype)

                    slot = p if up or d > 1 else at.line
                    self.line_copy(b, p, slot, up).start()

    def result(self, b, store):
        at = self.at
        p = at.outer
        self.inner_copy(b, p).wait_recv()
        lo, hi = at.has_down, at.has_up

        @pl.when(lo)
        def _():
            self.line_copy(b, p, p, True).wait_recv()

        @pl.when(hi)
        def _():
            self.line_copy(b, p, at.line, False).wait_recv()

        @pl.when(jnp.logical_and(lo, hi))
        def _():
            store(self.total(b, p, [p, at.line]))

        @pl.when(jnp.logical_and(lo, jnp.logical_not(hi)))
        def _():
            store(self.total(b, p, [p]))

        @pl.when(jnp.logical_and(hi, jnp.logical_not(lo)))
        def _():
            store(self.total(b, p, [at.line]))

    def finish(self):
        at = self.at
        for b in range(len(self.parts)):
            for p in range(at.line):
                self.inner_copy(b, p).wait_send()

                @pl.when(p != at.outer)
                def _():
                    self.line_copy(b, p, p, True).wait_send()


class CtxGather:
    def __init__(self, place, buf, sems):
        self.at, self.buf, self.sems = place, buf, sems

    def copy(self, k, owner):
        block = self.buf.at[owner]
        ctx = self.at.c_x if k == 1 else self.at.c_core
        return rcopy(block, block, self.sems.at[0, k], self.sems.at[1, k], ctx=ctx)

    def start(self):
        self.copy(1, self.at.ctx).start()
        self.copy(0, self.at.ctx).start()

    def forward(self):
        self.copy(1, self.at.c_x).wait_recv()
        self.copy(2, self.at.c_x).start()

    def arrive(self):
        self.copy(0, self.at.c_core).wait_recv()
        self.copy(2, self.at.c_far).wait_recv()

    def finish(self):
        for k in range(3):
            self.copy(k, self.at.ctx).wait_send()


class CtxReduce:
    def __init__(self, place, part, got, sems):
        self.at, self.part, self.got, self.sems = place, part, got, sems

    def copy(self, k):
        at = self.at
        block = self.got.at[1] if k == 2 else self.part.at[(at.c_core, at.c_far)[k]]
        return rcopy(block, self.got.at[k], self.sems.at[0, k], self.sems.at[1, k], ctx=at.c_x if k == 2 else at.c_core)

    def start(self):
        self.copy(1).start()
        self.copy(0).start()

    def across(self):
        self.copy(1).wait_recv()
        into = self.got.at[1]
        into[...] = (self.part[self.at.c_x].astype(F32) + into[...].astype(F32)).astype(into.dtype)
        self.copy(2).start()

    def result(self):
        self.copy(0).wait_recv()
        self.copy(2).wait_recv()
        return self.part[self.at.ctx].astype(F32) + self.got[0].astype(F32) + self.got[2].astype(F32)

    def finish(self):
        for k in range(3):
            self.copy(k).wait_send()


class Quarters:
    def __init__(self, place, src, dst, sems):
        self.at, self.src, self.dst, self.sems = place, src, dst, sems

    def copies(self):
        at = self.at
        return [
            rcopy(self.src.at[c], self.dst.at[at.ctx], self.sems.at[0, k], self.sems.at[1, k], ctx=c)
            for k, c in enumerate((at.c_x, at.c_far, at.c_core))
        ]

    def start(self):
        for c in self.copies():
            c.start()
        self.dst[self.at.ctx] = self.src[self.at.ctx]

    def finish(self):
        for c in self.copies():
            c.wait()


class Slab:
    def __init__(self, place, src, dst, sems, to):
        self.at, self.src, self.dst, self.sems, self.to = place, src, dst, sems, to

    def copy(self):
        return rcopy(self.src, self.dst, self.sems.at[0, 0], self.sems.at[1, 0], **self.to)

    def start(self):
        @pl.when(self.at.slab_stays)
        def _():
            self.dst[...] = self.src[...]

        @pl.when(jnp.logical_not(self.at.slab_stays))
        def _():
            self.copy().start()

    def finish(self):
        @pl.when(jnp.logical_not(self.at.slab_stays))
        def _():
            self.copy().wait()


class Exchange:
    def __init__(self, place, src, dst, cap, sems):
        self.at, self.src, self.dst, self.cap, self.sems = place, src, dst, cap, sems

    def rows(self, ref, j):
        if len(ref.shape) == 3:
            size = ref.shape[1]
            start = j * self.cap
            return ref.at[start // size, pl.ds(pl.multiple_of(start % size, self.cap), self.cap)]
        return ref.at[pl.ds(pl.multiple_of(j * self.cap, self.cap), self.cap)]

    def copy(self, k):
        at = self.at
        to = (at.dp + k) % at.n
        return rcopy(self.rows(self.src, to), self.rows(self.dst, at.dp), self.sems.at[0, k], self.sems.at[1, k], dp=to)

    def start(self):
        for k in range(1, self.at.n):
            self.copy(k).start()
        self.rows(self.dst, self.at.dp)[...] = self.rows(self.src, self.at.dp)[...]

    def finish(self):
        for k in range(1, self.at.n):
            self.copy(k).wait()


def sem_pairs(count):
    return pltpu.SemaphoreType.DMA((2, count))


def norm_back(c, v, gain):
    r = lax.rsqrt(jnp.mean(v * v, axis=-1, keepdims=True) + EPS)
    nv = v * r
    cg = c * gain
    return jnp.sum(c * nv, axis=0, keepdims=True), r * (cg - nv * jnp.mean(cg * nv, axis=-1, keepdims=True))


def into(ref):
    def store(v):
        ref[...] = v.astype(ref.dtype)

    return store


def quarter_columns(dst_ref, weights):
    for c in range(4):
        start = 0
        for w in weights:
            size = w.shape[1] // 4
            dst_ref[c, :, start : start + size] = w[:, c * size : (c + 1) * size]
            start += size


def unit_columns(n, dst_ref, weights):
    size = weights[0].shape[1] // (4 * n)
    for c in range(4):
        for k, w in enumerate(weights):
            for d in range(n):
                start = (k * n + d) * size
                dst_ref[c, :, start : start + size] = w[:, (d * 4 + c) * size : (d * 4 + c + 1) * size]


def route(n, cap, dest_ref, place_ref, labs_ref):
    tok = dest_ref.shape[1]
    dest = dest_ref[...]
    owner = jnp.right_shift(dest, (4 * tok).bit_length() - 1)
    slot = jnp.bitwise_and(dest, tok - 1)
    lines = lax.broadcasted_iota(jnp.int32, (n, tok), 0)
    hot = (lines == owner).astype(F32)
    before = lax.broadcasted_iota(jnp.int32, (tok, tok), 0) < lax.broadcasted_iota(jnp.int32, (tok, tok), 1)
    rank = dot(hot.astype(BF), before.astype(BF))
    send = jnp.sum(hot * (rank + (lines * cap).astype(F32)), axis=0, keepdims=True).astype(jnp.int32)
    place = (lax.broadcasted_iota(jnp.int32, (n * cap, tok), 0) == send).astype(BF)
    place_ref[...] = place
    labels = dot_nt(jnp.broadcast_to((slot + 1).astype(F32), (8, tok)).astype(BF), place)
    labs_ref[...] = jnp.zeros_like(labs_ref)
    for j in range(n):
        labs_ref[j * 8 : j * 8 + 8, :cap] = labels[:, j * cap : (j + 1) * cap]


def gain_tile(at, raw_ref, counts):
    index = at.dp * 4 + at.ctx
    raw = jnp.broadcast_to(raw_ref[...], (8, 128)).astype(BF)
    source = lax.broadcasted_iota(jnp.int32, (128, 128), 0)
    target = lax.broadcasted_iota(jnp.int32, (128, 128), 1)
    lines = lax.broadcasted_iota(jnp.int32, (8, 128), 0)
    total, start = jnp.zeros((8, 128), F32), 0
    for k, count in enumerate(counts):
        move = (target - (index * count) % 128 == source - start) & (source >= start) & (source < start + count)
        total = total + jnp.where(lines == k, dot(raw, move.astype(BF)), 0.0)
        start += count
    return total


def final_body(counts, ig, layer, qkv, o, gu, gd, small, layer_out, ig_out, ga, gq, gk, gv, gqg, gkg, go, gm, gg, gup, gdn):
    index = lax.axis_index("dp") * 4 + lax.axis_index("ctx")
    layer_out[...] = layer[...]
    ig_out[...] = ig[...]
    for c in range(4):
        start = 0
        for out in (gq, gk, gv):
            size = out.shape[1] // 4
            out[:, c * size : (c + 1) * size] = qkv[c, :, start : start + size].astype(F32)
            start += size
        size = gdn.shape[0]
        n = gg.shape[1] // (4 * size)
        for k, out in enumerate((gg, gup)):
            for d in range(n):
                start = (k * n + d) * size
                out[:, (d * 4 + c) * size : (d * 4 + c + 1) * size] = gu[c, :, start : start + size].astype(F32)
    go[...] = o[...].astype(F32)
    gdn[...] = gd[...].astype(F32)
    for k, (out, count) in enumerate(zip((ga, gm, gqg, gkg), counts)):
        row = pltpu.roll(small[...], (128 - (index * count) % 128) % 128, 1)
        out[...] = row[k : k + 1, :count]


def layer_body(
    n, cap, counts,
    in_ref, dest_ref, doc_ref, raw_ref, og_ref, wq_src, wk_src, wv_src, wo_src, wg_src, wu_src, wd_src, cos_ref, sin_ref,
    ig_ref, layer_ref, qkv_out, o_out, gu_out, gd_out, gain_out,
    wqkv_ref, wo_ref, wgu_ref, wd_ref, og_all, x_own, pick_ref, ga_ref, gm_ref, q_ref, k_ref, v_ref, p_ref, xn_ref, att_ref, nm_ref, mid_ref,
    recv, labels, gains_c, gains_n, x_ref, part_ref, got, mask_ref,
    hid_ref, dgu_ref, outp_ref, got_d, got_o, dmid_ref, dq_ref, dk_ref, dv_ref, ggq_ref, ggk_ref, ggm_ref, gains, recv_back,
    yi0, yi1, ln0, ln1, s_ra, yo, lo, s_rb, yq, yg, lq, lg, s_rc,
    gain_sum, gain_all, qkv_ref, gu_ref, place_ref, lab_ref, gwd_ref,
    s_ga, s_gb, s_gc, s_gd4, s_rows, s_labs, s_qkv, s_gu, s_wo, s_gain, s_x, s_og, s_red, s_nm,
    s_dnm, s_out, s_db, s_dxn, s_rows_back, s_gu_back, s_qkv_back, s_o, s_gain_back,
):
    at = Place(n)
    barrier, count = greet(at, (at.slab_from, at.slab_to))
    quarter_columns(qkv_ref, (wq_src, wk_src, wv_src))
    gains_c[at.ctx] = gain_tile(at, raw_ref, counts)
    route(n, cap, dest_ref, place_ref, lab_ref)
    tok = in_ref.shape[0]
    for half in range(n * cap // tok):
        part_ref[half] = dot(place_ref[half * tok : (half + 1) * tok, :], in_ref[...]).astype(BF)
    pl.semaphore_wait(barrier, count)
    qkv = Quarters(at, qkv_ref, wqkv_ref.at[at.dp], s_qkv)
    rows = Exchange(at, part_ref, recv, cap, s_rows)
    labs = Exchange(at, lab_ref, labels, 8, s_labs)
    qkv.start()
    gain_copies = [
        rcopy(gains_c.at[at.ctx], gains_c.at[at.ctx], s_gain.at[0, k], s_gain.at[1, k], ctx=c)
        for k, c in enumerate((at.c_x, at.c_far, at.c_core))
    ]
    for g in gain_copies:
        g.start()
    unit_columns(n, gu_ref, (wg_src, wu_src))
    wo = Slab(at, wo_src, wo_ref.at[at.slab_to["dp"]], s_wo, at.slab_to)
    wd_ref[at.dp] = wd_src[...]
    gu = Quarters(at, gu_ref, wgu_ref.at[at.dp], s_gu)
    labs.start()
    rows.start()
    gu.start()
    wo.start()
    for g in gain_copies:
        g.wait()
    gains_n[at.dp] = gains_c[0] + gains_c[1] + gains_c[2] + gains_c[3]
    qkv.finish()
    first = Gather(at, [wqkv_ref, gains_n], s_ga)
    first.start()
    og_all[at.ctx] = og_ref[...]
    og = CtxGather(at, og_all, s_og)
    gu.finish()
    og.start()
    third = Gather(at, [wgu_ref], s_gc)
    third.start_inner()
    labs.finish()
    slots = lax.broadcasted_iota(jnp.int32, (tok, cap), 0).astype(F32) + 1.0
    for j in range(n):
        pick_ref[:, j * cap : (j + 1) * cap] = (slots == labels[j * 8 : j * 8 + 1, :cap]).astype(BF)
    first.step(1)
    rows.finish()
    owned = dot(pick_ref[...], recv[...]).astype(BF)
    x_ref[at.ctx] = owned
    x_own[...] = owned
    x = CtxGather(at, x_ref, s_x)
    x.start()
    first.step(2)
    third.start_line()
    wo.finish()
    second = Gather(at, [wo_ref], s_gb)
    second.start()
    for t in range(3, at.line):
        first.step(t)
    second.step(1)
    og.forward()
    x.forward()
    first.arrive()
    own = 4 * ga_ref.shape[1] // (4 * n)
    ga_ref[...] = jnp.zeros_like(ga_ref)
    gm_ref[...] = jnp.zeros_like(gm_ref)
    gqk = jnp.zeros((8, 128), F32)
    for d in range(n):
        tile = slice(d * own // 128 * 128, d * own // 128 * 128 + 128)
        block = gains_n[d]
        ga_ref[0:1, tile] += block[0:1]
        gm_ref[0:1, tile] += block[1:2]
        gqk = gqk + block
    off = jnp.where(doc_ref[0:1, 0:1] > 0, 0.0, MASKED).astype(F32)
    mask_ref[...] = mask_block(off)
    x.arrive()
    second.step(2)
    attn_project(x_ref, wqkv_ref, ga_ref, gqk[2:3], gqk[3:4], cos_ref, sin_ref, q_ref, k_ref, v_ref, p_ref, xn_ref)
    for t in range(3, at.line):
        second.step(t)
    third.step(1)
    nk = k_ref.shape[1] // HD

    @pl.loop(0, nk)
    def _(g):
        attn_group(g, off, q_ref, k_ref, v_ref, att_ref, mask_ref)

    third.step(2)
    second.arrive()

    @pl.loop(0, 4)
    def _(i):
        part_ref[i] = dot(att_ref[lanes(i, tok), :], rows_of(wo_ref)).astype(BF)

    red = CtxReduce(at, part_ref, got, s_red)
    red.start()
    red.across()
    for t in range(3, at.line):
        third.step(t)
    fourth = Gather(at, [wd_ref], s_gd4)
    fourth.start()
    middle = x_own[...].astype(F32) + red.result()
    mid_ref[...] = middle
    r = lax.rsqrt(jnp.mean(middle * middle, axis=-1, keepdims=True) + EPS)
    nm_ref[at.ctx] = (middle * r * gm_ref[0:1, :]).astype(BF)
    nm = CtxGather(at, nm_ref, s_nm)
    nm.start()
    fourth.step(1)
    nm.forward()
    fourth.step(2)
    nm.arrive()
    og.arrive()
    for t in range(3, at.line):
        fourth.step(t)
    third.arrive()
    feed_up(nm_ref, wgu_ref, hid_ref, dgu_ref)
    weight_grad(gwd_ref, hid_ref, og_all, 384)
    grads = Reduce(at, [wgu_ref, gwd_ref], [yi0, yi1], [ln0, ln1], s_ra)
    grads.start([1])
    fourth.arrive()
    for part in (first, second, third, fourth, og, x, nm, red):
        part.finish()
    first = grads
    feed_down(og_all, wgu_ref, wd_ref, hid_ref, dgu_ref, outp_ref, part_ref)
    db_ref, da_ref, dp_ref = x_ref, hid_ref.at[:, : q_ref.shape[1]], dgu_ref.at[:, : wqkv_ref.shape[-1]]
    last = at.line - 1
    dnm = CtxReduce(at, part_ref, got_d, s_dnm)
    dnm.start()
    first.step(last, [1])
    dnm.across()
    weight_grad(wgu_ref, nm_ref, dgu_ref)
    first.start([0])
    out = CtxReduce(at, outp_ref, got_o, s_out)
    dk_ref[...] = jnp.zeros_like(dk_ref)
    dv_ref[...] = jnp.zeros_like(dv_ref)
    first.step(last - 1, [1])
    gg, d = norm_back(dnm.result(), mid_ref[...], gm_ref[0:1, :])
    ggm_ref[...] = gg
    d = d + og_ref[...].astype(F32)
    dmid_ref[...] = d
    db_ref[at.ctx] = d.astype(BF)
    db = CtxGather(at, db_ref, s_db)
    db.start()
    out.start()
    for t in range(last - 2, 0, -1):
        first.step(t, [1])
    db.forward()
    out.across()
    db.arrive()
    tok = db_ref.shape[1]

    @pl.loop(0, 4)
    def _(i):
        da_ref[lanes(i, tok), :] = dot_nt(db_ref[i], rows_of(wo_ref)).astype(BF)

    first.step(last, [0])
    for g in range(k_ref.shape[1] // HD):
        for i in range(q_ref.shape[0] // QB):
            attn_group_back(g, i, off, q_ref, k_ref, v_ref, att_ref, da_ref, dq_ref, dk_ref, dv_ref, mask_ref)
        if g == 0:
            for t in range(last - 1, 1, -1):
                first.step(t, [0])
    dxn_ref = nm_ref
    attn_unproject(gqk[2:3], gqk[3:4], cos_ref, sin_ref, p_ref, dq_ref, dk_ref, dv_ref, dp_ref, wqkv_ref, dxn_ref, ggq_ref, ggk_ref)
    dxn = CtxReduce(at, dxn_ref, got, s_dxn)
    dxn.start()
    first.step(1, [0])
    weight_grad(wqkv_ref, xn_ref, dp_ref)
    third = Reduce(at, [wqkv_ref, gains], [yq, yg], [lq, lg], s_rc)
    third.start([0])
    dxn.across()
    weight_grad(wo_ref, att_ref, db_ref)
    second = Reduce(at, [wo_ref], [yo], [lo], s_rb)
    second.start([0])
    first.result(1, into(gd_out))
    first.result(0, into(yi0.at[at.outer]))
    gu = Quarters(at, yi0.at[at.outer], gu_out, s_gu_back)
    gu.start()
    third.step(last, [0])
    gg, d = norm_back(dxn.result(), x_own[...].astype(F32), ga_ref[0:1, :])
    owned = (dmid_ref[...] + d).astype(BF)
    recv[...] = dot_tn(pick_ref[...], owned).astype(BF)
    rows = Exchange(at, recv, recv_back, cap, s_rows_back)
    rows.start()
    own = 4 * gg.shape[1] // (4 * n)
    lines = lax.broadcasted_iota(jnp.int32, (8, 128), 0)
    for j in range(n):
        tile = slice(j * own // 128 * 128, j * own // 128 * 128 + 128)
        gains[j] = (
            jnp.where(lines == 0, gg[:, tile], 0.0) + jnp.where(lines == 1, ggm_ref[0:1, tile], 0.0)
            + jnp.where(lines == 2, ggq_ref[0:1, :], 0.0) + jnp.where(lines == 3, ggk_ref[0:1, :], 0.0)
        )
    third.start([1])
    second.step(last, [0])
    for t in range(last - 1, 0, -1):
        second.step(t, [0])
        third.step(t, [0])
    layer_ref[...] = (mid_ref[...] + out.result()).astype(BF)
    for t in range(last, 0, -1):
        third.step(t, [1])
    second.result(0, into(yo.at[at.outer]))
    o = Slab(at, yo.at[at.outer], o_out, s_o, at.slab_from)
    o.start()
    third.result(0, into(yq.at[at.outer]))
    qkv = Quarters(at, yq.at[at.outer], qkv_out, s_qkv_back)
    qkv.start()
    third.result(1, into(gain_sum))
    small = [
        rcopy(gain_sum, gain_all.at[at.ctx], s_gain_back.at[0, k], s_gain_back.at[1, k], ctx=c)
        for k, c in enumerate((at.c_x, at.c_far, at.c_core))
    ]
    for g in small:
        g.start()
    gain_all[at.ctx] = gain_sum[...]
    rows.finish()
    ig_ref[...] = dot_tn(place_ref[...], recv_back[...]).astype(BF)
    for g in small:
        g.wait()
    gain_out[...] = gain_all[0] + gain_all[1] + gain_all[2] + gain_all[3]
    for part in (qkv, o, gu, dxn, db, out, dnm, first, second, third):
        part.finish()


def shape(*dims, dtype=BF):
    return jax.ShapeDtypeStruct(dims, dtype)


def linked(body, outs, scratch, name, number):
    return pl.pallas_call(
        body,
        out_shape=outs,
        scratch_shapes=scratch,
        compiler_params=pltpu.CompilerParams(vmem_limit_bytes=VMEM_LIMIT, collective_id=number, has_side_effects=True),
        name=name,
    )


def local(
    layer_input, dest_slot, doc_len, out_grad, attn_gain, w_query, w_key, w_value, q_gain, k_gain,
    w_out, mlp_gain, w_gate, w_up, w_down,
):
    tok, width = layer_input.shape
    n = lax.axis_size("dp")
    cap = 2 * tok // n
    rows = 4 * tok
    slabs = n * cap
    rq, ro, rd = w_query.shape[0], w_out.shape[0], w_down.shape[0]
    ff = rd * n
    counts = (attn_gain.shape[0], mlp_gain.shape[0], q_gain.shape[0], k_gain.shape[0])
    raw = jnp.pad(jnp.concatenate([attn_gain, mlp_gain, q_gain, k_gain]), (0, 128 - sum(counts))).astype(F32).reshape(1, 128)
    fw = 2 * ff
    cos, sin = rope_tables(rows)
    blocks = ([((4, rq, fw), BF), ((rd, width), BF)], [((ro, width), BF)], [((4, rq, 1024), BF), ((8, 128), F32)])
    reduces = []
    for red, lines, sems in (Reduce.scratch(n, b) for b in blocks):
        reduces += [*red, *lines, sems]
    vm = pltpu.VMEM
    group = (4, tok, width)
    input_grad, layer_output, g_qkv, g_o, g_gu, g_d, small = linked(
        functools.partial(layer_body, n, cap, counts),
        (shape(tok, width), shape(tok, width), shape(4, rq, 1024), shape(ro, width), shape(4, rq, fw), shape(rd, width), shape(8, 128, dtype=F32)),
        [vm((n, 4, rq, 1024), BF), vm((n, ro, width), BF), vm((n, 4, rq, fw), BF), vm((n, rd, width), BF), vm(group, BF), vm((tok, width), BF),
         vm((tok, slabs), BF), vm((8, width), F32), vm((8, width), F32), vm((rows, 512), BF), vm((rows, 256), BF), vm((rows, 256), BF),
         vm((rows, 768), BF), vm((rows, width), BF), vm((rows, 512), BF), vm(group, BF), vm((tok, width), F32),
         vm((slabs, width), BF), vm((n * 8, 128), F32), vm((4, 8, 128), F32), vm((n, 8, 128), F32),
         vm(group, BF), vm(group, BF), vm((3, tok, width), BF), vm((QB, QB), F32),
         vm((rows, ff), BF), vm((rows, fw), BF), vm(group, BF), vm((3, tok, width), BF), vm((3, tok, width), BF),
         vm((tok, width), F32), vm((rows, 512), F32), vm((rows, 256), F32), vm((rows, 256), F32),
         vm((8, HD), F32), vm((8, HD), F32), vm((1, width), F32), vm((n, 8, 128), F32), vm((slabs, width), BF),
         *reduces,
         vm((8, 128), F32), vm((4, 8, 128), F32), vm((4, rq, 1024), BF), vm((4, rq, fw), BF), vm((slabs, tok), BF), vm((n * 8, 128), F32), vm((n, rd, width), BF),
         Gather.scratch(n, 2), Gather.scratch(n, 1), Gather.scratch(n, 1), Gather.scratch(n, 1), sem_pairs(n), sem_pairs(n), sem_pairs(3), sem_pairs(3),
         sem_pairs(1), sem_pairs(3), sem_pairs(3), sem_pairs(3), sem_pairs(3), sem_pairs(3),
         sem_pairs(3), sem_pairs(3), sem_pairs(3), sem_pairs(3), sem_pairs(n), sem_pairs(3), sem_pairs(3), sem_pairs(1), sem_pairs(3)],
        "layer", 0,
    )(layer_input, dest_slot.reshape(1, tok), doc_len, raw, out_grad, w_query, w_key, w_value, w_out, w_gate, w_up, w_down, cos, sin)
    grads = [shape(*w.shape, dtype=F32) for w in (w_query, w_key, w_value, w_out, w_gate, w_up, w_down)]
    gains = [shape(1, c, dtype=F32) for c in counts]
    outs = (shape(tok, width), shape(tok, width), gains[0], *grads[:3], gains[2], gains[3], grads[3], gains[1], *grads[4:])
    outs = pl.pallas_call(functools.partial(final_body, counts), out_shape=outs, name="final")(
        input_grad, layer_output, g_qkv, g_o, g_gu, g_d, small
    )
    return tuple(o.reshape(-1) if o.shape[0] == 1 else o for o in outs)


def solution(mesh):
    rows = P(BOTH, None)
    vec = P(BOTH)
    return jax.shard_map(
        local,
        mesh=mesh,
        in_specs=(rows, vec, P("dp", None), rows, vec, rows, rows, rows, vec, vec, rows, vec, rows, rows, rows),
        out_specs=(rows, rows, vec, rows, rows, rows, vec, vec, rows, vec, rows, rows, rows),
        check_vma=False,
    )
```
